32 devices in a mesh: dp: 8 (over z, y), shard: 4 (over x, core).
Axes of the slice: x: 2, y: 2, z: 4, core: 2. Of those that a mesh axis runs over, the one named last changes fastest.
Arguments:
- tokens: bfloat16 [32768, 512], P(('dp', 'shard')), may hold values from -6 to 6
- memory: bfloat16 [32768, 512], P(('dp', 'shard')), may hold values from -6 to 6
- target_lengths: int32 [32, 16], P(('dp', 'shard')), may hold values from 1 to 512, 1024 in all within a row
- source_lengths: int32 [32, 16], P(('dp', 'shard')), may hold values from 1 to 512, 1024 in all within a row
- out_grad: bfloat16 [32768, 512], P(('dp', 'shard')), may hold values from -6 to 6
- weights: float32 [4, 512, 2048], P(None, ('dp', 'shard')), may hold values from -1 to 1
- vectors: float32 [17, 512], P(None, ('dp', 'shard')), may hold values from -1 to 3
- weight_moments: float32 [2, 4, 512, 2048], P(None, None, ('dp', 'shard')), may hold values from -1 to 1, as said below
- vector_moments: float32 [2, 17, 512], P(None, None, ('dp', 'shard')), may hold values from -1 to 1, as said below
Outputs:
- layer_out: bfloat16 [32768, 512], P(('dp', 'shard'))
- input_grad: float32 [32768, 512], P(('dp', 'shard'))
- memory_grad: float32 [32768, 512], P(('dp', 'shard'))
- grad_norm: float32 [], replicated
- weight_grads: float32 [4, 512, 2048], P(None, ('dp', 'shard'))
- vector_grads: float32 [17, 512], P(None, ('dp', 'shard'))
- weight_steps: float32 [4, 512, 2048], P(None, ('dp', 'shard'))
- vector_steps: float32 [17, 512], P(None, ('dp', 'shard'))
- new_weight_first: float32 [4, 512, 2048], P(None, ('dp', 'shard'))
- new_weight_second: float32 [4, 512, 2048], P(None, ('dp', 'shard'))
- new_vector_first: float32 [17, 512], P(None, ('dp', 'shard'))
- new_vector_second: float32 [17, 512], P(None, ('dp', 'shard'))
The draws below stay inside these ranges and needn't reach their ends.
Inputs may be any that keep to these rules, and one draw needn't show every extreme that they name: `target_lengths`: the lengths of each packed row sum to 1024; target sentence i of a row is the translation of source sentence i of the same row. `source_lengths`: the lengths of each packed row sum to 1024. `weight_moments`: the second moments, index 1 of the first dimension, are not negative. `vector_moments`: the second moments, index 1 of the first dimension, are not negative.
All inputs are finite; a program needn't handle non-finite values.
Results may differ from the reference program's by a relative error of at most 0.018.
The reference program's roundings to bfloat16 on the way count: a program that leaves them out, or rounds other values in their place, can miss the bound.
Values may be sent and summed in bfloat16 or wider, within the bound.
A program may use at most 192 MiB of HBM per device.

```python
import math
import jax
import jax.numpy as jnp
import numpy as np
from jax import lax

D = 512
H = 8
HD = 64
FF = 2048
ROW_LEN = 1024
MAXLEN = 512
SENTS = 16
ROWS = 32
TOKENS = 32768


def draw_weights(key, part):
    shape = (4, D, 4 * D)
    base = jax.random.truncated_normal(key, -4.0, 4.0, shape, jnp.float32)
    columns = jnp.arange(4 * D)
    attention_scale = jnp.where(columns < 3 * D, 1.0, 3.0) * D ** (-0.5)
    up_scale = jnp.full((4 * D,), D ** (-0.5), jnp.float32)
    down_scale = jnp.full((4 * D,), 1.5 * FF ** (-0.5), jnp.float32)
    scale_table = jnp.stack([attention_scale, attention_scale, up_scale, down_scale]).astype(jnp.float32)
    return base * scale_table[:, None, :]


def draw_vectors(key, part):
    gain_key = jax.random.fold_in(key, 11)
    bias_key = jax.random.fold_in(key, 12)
    row_ids = jnp.arange(17)[:, None]
    is_gain = (row_ids == 3) | (row_ids == 8) | (row_ids == 15)
    feature_place = jnp.arange(D).astype(jnp.float32) / (D - 1) - 0.5
    ramp = jnp.exp(math.log(3.0) * feature_place)
    spread = ramp[None, :] * jax.random.uniform(gain_key, (17, D), jnp.float32, 0.8, 1.2)
    offsets = 0.2 * jax.random.truncated_normal(bias_key, -4.0, 4.0, (17, D), jnp.float32)
    return jnp.where(is_gain, spread, offsets)


def moment_pair(key, shape, scale):
    early_key = jax.random.fold_in(key, 21)
    later_key = jax.random.fold_in(key, 22)
    early = scale * jax.random.truncated_normal(early_key, -4.0, 4.0, shape, jnp.float32)
    later = scale * jax.random.truncated_normal(later_key, -4.0, 4.0, shape, jnp.float32)
    first_m = 0.09 * early + 0.1 * later
    second_m = 0.000999 * early * early + 0.001 * later * later
    return jnp.stack([first_m, second_m])


def draw_weight_moments(key, part):
    key = jax.random.fold_in(key, 31)
    return moment_pair(key, (4, D, 4 * D), 0.5 / (4.0 * D))


def draw_vector_moments(key, part):
    key = jax.random.fold_in(key, 32)
    return moment_pair(key, (17, D), 0.03 * (17.0 * D) ** (-0.5))


def levels(own_key, dims, cuts, low, largest):
    def one(axis_at, parts):
        heights = jax.random.uniform(jax.random.fold_in(jax.random.fold_in(own_key, 6), axis_at), (parts,), jnp.float32, low / len(cuts), largest / len(cuts))
        return jnp.repeat(jnp.exp(heights), dims[axis_at] // parts).reshape((-1,) + (1,) * (len(dims) - axis_at - 1))

    level = one(*cuts[0])
    for cut in cuts[1:]:
        level = level * one(*cut)
    return level


def length_profile(number_of, total, bound, slope):
    portions = [(1 << 20) // math.isqrt(rank ** slope) + 1 for rank in range(2, number_of + 1)]
    surplus, holding = total - bound - (number_of - 1), [1] * (number_of - 1)
    while surplus > 0:
        movable = [i for i in range(number_of - 1) if holding[i] < bound]
        whole, budget = sum([portions[i] for i in movable]), surplus
        for i in movable:
            addition = min(bound - holding[i], max(1, budget * portions[i] // whole), surplus)
            holding[i] = holding[i] + addition
            surplus = surplus - addition
    return np.array([bound] + holding)


def ragged(key, count, total, bound, lean):
    if count == 2:
        one = jax.random.randint(key, (), max(1, total - bound), min(bound, total - 1) + 1)
        return jnp.stack([one, total - one])
    sizes = jnp.asarray(length_profile(count, total, bound, lean), jnp.int32)
    couples = (count - 1) // 2
    source_of, receiver = sizes[1:1 + 2 * couples:2], sizes[2:2 + 2 * couples:2]
    margin = jnp.minimum(source_of - 1, bound - receiver)
    passed = jax.random.randint(jax.random.fold_in(key, 1), (couples,), 0, 1 << 20) % (margin + 1)
    sizes = sizes.at[1:1 + 2 * couples:2].set(source_of - passed).at[2:2 + 2 * couples:2].set(receiver + passed)
    return sizes[jax.random.permutation(jax.random.fold_in(key, 2), count)]


def noise(key, extent, deviation, bound, shards=(), held_as=jnp.bfloat16):
    values = deviation * jax.random.normal(key, extent, jnp.float32)
    if shards:
        values = values * levels(key, extent, shards, -0.22, 0.18)
    return jnp.clip(values, -bound, bound).astype(held_as)


def setup_inputs(seed: int = 0) -> dict:
    seeds = jax.random.split(jax.random.key(seed), 10)
    tokens = noise(seeds[0], (TOKENS, D), 1.0, 6.0, ((0, 32),))
    memory = noise(seeds[1], (TOKENS, D), 1.0, 6.0, ((0, 32),))
    target_lengths = jax.vmap(lambda own: ragged(own, SENTS, ROW_LEN, MAXLEN, 2))(jax.random.split(seeds[2], ROWS)).reshape((ROWS, SENTS)).astype(jnp.int32)
    source_lengths = jax.vmap(lambda own: ragged(own, SENTS, ROW_LEN, MAXLEN, 2))(jax.random.split(seeds[3], ROWS)).reshape((ROWS, SENTS)).astype(jnp.int32)
    out_grad = noise(seeds[4], (TOKENS, D), 1.0, 6.0, ((0, 32),))
    weights = draw_weights(jax.random.fold_in(seeds[9], 71), 0)
    vectors = draw_vectors(jax.random.fold_in(seeds[9], 71), 0)
    weight_moments = draw_weight_moments(jax.random.fold_in(seeds[9], 71), 0)
    vector_moments = draw_vector_moments(jax.random.fold_in(seeds[9], 71), 0)
    return dict(tokens=tokens, memory=memory, target_lengths=target_lengths, source_lengths=source_lengths, out_grad=out_grad, weights=weights, vectors=vectors, weight_moments=weight_moments, vector_moments=vector_moments)


EPSILON = 1e-05
MASKED = -1000000000.0
CLIP_NORM = 1.0
LEARN_RATE = 0.001
BETA_ONE = 0.9
BETA_TWO = 0.999
ADAM_EPS = 1e-08
WEIGHT_DECAY = 0.1
CORRECT_ONE = 1.0 - 0.9 ** 3
CORRECT_TWO = 1.0 - 0.999 ** 3
HIGHEST = lax.Precision.HIGHEST

@jax.custom_vjp
def low(v):
    return lax.optimization_barrier(v.astype(jnp.bfloat16)).astype(jnp.float32)

@jax.custom_vjp
def low_back(v):
    return v

def low_keep(v):
    return (low(v), None)

def low_pass(kept, grad):
    return (grad,)

def back_keep(v):
    return (v, None)

def back_low(kept, grad):
    return (low(grad),)
low.defvjp(low_keep, low_pass)
low_back.defvjp(back_keep, back_low)

def matmul(left, right):
    return jnp.dot(left, right, precision=HIGHEST, preferred_element_type=jnp.float32)

def layer_norm(inputs, gain_row, bias_row):
    centred = inputs - lax.optimization_barrier(jnp.mean(inputs, axis=-1, keepdims=True))
    inverse = lax.rsqrt(lax.optimization_barrier(jnp.mean(centred * centred, axis=-1, keepdims=True)) + EPSILON)
    return centred * inverse * gain_row + bias_row

def segment_ids(lengths):
    sentence_ends = jnp.cumsum(lengths, axis=-1)
    places = lax.iota(jnp.int32, ROW_LEN)
    return lax.optimization_barrier(jnp.sum((sentence_ends[:, None, :] <= places[None, :, None]).astype(jnp.int32), axis=-1))

def attention(queries, key_rows, value_rows, allowed):
    seq_len = queries.shape[0]
    query_heads = queries.reshape(seq_len, H, HD)
    key_heads = key_rows.reshape(key_rows.shape[0], H, HD)
    value_heads = value_rows.reshape(value_rows.shape[0], H, HD)
    scores = jnp.einsum('qhd,khd->hqk', query_heads, key_heads, precision=HIGHEST) * HD ** (-0.5)
    scores = low_back(jnp.where(allowed[None], scores, MASKED))
    soft_weights = low(jax.nn.softmax(scores, axis=-1))
    outputs = jnp.einsum('hqk,khd->qhd', soft_weights, value_heads, precision=HIGHEST)
    return low_back(low(outputs.reshape(seq_len, H * HD)))

def row_forward(low_mats, low_vecs, inputs, source, target_ids, source_ids):
    positions = lax.iota(jnp.int32, ROW_LEN)
    causal = (target_ids[:, None] == target_ids[None, :]) & (positions[None, :] <= positions[:, None])
    crossed = target_ids[:, None] == source_ids[None, :]
    self_weight = low_mats[0]
    queries = low_back(low(matmul(inputs, self_weight[:, :D]) + low_vecs[0]))
    key_rows = low_back(low(matmul(inputs, self_weight[:, D:2 * D])))
    value_rows = low_back(low(matmul(inputs, self_weight[:, 2 * D:3 * D]) + low_vecs[1]))
    attended = attention(queries, key_rows, value_rows, causal)
    branch = low_back(matmul(attended, self_weight[:, 3 * D:]) + low_vecs[2])
    first_out = layer_norm(inputs + branch, low_vecs[3], low_vecs[4])
    first_low = low(first_out)
    cross_weight = low_mats[1]
    cross_query = low_back(low(matmul(first_low, cross_weight[:, :D]) + low_vecs[5]))
    cross_keys = low_back(low(matmul(source, cross_weight[:, D:2 * D])))
    cross_values = low_back(low(matmul(source, cross_weight[:, 2 * D:3 * D]) + low_vecs[6]))
    cross_attn = attention(cross_query, cross_keys, cross_values, crossed)
    cross_branch = low_back(matmul(cross_attn, cross_weight[:, 3 * D:]) + low_vecs[7])
    second = layer_norm(first_out + cross_branch, low_vecs[8], low_vecs[9])
    second_low = low(second)
    pre_hidden = low_back(matmul(second_low, low_mats[2]) + low_vecs[10:14].reshape(FF))
    hidden = low(jax.nn.silu(pre_hidden))
    ffn_out = low_back(matmul(hidden, low_mats[3].T) + low_vecs[14])
    return layer_norm(second + ffn_out, low_vecs[15], low_vecs[16])

def adam_update(params, grad_in, moments, factor):
    clipped = factor * grad_in
    first_m = BETA_ONE * moments[0] + (1.0 - BETA_ONE) * clipped
    second_m = BETA_TWO * moments[1] + (1.0 - BETA_TWO) * clipped * clipped
    stepped = first_m / CORRECT_ONE / (jnp.sqrt(second_m / CORRECT_TWO) + ADAM_EPS)
    return (-LEARN_RATE * (stepped + WEIGHT_DECAY * params), first_m, second_m)

def reference(tokens, memory, target_lengths, source_lengths, out_grad, weights, vectors, weight_moments, vector_moments):
    target_ids = segment_ids(target_lengths)
    source_ids = segment_ids(source_lengths)

    def forward(inputs, source, matrices, vec_rows):
        low_mats = low(matrices)
        low_vecs = low(vec_rows)
        token_rows = inputs.reshape(ROWS, ROW_LEN, D)
        source_rows = source.reshape(ROWS, ROW_LEN, D)
        row_step = jax.checkpoint(row_forward)

        def scan_step(unused, pieces):
            return (unused, row_step(low_mats, low_vecs, pieces[0], pieces[1], pieces[2], pieces[3]))
        unused, outputs = lax.scan(scan_step, jnp.zeros((), jnp.float32), (token_rows, source_rows, target_ids, source_ids))
        return outputs.reshape(TOKENS, D)
    result, pullback = jax.vjp(forward, tokens.astype(jnp.float32), memory.astype(jnp.float32), weights, vectors)
    input_grad, memory_grad, weight_grads, vector_grads = pullback(out_grad.astype(jnp.float32))
    grad_norm = jnp.sqrt(jnp.sum(weight_grads * weight_grads) + jnp.sum(vector_grads * vector_grads))
    factor = jnp.minimum(1.0, CLIP_NORM / (grad_norm + 1e-06))
    weight_steps, weight_first, weight_second = adam_update(weights, weight_grads, weight_moments, factor)
    vector_steps, vector_first, vector_second = adam_update(vectors, vector_grads, vector_moments, factor)
    return (result.astype(jnp.bfloat16), input_grad, memory_grad, grad_norm, weight_grads, vector_grads, weight_steps, vector_steps, weight_first, weight_second, vector_first, vector_second)
```

```python
import functools
import jax
import jax.numpy as jnp
from jax import lax
from jax.experimental import pallas as pl
from jax.experimental.pallas import tpu as pltpu
from jax.sharding import PartitionSpec as P

HD = 64
EPSILON = 1e-05
MASKED = -1e30
BF = jnp.bfloat16
F32 = jnp.float32
TILE = 256
VROWS = 24
CLIP_NORM = 1.0
LEARN_RATE = 0.001
BETA_ONE = 0.9
BETA_TWO = 0.999
ADAM_EPS = 1e-08
WEIGHT_DECAY = 0.1
CORRECT_ONE = 1.0 - 0.9**3
CORRECT_TWO = 1.0 - 0.999**3


def mm(left, right):
    return jnp.dot(left, right, preferred_element_type=F32)


def mm_t(left, right):
    return lax.dot_general(left, right, (((1,), (1,)), ((), ())), preferred_element_type=F32)


def t_mm(left, right):
    return lax.dot_general(left, right, (((0,), (0,)), ((), ())), preferred_element_type=F32)


def rows_of(i, size=TILE):
    return pl.ds(pl.multiple_of(i * size, size), size)


def normed(z):
    centred = z - jnp.mean(z, axis=-1, keepdims=True)
    inverse = lax.rsqrt(jnp.mean(centred * centred, axis=-1, keepdims=True) + EPSILON)
    return centred * inverse, inverse


def norm_back(grad, n, inverse, gain):
    scaled = grad * gain
    return inverse * (
        scaled
        - jnp.mean(scaled, axis=-1, keepdims=True)
        - n * jnp.mean(scaled * n, axis=-1, keepdims=True)
    )


def fold(values):
    r, c = values.shape
    return jnp.sum(values.astype(F32).reshape(r // 8, 8, c), axis=0)


def heads_join(ref, rows):
    return jnp.concatenate([ref[p, rows, :] for p in range(4)], axis=1)


def heads_split(ref, rows, value):
    for p in range(4):
        ref[p, rows, :] = value[:, p * 128 : (p + 1) * 128]


class Bag:
    pass


def head_mask(h, dtype):
    lane = lax.broadcasted_iota(jnp.int32, (1, 128), 1)
    return jnp.where((lane < HD) if h == 0 else (lane >= HD), 1.0, 0.0).astype(dtype)


def segments(r, lengths, row_ref, col_ref):
    ends = []
    total = jnp.int32(0)
    for s in range(16):
        total = total + lengths[0, s]
        ends.append(total)
    place = lax.broadcasted_iota(jnp.int32, (8, 1024), 1)
    seg = jnp.zeros((8, 1024), jnp.int32)
    for e in ends:
        seg = seg + jnp.where(e <= place, 1, 0)
    row_ref[...] = seg

    def col(i, _):
        at = lax.broadcasted_iota(jnp.int32, (TILE, 128), 0) + i * TILE
        c = jnp.zeros((TILE, 128), jnp.int32)
        for e in ends:
            c = c + jnp.where(e <= at, 1, 0)
        col_ref[rows_of(i), :] = c
        return 0

    lax.fori_loop(0, 4, col, 0)


def attend(r, q_ref, k_ref, v_ref, out_ref, lse_ref, tile, key_start, key_count, bias):
    rows = rows_of(tile)
    keys = pl.ds(key_start, key_count)
    lane = lax.broadcasted_iota(jnp.int32, (TILE, 128), 1)

    def pair(p, lses):
        q = q_ref[p, rows, :]
        k = k_ref[p, keys, :]
        v = v_ref[p, keys, :]
        outs = []
        for h in range(2):
            s = mm_t(q * head_mask(h, BF), k) + bias[:, :key_count]
            top = jnp.max(s, axis=-1, keepdims=True)
            e = jnp.exp(s - top)
            total = jnp.sum(e, axis=-1, keepdims=True)
            outs.append(mm(e.astype(BF), v) * (1.0 / total))
            lses = jnp.where(lane == 2 * p + h, top + jnp.log(total), lses)
        out_ref[p, rows, :] = jnp.where(lane < HD, outs[0], outs[1]).astype(BF)
        return lses

    lses = lax.fori_loop(0, 4, pair, jnp.zeros((TILE, 128), F32))
    flipped = lses.T
    for h in range(8):
        lse_ref[h, :, rows_of(tile)] = flipped[h : h + 1, :]


def deltas(r, out_ref, grad_ref, delta_ref, tile):
    rows = rows_of(tile)
    lane = lax.broadcasted_iota(jnp.int32, (TILE, 128), 1)
    table = jnp.zeros((TILE, 128), F32)
    for p in range(4):
        prod = out_ref[p, rows, :].astype(F32) * grad_ref[p, rows, :].astype(F32)
        for h in range(2):
            one = jnp.sum(prod * head_mask(h, F32), axis=-1, keepdims=True)
            table = jnp.where(lane == 2 * p + h, one, table)
    flipped = table.T
    for h in range(8):
        delta_ref[h, :, rows] = flipped[h : h + 1, :]


def attend_back(r, q_ref, k_ref, v_ref, grad_ref, lse_ref, delta_ref, bias, i, j):
    qr, kr = rows_of(i), rows_of(j)
    lane = lax.broadcasted_iota(jnp.int32, (TILE, 128), 1)

    def pair(p, _):
        q, k, v, g = q_ref[p, qr, :], k_ref[p, kr, :], v_ref[p, kr, :], grad_ref[p, qr, :]
        dv, dk, dq = [], [], []
        for h in range(2):
            m = head_mask(h, BF)
            s = mm_t(k * m, q) + bias[...]
            w = jnp.exp(s - lse_ref[2 * p + h, :, qr])
            dp = mm_t(v * m, g)
            ds = (w * (dp - delta_ref[2 * p + h, :, qr])).astype(BF)
            dv.append(mm(w.astype(BF), g))
            dk.append(mm(ds, q))
            dq.append(t_mm(ds, k))
        r.dv[p, kr, :] += jnp.where(lane < HD, dv[0], dv[1])
        r.dk[p, kr, :] += jnp.where(lane < HD, dk[0], dk[1])
        r.dq[p, qr, :] += jnp.where(lane < HD, dq[0], dq[1])
        return 0

    lax.fori_loop(0, 4, pair, 0)


def zero_grads(r):
    def step(i, _):
        z = jnp.zeros((4, TILE, 128), F32)
        r.dq[:, rows_of(i), :] = z
        r.dk[:, rows_of(i), :] = z
        r.dv[:, rows_of(i), :] = z
        return 0

    lax.fori_loop(0, 4, step, 0)


def vec(r, row):
    return r.vecs[row : row + 1, :]


def add_vec(r, row, value):
    r.vg[row] += value


def project_self(r, i):
    rows = rows_of(i)
    x = r.tokens[rows, :]
    heads_split(r.q, rows, ((mm(x, r.w[0, :, 0:512]) + vec(r, 0)).astype(BF) * 0.125).astype(BF))
    heads_split(r.k, rows, mm(x, r.w[0, :, 512:1024]).astype(BF))
    heads_split(r.v, rows, (mm(x, r.w[0, :, 1024:1536]) + vec(r, 1)).astype(BF))


def self_bias(r, i, start, count):
    qs = r.tcol[rows_of(i), 0:1]
    ks = r.trow[0:1, start : start + count]
    at = lax.broadcasted_iota(jnp.int32, (TILE, count), 0) + i * TILE
    key = lax.broadcasted_iota(jnp.int32, (TILE, count), 1) + start
    r.bias[:, 0:count] = jnp.where((qs == ks) & (key <= at), 0.0, MASKED)


def after_self(r, i):
    rows = rows_of(i)
    a = heads_join(r.a, rows)
    z = r.tokens[rows, :].astype(F32) + (mm(a, r.w[0, :, 1536:2048]) + vec(r, 2))
    n, inverse = normed(z)
    r.n1[rows, :] = n
    r.r1[rows, :] = jnp.broadcast_to(inverse, (TILE, 128))
    y = (n * vec(r, 3) + vec(r, 4)).astype(BF)
    r.y1[rows, :] = y
    heads_split(r.q2, rows, ((mm(y, r.w[1, :, 0:512]) + vec(r, 5)).astype(BF) * 0.125).astype(BF))


def project_cross(r, i):
    rows = rows_of(i)
    m = r.memory[rows, :]
    heads_split(r.k2, rows, mm(m, r.w[1, :, 512:1024]).astype(BF))
    heads_split(r.v2, rows, (mm(m, r.w[1, :, 1024:1536]) + vec(r, 6)).astype(BF))


def cross_bias(r, i):
    qs = r.tcol[rows_of(i), 0:1]
    ks = r.srow[0:1, :]
    r.bias[...] = jnp.where(qs == ks, 0.0, MASKED)


def middle(r, i):
    rows = rows_of(i)
    y1 = r.n1[rows, :] * vec(r, 3) + vec(r, 4)
    z2 = y1 + (mm(heads_join(r.a2, rows), r.w[1, :, 1536:2048]) + vec(r, 7))
    n2, r2 = normed(z2)
    y2 = n2 * vec(r, 8) + vec(r, 9)
    y2l = y2.astype(BF)
    r.y2[rows, :] = y2l
    f = jnp.zeros((TILE, 512), F32)
    for c in range(4):
        cols = slice(c * 512, (c + 1) * 512)
        u = mm(y2l, r.w[2, :, cols]) + vec(r, 10 + c)
        s = jax.nn.sigmoid(u)
        hd = (u * s).astype(BF)
        r.hd[rows, cols] = hd
        r.gate[:, cols] = s * (1.0 + u * (1.0 - s))
        f = f + mm_t(hd, r.w[3, :, cols])
    n3, r3 = normed(y2 + (f + vec(r, 14)))
    r.layer_out[rows, :] = (n3 * vec(r, 15) + vec(r, 16)).astype(BF)
    g = r.out_grad[rows, :].astype(F32)
    add_vec(r, 15, fold(g * n3))
    add_vec(r, 16, fold(g))
    dz3 = norm_back(g, n3, r3, vec(r, 15))
    df = dz3.astype(BF)
    r.df[rows, :] = df
    add_vec(r, 14, fold(df))
    dy2 = dz3
    for c in range(4):
        cols = slice(c * 512, (c + 1) * 512)
        du = (mm(df, r.w[3, :, cols]) * r.gate[:, cols]).astype(BF)
        r.du[rows, cols] = du
        add_vec(r, 10 + c, fold(du))
        dy2 = dy2 + mm_t(du, r.w[2, :, cols])
    add_vec(r, 8, fold(dy2 * n2))
    add_vec(r, 9, fold(dy2))
    dz2 = norm_back(dy2, n2, r2, vec(r, 8))
    r.dz[rows, :] = dz2
    db = dz2.astype(BF)
    r.db[rows, :] = db
    add_vec(r, 7, fold(db))
    heads_split(r.da, rows, mm_t(db, r.w[1, :, 1536:2048]).astype(BF))
    deltas(r, r.a2, r.da, r.delta, i)


def finish_heads(r, i, scale_rows):
    rows = rows_of(i)
    r.g[rows, 0:512] = (heads_join(r.dq, rows) * 0.125).astype(BF)
    r.g[rows, 512:1024] = heads_join(r.dk, rows).astype(BF)
    r.g[rows, 1024:1536] = heads_join(r.dv, rows).astype(BF)
    add_vec(r, scale_rows, fold(r.g[rows, 0:512]))
    add_vec(r, scale_rows + 1, fold(r.g[rows, 1024:1536]))


def after_cross_back(r, i):
    rows = rows_of(i)
    dq, dk, dv = r.g[rows, 0:512], r.g[rows, 512:1024], r.g[rows, 1024:1536]
    r.memory_grad[rows, :] = mm_t(dk, r.w[1, :, 512:1024]) + mm_t(dv, r.w[1, :, 1024:1536])
    dy1 = r.dz[rows, :] + mm_t(dq, r.w[1, :, 0:512])
    n1 = r.n1[rows, :]
    add_vec(r, 3, fold(dy1 * n1))
    add_vec(r, 4, fold(dy1))
    dz1 = norm_back(dy1, n1, r.r1[rows, 0:1], vec(r, 3))
    r.dz[rows, :] = dz1
    db = dz1.astype(BF)
    r.db[rows, :] = db
    add_vec(r, 2, fold(db))
    heads_split(r.da, rows, mm_t(db, r.w[0, :, 1536:2048]).astype(BF))
    deltas(r, r.a, r.da, r.delta, i)


def after_self_back(r, i):
    rows = rows_of(i)
    dq, dk, dv = r.g[rows, 0:512], r.g[rows, 512:1024], r.g[rows, 1024:1536]
    r.input_grad[rows, :] = r.dz[rows, :] + (
        mm_t(dq, r.w[0, :, 0:512]) + mm_t(dk, r.w[0, :, 512:1024]) + mm_t(dv, r.w[0, :, 1024:1536])
    )


def cross_bias_t(r, i, j):
    ks = r.scol[rows_of(j), 0:1]
    qs = r.trow[0:1, rows_of(i)]
    r.bias_t[...] = jnp.where(ks == qs, 0.0, MASKED)


def self_bias_t(r, i, j):
    ks = r.tcol[rows_of(j), 0:1]
    qs = r.trow[0:1, rows_of(i)]
    key = lax.broadcasted_iota(jnp.int32, (TILE, TILE), 0) + j * TILE
    at = lax.broadcasted_iota(jnp.int32, (TILE, TILE), 1) + i * TILE
    r.bias_t[...] = jnp.where((ks == qs) & (key <= at), 0.0, MASKED)


def loop(n, body):
    def step(i, _):
        body(i)
        return 0

    lax.fori_loop(0, n, step, 0)


def flip(r, source):
    def one(i):
        r.xt[:, rows_of(i)] = source(rows_of(i)).T

    loop(4, one)


def weight_grad(r, chunk_of, count, emit):
    def one(c):
        cols = pl.ds(pl.multiple_of(c * 256, 256), 256)
        emit(c, mm(r.xt[...], chunk_of(cols)))

    loop(count, one)


def run(r, emit, hook=lambda name: None):

    segments(r, r.tlen, r.trow, r.tcol)
    segments(r, r.slen, r.srow, r.scol)

    def clear(i):
        r.vg[i] = jnp.zeros((8, 512), F32)

    loop(24, clear)
    hook("start")
    loop(4, lambda i: project_self(r, i))
    hook("projected")
    for i in range(4):
        start = max(0, i - 2) * TILE
        count = (i + 1) * TILE - start
        self_bias(r, i, start, count)
        attend(r, r.q, r.k, r.v, r.a, r.lse, i, start, count, r.bias)
        hook("self%d" % i)
    loop(4, lambda i: project_cross(r, i))
    loop(4, lambda i: after_self(r, i))
    hook("cross_ready")

    def cross(i):
        cross_bias(r, i)
        attend(r, r.q2, r.k2, r.v2, r.a2, r.lse2, i, 0, 1024, r.bias)

    loop(4, cross)
    hook("crossed")
    loop(4, lambda i: middle(r, i))
    flip(r, lambda rows: r.df[rows, :])
    weight_grad(r, lambda cols: r.hd[:, cols], 8, emit(3, 0))
    flip(r, lambda rows: r.y2[rows, :])
    weight_grad(r, lambda cols: r.du[:, cols], 8, emit(2, 0))
    flip(r, lambda rows: heads_join(r.a2, rows))
    weight_grad(r, lambda cols: r.db[:, cols], 2, emit(1, 6))
    hook("ffn_grads")
    zero_grads(r)

    def cross_back(t):
        i, j = t % 4, t // 4
        cross_bias_t(r, i, j)
        attend_back(r, r.q2, r.k2, r.v2, r.da, r.lse2, r.delta, r.bias_t, i, j)

    loop(16, cross_back)
    loop(4, lambda i: finish_heads(r, i, 5))
    flip(r, lambda rows: r.y1[rows, :])
    weight_grad(r, lambda cols: r.g[:, cols], 2, emit(1, 0))
    flip(r, lambda rows: r.memory[rows, :])
    weight_grad(r, lambda cols: r.g[:, pl.ds(cols.start + 512, 256)], 4, emit(1, 2))
    loop(4, lambda i: after_cross_back(r, i))
    flip(r, lambda rows: heads_join(r.a, rows))
    weight_grad(r, lambda cols: r.db[:, cols], 2, emit(0, 6))
    hook("cross_grads")
    zero_grads(r)

    def self_back_keys(j, _):
        def self_back(i, _):
            self_bias_t(r, i, j)
            attend_back(r, r.q, r.k, r.v, r.da, r.lse, r.delta, r.bias_t, i, j)
            return 0

        return lax.fori_loop(j, jnp.minimum(j + 3, 4), self_back, 0)

    lax.fori_loop(0, 4, self_back_keys, 0)
    loop(4, lambda i: finish_heads(r, i, 0))
    flip(r, lambda rows: r.tokens[rows, :])
    weight_grad(r, lambda cols: r.g[:, cols], 6, emit(0, 0))
    hook("self_grads")
    loop(4, lambda i: after_self_back(r, i))


SCRATCH = [
    ("trow", (8, 1024), jnp.int32), ("tcol", (1024, 128), jnp.int32),
    ("srow", (8, 1024), jnp.int32), ("scol", (1024, 128), jnp.int32),
    ("q", (4, 1024, 128), BF), ("k", (4, 1024, 128), BF), ("v", (4, 1024, 128), BF), ("a", (4, 1024, 128), BF),
    ("q2", (4, 1024, 128), BF), ("k2", (4, 1024, 128), BF), ("v2", (4, 1024, 128), BF), ("a2", (4, 1024, 128), BF),
    ("da", (4, 1024, 128), BF), ("lse", (8, 1, 1024), F32), ("lse2", (8, 1, 1024), F32), ("delta", (8, 1, 1024), F32),
    ("n1", (1024, 512), F32), ("r1", (1024, 128), F32), ("y1", (1024, 512), BF), ("y2", (1024, 512), BF),
    ("hd", (1024, 2048), BF), ("du", (1024, 2048), BF), ("df", (1024, 512), BF), ("db", (1024, 512), BF),
    ("gate", (256, 2048), F32), ("dz", (1024, 512), F32), ("bias", (256, 1024), F32), ("bias_t", (256, 256), F32),
    ("dq", (4, 1024, 128), F32), ("dk", (4, 1024, 128), F32), ("dv", (4, 1024, 128), F32),
    ("xt", (512, 1024), BF), ("vg", (24, 8, 512), F32),
]


def plain_kernel(tlen, slen, tokens, memory, out_grad, w, vecs, layer_out, input_grad, memory_grad, mat_grad, vec_grad, stage, sems, *scratch):
    r = Bag()
    r.tlen, r.slen, r.tokens, r.memory, r.out_grad, r.w, r.vecs = tlen, slen, tokens, memory, out_grad, w, vecs
    r.layer_out, r.input_grad, r.memory_grad = layer_out, input_grad, memory_grad
    for (name, _, _), ref in zip(SCRATCH, scratch):
        setattr(r, name, ref)
    r.g = r.du

    def emit(m, first):
        def one(c, value):
            stage[...] = value
            cp = pltpu.make_async_copy(stage, mat_grad.at[m, :, pl.ds(pl.multiple_of((first + c) * 256, 256), 256)], sems)
            cp.start()
            cp.wait()
        return one

    run(r, emit)
    vec_grad[...] = jnp.sum(r.vg[...], axis=1)


def plain(tlen, slen, tokens, memory, out_grad, w, vecs):
    V = pl.BlockSpec(memory_space=pltpu.VMEM)
    S = pl.BlockSpec(memory_space=pltpu.SMEM)
    return pl.pallas_call(
        plain_kernel,
        out_shape=(
            jax.ShapeDtypeStruct((1024, 512), BF), jax.ShapeDtypeStruct((1024, 512), F32), jax.ShapeDtypeStruct((1024, 512), F32),
            jax.ShapeDtypeStruct((4, 512, 2048), F32), jax.ShapeDtypeStruct((24, 512), F32)),
        in_specs=[S, S, V, V, V, V, V],
        out_specs=(V, V, V, pl.BlockSpec(memory_space=pl.ANY), V),
        scratch_shapes=[pltpu.VMEM((512, 256), F32), pltpu.SemaphoreType.DMA] + [pltpu.VMEM(s, d) for _, s, d in SCRATCH],
        compiler_params=pltpu.CompilerParams(vmem_limit_bytes=63400000),
        name="layer",
    )(tlen, slen, tokens, memory, out_grad, w, vecs)


def adam_update(params, grad_in, moments, factor):
    clipped = factor * grad_in
    first_m = BETA_ONE * moments[0] + (1.0 - BETA_ONE) * clipped
    second_m = BETA_TWO * moments[1] + (1.0 - BETA_TWO) * clipped * clipped
    stepped = first_m / CORRECT_ONE / (jnp.sqrt(second_m / CORRECT_TWO) + ADAM_EPS)
    return (-LEARN_RATE * (stepped + WEIGHT_DECAY * params), first_m, second_m)


def generic_body(tokens, memory, target_lengths, source_lengths, out_grad, weights, vectors, weight_moments, vector_moments):
    axes = ("dp", "shard")
    w = lax.all_gather(weights.astype(BF), axes, axis=1, tiled=True)
    vecs = lax.all_gather(vectors.astype(BF), axes, axis=1, tiled=True).astype(F32)
    vecs = jnp.concatenate([vecs, jnp.zeros((VROWS - vecs.shape[0], vecs.shape[1]), F32)], axis=0)
    layer_out, input_grad, memory_grad, mat_grad, vec_grad = plain(
        target_lengths, source_lengths, tokens, memory, out_grad, w, vecs
    )
    mat_share = lax.psum_scatter(mat_grad, axes, scatter_dimension=1, tiled=True)
    vec_share = lax.psum_scatter(vec_grad[: vectors.shape[0]], axes, scatter_dimension=1, tiled=True)
    squares = jnp.sum(mat_share * mat_share) + jnp.sum(vec_share * vec_share)
    grad_norm = jnp.sqrt(lax.psum(squares, axes))
    factor = jnp.minimum(1.0, CLIP_NORM / (grad_norm + 1e-06))
    weight_steps, weight_first, weight_second = adam_update(weights, mat_share, weight_moments, factor)
    vector_steps, vector_first, vector_second = adam_update(vectors, vec_share, vector_moments, factor)
    return (
        layer_out, input_grad, memory_grad, grad_norm, mat_share, vec_share,
        weight_steps, vector_steps, weight_first, weight_second, vector_first, vector_second,
    )


def solution(mesh):
    both = ("dp", "shard")
    rows, mats, vecs = P(both, None), P(None, both, None), P(None, both)
    return jax.shard_map(
        generic_body,
        mesh=mesh,
        in_specs=(rows, rows, rows, rows, rows, mats, vecs, P(None, None, both, None), P(None, None, both)),
        out_specs=(rows, rows, rows, P(), mats, vecs, mats, vecs, mats, mats, vecs, vecs),
        check_vma=False,
    )
```

```python
import functools
import jax
import jax.numpy as jnp
from jax import lax
from jax.experimental import pallas as pl
from jax.experimental.pallas import tpu as pltpu
from jax.sharding import PartitionSpec as P

HD = 64
EPSILON = 1e-05
MASKED = -1e30
BF = jnp.bfloat16
F32 = jnp.float32
TILE = 256
VROWS = 24
MESH = pl.DeviceIdType.MESH
CLIP_NORM = 1.0
LEARN_RATE = 0.001
BETA_ONE = 0.9
BETA_TWO = 0.999
ADAM_EPS = 1e-08
WEIGHT_DECAY = 0.1
CORRECT_ONE = 1.0 - 0.9**3
CORRECT_TWO = 1.0 - 0.999**3


def mm(left, right):
    return jnp.dot(left, right, preferred_element_type=F32)


def mm_t(left, right):
    return lax.dot_general(left, right, (((1,), (1,)), ((), ())), preferred_element_type=F32)


def t_mm(left, right):
    return lax.dot_general(left, right, (((0,), (0,)), ((), ())), preferred_element_type=F32)


def rows_of(i, size=TILE):
    return pl.ds(pl.multiple_of(i * size, size), size)


def normed(z):
    centred = z - jnp.mean(z, axis=-1, keepdims=True)
    inverse = lax.rsqrt(jnp.mean(centred * centred, axis=-1, keepdims=True) + EPSILON)
    return centred * inverse, inverse


def norm_back(grad, n, inverse, gain):
    scaled = grad * gain
    return inverse * (
        scaled
        - jnp.mean(scaled, axis=-1, keepdims=True)
        - n * jnp.mean(scaled * n, axis=-1, keepdims=True)
    )


def fold(values):
    r, c = values.shape
    return jnp.sum(values.astype(F32).reshape(r // 8, 8, c), axis=0)


def heads_join(ref, rows):
    return jnp.concatenate([ref[p, rows, :] for p in range(4)], axis=1)


def heads_split(ref, rows, value):
    for p in range(4):
        ref[p, rows, :] = value[:, p * 128 : (p + 1) * 128]


class Bag:
    pass


def head_mask(h, dtype):
    lane = lax.broadcasted_iota(jnp.int32, (1, 128), 1)
    return jnp.where((lane < HD) if h == 0 else (lane >= HD), 1.0, 0.0).astype(dtype)


def segments(r, lengths, row_ref, lane):
    ends = []
    total = jnp.int32(0)
    for s in range(16):
        total = total + lengths[0, s]
        ends.append(total)

    def number(at):
        seg = jnp.zeros(at.shape, F32)
        for e in ends:
            seg = seg + jnp.where(e <= at, 1.0, 0.0)
        return seg

    row_ref[...] = number(lax.broadcasted_iota(jnp.int32, (8, 1024), 1))

    def col(i):
        r.cols[rows_of(i), lane : lane + 1] = number(lax.broadcasted_iota(jnp.int32, (TILE, 128), 0) + i * TILE)[:, 0:1]

    loop(4, col)


def attend(r, q_ref, k_ref, v_ref, out_ref, lse_ref, tile, key_start, key_count, bias):
    rows = rows_of(tile)
    keys = pl.ds(key_start, key_count)
    lane = lax.broadcasted_iota(jnp.int32, (TILE, 128), 1)

    def pair(p, lses):
        q = q_ref[p, rows, :]
        k = k_ref[p, keys, :]
        v = v_ref[p, keys, :]
        outs = []
        for h in range(2):
            s = mm_t(q * head_mask(h, BF), k) + bias[:, :key_count]
            top = jnp.max(s, axis=-1, keepdims=True)
            e = jnp.exp(s - top)
            total = jnp.sum(e, axis=-1, keepdims=True)
            outs.append(mm(e.astype(BF), v) * (1.0 / total))
            lses = jnp.where(lane == 2 * p + h, top + jnp.log(total), lses)
        out_ref[p, rows, :] = jnp.where(lane < HD, outs[0], outs[1]).astype(BF)
        return lses

    lses = lax.fori_loop(0, 4, pair, jnp.zeros((TILE, 128), F32))
    flipped = lses.T
    for h in range(8):
        lse_ref[h, :, rows_of(tile)] = flipped[h : h + 1, :]


def deltas(r, out_ref, grad_ref, delta_ref, tile):
    rows = rows_of(tile)
    lane = lax.broadcasted_iota(jnp.int32, (TILE, 128), 1)
    table = jnp.zeros((TILE, 128), F32)
    for p in range(4):
        prod = out_ref[p, rows, :].astype(F32) * grad_ref[p, rows, :].astype(F32)
        for h in range(2):
            one = jnp.sum(prod * head_mask(h, F32), axis=-1, keepdims=True)
            table = jnp.where(lane == 2 * p + h, one, table)
    flipped = table.T
    for h in range(8):
        delta_ref[h, :, rows] = flipped[h : h + 1, :]


def attend_back(r, q_ref, k_ref, v_ref, grad_ref, lse_ref, delta_ref, bias, i, j):
    qr, kr = rows_of(i), rows_of(j)
    lane = lax.broadcasted_iota(jnp.int32, (TILE, 128), 1)

    def pair(p, _):
        q, k, v, g = q_ref[p, qr, :], k_ref[p, kr, :], v_ref[p, kr, :], grad_ref[p, qr, :]
        dv, dk, dq = [], [], []
        for h in range(2):
            m = head_mask(h, BF)
            s = mm_t(k * m, q) + bias[...]
            w = jnp.exp(s - lse_ref[2 * p + h, :, qr])
            dp = mm_t(v * m, g)
            ds = (w * (dp - delta_ref[2 * p + h, :, qr])).astype(BF)
            dv.append(mm(w.astype(BF), g))
            dk.append(mm(ds, q))
            dq.append(t_mm(ds, k))
        r.dv[p, kr, :] += jnp.where(lane < HD, dv[0], dv[1])
        r.dk[p, kr, :] += jnp.where(lane < HD, dk[0], dk[1])
        r.dq[p, qr, :] += jnp.where(lane < HD, dq[0], dq[1])
        return 0

    lax.fori_loop(0, 4, pair, 0)


def zero_grads(r):
    def step(i, _):
        z = jnp.zeros((4, TILE, 128), F32)
        r.dq[:, rows_of(i), :] = z
        r.dk[:, rows_of(i), :] = z
        r.dv[:, rows_of(i), :] = z
        return 0

    lax.fori_loop(0, 4, step, 0)


def vec(r, row):
    return r.vecs[row : row + 1, :]


def add_vec(r, row, value):
    r.vg[row] += value


def project_self(r, i):
    rows = rows_of(i)
    x = r.tokens[rows, :]
    heads_split(r.q, rows, ((mm(x, r.w(0, 0, 512)) + vec(r, 0)).astype(BF) * 0.125).astype(BF))
    heads_split(r.k, rows, mm(x, r.w(0, 512, 1024)).astype(BF))
    heads_split(r.v, rows, (mm(x, r.w(0, 1024, 1536)) + vec(r, 1)).astype(BF))


def self_bias(r, i, start, count):
    qs = r.cols[rows_of(i), 0:1]
    ks = r.trow[0:1, start : start + count]
    at = lax.broadcasted_iota(jnp.int32, (TILE, count), 0) + i * TILE
    key = lax.broadcasted_iota(jnp.int32, (TILE, count), 1) + start
    r.bias[:, 0:count] = jnp.where((qs == ks) & (key <= at), 0.0, MASKED)


def after_self(r, i):
    rows = rows_of(i)
    a = heads_join(r.a, rows)
    z = r.tokens[rows, :].astype(F32) + (mm(a, r.w(0, 1536, 2048)) + vec(r, 2))
    n, inverse = normed(z)
    r.n1[rows, :] = n
    r.cols[rows, 2:3] = inverse
    y = (n * vec(r, 3) + vec(r, 4)).astype(BF)
    r.y1[rows, :] = y
    heads_split(r.q2, rows, ((mm(y, r.w(1, 0, 512)) + vec(r, 5)).astype(BF) * 0.125).astype(BF))


def project_cross(r, i):
    rows = rows_of(i)
    m = r.memory[rows, :]
    heads_split(r.k2, rows, mm(m, r.w(1, 512, 1024)).astype(BF))
    heads_split(r.v2, rows, (mm(m, r.w(1, 1024, 1536)) + vec(r, 6)).astype(BF))


def cross_bias(r, i):
    qs = r.cols[rows_of(i), 0:1]
    ks = r.srow[0:1, :]
    r.bias[...] = jnp.where(qs == ks, 0.0, MASKED)


def middle(r, i):
    rows = rows_of(i)
    y1 = r.n1[rows, :] * vec(r, 3) + vec(r, 4)
    z2 = y1 + (mm(heads_join(r.a2, rows), r.w(1, 1536, 2048)) + vec(r, 7))
    n2, r2 = normed(z2)
    y2 = n2 * vec(r, 8) + vec(r, 9)
    y2l = y2.astype(BF)
    r.y2[rows, :] = y2l
    f = jnp.zeros((TILE, 512), F32)
    for c in range(4):
        cols = slice(c * 512, (c + 1) * 512)
        u = mm(y2l, r.w(2, cols.start, cols.stop)) + vec(r, 10 + c)
        s = jax.nn.sigmoid(u)
        hd = (u * s).astype(BF)
        r.put_hidden(i, cols, hd)
        r.gate[:, cols] = s * (1.0 + u * (1.0 - s))
        f = f + mm_t(hd, r.w(3, cols.start, cols.stop))
    n3, r3 = normed(y2 + (f + vec(r, 14)))
    r.put_layer_out(i, (n3 * vec(r, 15) + vec(r, 16)).astype(BF))
    g = r.get_out_grad(i).astype(F32)
    add_vec(r, 15, fold(g * n3))
    add_vec(r, 16, fold(g))
    dz3 = norm_back(g, n3, r3, vec(r, 15))
    df = dz3.astype(BF)
    r.df[rows, :] = df
    add_vec(r, 14, fold(df))
    dy2 = dz3
    for c in range(4):
        cols = slice(c * 512, (c + 1) * 512)
        du = (mm(df, r.w(3, cols.start, cols.stop)) * r.gate[:, cols]).astype(BF)
        r.du[rows, cols] = du
        add_vec(r, 10 + c, fold(du))
        dy2 = dy2 + mm_t(du, r.w(2, cols.start, cols.stop))
    add_vec(r, 8, fold(dy2 * n2))
    add_vec(r, 9, fold(dy2))
    dz2 = norm_back(dy2, n2, r2, vec(r, 8))
    r.dz[rows, :] = dz2
    db = dz2.astype(BF)
    r.db[rows, :] = db
    add_vec(r, 7, fold(db))
    heads_split(r.da, rows, mm_t(db, r.w(1, 1536, 2048)).astype(BF))
    deltas(r, r.a2, r.da, r.delta, i)


def finish_heads(r, i, scale_rows):
    rows = rows_of(i)
    r.g[rows, 0:512] = (heads_join(r.dq, rows) * 0.125).astype(BF)
    r.g[rows, 512:1024] = heads_join(r.dk, rows).astype(BF)
    r.g[rows, 1024:1536] = heads_join(r.dv, rows).astype(BF)
    add_vec(r, scale_rows, fold(r.g[rows, 0:512]))
    add_vec(r, scale_rows + 1, fold(r.g[rows, 1024:1536]))


def after_cross_back(r, i):
    rows = rows_of(i)
    dq, dk, dv = r.g[rows, 0:512], r.g[rows, 512:1024], r.g[rows, 1024:1536]
    r.put_memory_grad(i, mm_t(dk, r.w(1, 512, 1024)) + mm_t(dv, r.w(1, 1024, 1536)))
    dy1 = r.dz[rows, :] + mm_t(dq, r.w(1, 0, 512))
    n1 = r.n1[rows, :]
    add_vec(r, 3, fold(dy1 * n1))
    add_vec(r, 4, fold(dy1))
    dz1 = norm_back(dy1, n1, r.cols[rows, 2:3], vec(r, 3))
    r.dz[rows, :] = dz1
    db = dz1.astype(BF)
    r.db[rows, :] = db
    add_vec(r, 2, fold(db))
    heads_split(r.da, rows, mm_t(db, r.w(0, 1536, 2048)).astype(BF))
    deltas(r, r.a, r.da, r.delta, i)


def after_self_back(r, i):
    rows = rows_of(i)
    dq, dk, dv = r.g[rows, 0:512], r.g[rows, 512:1024], r.g[rows, 1024:1536]
    r.put_input_grad(
        i,
        r.dz[rows, :]
        + (mm_t(dq, r.w(0, 0, 512)) + mm_t(dk, r.w(0, 512, 1024)) + mm_t(dv, r.w(0, 1024, 1536))),
    )


def cross_bias_t(r, i, j):
    ks = r.cols[rows_of(j), 1:2]
    qs = r.trow[0:1, rows_of(i)]
    r.bias[:, 0:TILE] = jnp.where(ks == qs, 0.0, MASKED)


def self_bias_t(r, i, j):
    ks = r.cols[rows_of(j), 0:1]
    qs = r.trow[0:1, rows_of(i)]
    key = lax.broadcasted_iota(jnp.int32, (TILE, TILE), 0) + j * TILE
    at = lax.broadcasted_iota(jnp.int32, (TILE, TILE), 1) + i * TILE
    r.bias[:, 0:TILE] = jnp.where((ks == qs) & (key <= at), 0.0, MASKED)


def loop(n, body):
    def step(i, _):
        body(i)
        return 0

    lax.fori_loop(0, n, step, 0)


def flip(r, source):
    def one(i):
        r.xt[:, rows_of(i)] = source(rows_of(i)).T

    loop(4, one)


def weight_grad(r, chunk_of, count, emit):
    def one(c):
        cols = pl.ds(pl.multiple_of(c * 256, 256), 256)
        emit(c, mm(r.xt[...], chunk_of(cols)))

    loop(count, one)


def run(r, emit, hook=lambda name: None, at_step=lambda name, t: None):
    segments(r, r.tlen, r.trow, 0)
    segments(r, r.slen, r.srow, 1)

    def clear(i):
        r.vg[i] = jnp.zeros((8, 512), F32)

    loop(VROWS, clear)
    hook("start")
    loop(4, lambda i: project_self(r, i))
    hook("projected")
    for i in range(4):
        start = max(0, i - 2) * TILE
        count = (i + 1) * TILE - start
        self_bias(r, i, start, count)
        attend(r, r.q, r.k, r.v, r.a, r.lse, i, start, count, r.bias)
        hook("self%d" % i)
    loop(4, lambda i: project_cross(r, i))
    loop(4, lambda i: after_self(r, i))
    hook("cross_ready")

    def cross(i):
        cross_bias(r, i)
        attend(r, r.q2, r.k2, r.v2, r.a2, r.lse2, i, 0, 1024, r.bias)
        at_step("cross", i)

    loop(4, cross)
    hook("crossed")
    loop(4, lambda i: middle(r, i))
    hook("middle")
    flip(r, lambda rows: r.df[rows, :])
    weight_grad(r, r.get_hidden, 8, emit(3, 0))
    hook("grads3")
    flip(r, lambda rows: r.y2[rows, :])
    weight_grad(r, lambda cols: r.du[:, cols], 8, emit(2, 0))
    hook("grads2")
    flip(r, lambda rows: heads_join(r.a2, rows))
    weight_grad(r, lambda cols: r.db[:, cols], 2, emit(1, 6))
    hook("grads1o")
    zero_grads(r)

    def cross_back(t):
        i, j = t % 4, t // 4
        cross_bias_t(r, i, j)
        attend_back(r, r.q2, r.k2, r.v2, r.da, r.lse2, r.delta, r.bias.at[:, 0:TILE], i, j)
        at_step("cross_back", t)

    loop(16, cross_back)
    loop(4, lambda i: finish_heads(r, i, 5))
    flip(r, lambda rows: r.y1[rows, :])
    weight_grad(r, lambda cols: r.g[:, cols], 2, emit(1, 0))
    flip(r, lambda rows: r.memory[rows, :])
    weight_grad(r, lambda cols: r.g[:, pl.ds(cols.start + 512, 256)], 4, emit(1, 2))
    hook("grads1")
    loop(4, lambda i: after_cross_back(r, i))
    flip(r, lambda rows: heads_join(r.a, rows))
    weight_grad(r, lambda cols: r.db[:, cols], 2, emit(0, 6))
    hook("grads0o")
    zero_grads(r)
    for gap in range(3):

        def self_back(j):
            self_bias_t(r, j + gap, j)
            attend_back(r, r.q, r.k, r.v, r.da, r.lse, r.delta, r.bias.at[:, 0:TILE], j + gap, j)
            at_step("self_back%d" % gap, j)

        loop(4 - gap, self_back)
    loop(4, lambda i: finish_heads(r, i, 0))
    flip(r, lambda rows: r.tokens[rows, :])
    weight_grad(r, lambda cols: r.g[:, cols], 6, emit(0, 0))
    hook("grads0")
    loop(4, lambda i: after_self_back(r, i))


SCRATCH = [
    ("trow", (8, 1024), F32), ("srow", (8, 1024), F32), ("cols", (1024, 128), F32),
    ("q", (4, 1024, 128), BF), ("k", (4, 1024, 128), BF), ("v", (4, 1024, 128), BF), ("a", (4, 1024, 128), BF),
    ("q2", (4, 1024, 128), BF), ("k2", (4, 1024, 128), BF), ("v2", (4, 1024, 128), BF), ("a2", (4, 1024, 128), BF),
    ("da", (4, 1024, 128), BF), ("lse", (8, 1, 1024), F32), ("lse2", (8, 1, 1024), F32), ("delta", (8, 1, 1024), F32),
    ("n1", (1024, 512), F32), ("y1", (1024, 512), BF), ("y2", (1024, 512), BF),
    ("hd", (2, 2, 4, 2, 2, 16, 2048), BF), ("du", (1024, 2048), BF), ("df", (1024, 512), BF), ("db", (1024, 512), BF),
    ("gate", (256, 2048), F32), ("dz", (1024, 512), F32), ("bias", (256, 1024), F32),
    ("dq", (4, 1024, 128), F32), ("dk", (4, 1024, 128), F32), ("dv", (4, 1024, 128), F32),
    ("xt", (512, 1024), BF), ("vg", (24, 8, 512), F32),
]


def hidden_access(r):
    def put(i, cols, value):
        r.hd[i // 2, i % 2, :, :, :, :, cols] = value.reshape(4, 2, 2, 16, 512)

    def get(cols):
        return r.hd[:, :, :, :, :, :, cols].reshape(1024, 256)

    r.put_hidden, r.get_hidden = put, get


def plain_kernel(
    tlen, slen, tokens, memory, out_grad, w, vecs, layer_out, input_grad, memory_grad, mat_grad, vec_grad, stage, sem, *scratch
):
    r = Bag()
    r.tlen, r.slen, r.tokens, r.memory, r.vecs = tlen, slen, tokens, memory, vecs
    for (name, _, _), ref in zip(SCRATCH, scratch):
        setattr(r, name, ref)
    r.g = r.du
    r.w = lambda m, a, b: w[m, :, a:b]
    hidden_access(r)
    r.get_out_grad = lambda i: out_grad[rows_of(i), :]

    def put_to(ref):
        def put(i, value):
            ref[rows_of(i), :] = value

        return put

    r.put_layer_out, r.put_memory_grad, r.put_input_grad = put_to(layer_out), put_to(memory_grad), put_to(input_grad)

    def emit(m, first):
        def one(c, value):
            stage[...] = value
            cols = pl.ds(pl.multiple_of((first + c) * 256, 256), 256)
            copy = pltpu.make_async_copy(stage, mat_grad.at[m, :, cols], sem)
            copy.start()
            copy.wait()

        return one

    run(r, emit)
    vec_grad[...] = jnp.sum(r.vg[...], axis=1)


def plain(tlen, slen, tokens, memory, out_grad, w, vecs):
    V = pl.BlockSpec(memory_space=pltpu.VMEM)
    S = pl.BlockSpec(memory_space=pltpu.SMEM)
    return pl.pallas_call(
        plain_kernel,
        out_shape=(
            jax.ShapeDtypeStruct((1024, 512), BF),
            jax.ShapeDtypeStruct((1024, 512), F32),
            jax.ShapeDtypeStruct((1024, 512), F32),
            jax.ShapeDtypeStruct((4, 512, 2048), F32),
            jax.ShapeDtypeStruct((VROWS, 512), F32),
        ),
        in_specs=[S, S, V, V, V, V, V],
        out_specs=(V, V, V, pl.BlockSpec(memory_space=pl.ANY), V),
        scratch_shapes=[pltpu.VMEM((512, 256), F32), pltpu.SemaphoreType.DMA] + [pltpu.VMEM(s, d) for _, s, d in SCRATCH],
        compiler_params=pltpu.CompilerParams(vmem_limit_bytes=63400000),
        name="layer",
    )(tlen, slen, tokens, memory, out_grad, w, vecs)


class Place:
    def __init__(self):
        dp, sh = lax.axis_index("dp"), lax.axis_index("shard")
        self.z, self.y, self.x, self.c = dp // 2, dp % 2, sh // 2, sh % 2
        z, y, x, c = self.z, self.y, self.x, self.c
        self.y1, self.x1 = y + c * (1 - 2 * y), x + (1 - c) * (1 - 2 * x)
        self.y2, self.x2 = y + (1 - c) * (1 - 2 * y), x + c * (1 - 2 * x)
        self.y3, self.x3 = 1 - y, 1 - x
        self.i1, self.i2 = x * (1 - c) + y * c, y * (1 - c) + x * c
        self.first = (z * 2 + self.y1, self.x1 * 2 + c)
        self.second = (z * 2 + self.y2, self.x2 * 2 + c)
        self.twin = (z * 2 + y, x * 2 + 1 - c)

    def along_z(self, d):
        return (lax.rem(self.z + d, 4) * 2 + self.y, self.x * 2 + self.c)

    def in_plane(self, n):
        flat = lax.rem(self.y * 4 + self.x * 2 + self.c + n, 8)
        return (self.z * 2 + flat // 4, flat % 4)


class Gather:
    def __init__(self, at, ref, cols, index, send, recv):
        self.at, self.ref, self.cols, self.index, self.send, self.recv = at, ref, cols, index, send, recv
        self.started = []

    def column(self, y, x, c):
        return self.ref.at[:, y, x, c, :, self.cols]

    def copy(self, slot, what, device):
        return pltpu.make_async_remote_copy(
            src_ref=what,
            dst_ref=what,
            send_sem=self.send.at[self.index, slot],
            recv_sem=self.recv.at[self.index, slot],
            device_id=device,
            device_id_type=MESH,
        )

    def go(self, slot, what, device):
        copy = self.copy(slot, what, device)
        copy.start()
        self.started.append(copy)

    def step0(self):
        p = self.at
        for d in range(1, 4):
            self.go(d - 1, self.ref.at[p.z, p.y, p.x, p.c, :, self.cols], p.along_z(d))

    def step1(self):
        p = self.at
        for d in range(1, 4):
            self.copy(d - 1, self.ref.at[lax.rem(p.z + 4 - d, 4), p.y, p.x, p.c, :, self.cols], p.along_z(d)).wait_recv()
        own = self.column(p.y, p.x, p.c)
        self.go(3, own, p.second)
        self.go(4, own, p.first)
        self.go(5, own, p.twin)

    def step2(self):
        p = self.at
        got = self.column(p.y2, p.x2, p.c)
        self.copy(3, got, p.second).wait_recv()
        self.go(6, got, p.first)
        self.go(7, got, p.twin)

    def step3(self):
        p = self.at
        got = self.column(p.y1, p.x1, p.c)
        self.copy(4, got, p.first).wait_recv()
        self.go(8, got, p.twin)
        far = self.column(p.y3, p.x3, p.c)
        self.copy(6, far, p.first).wait_recv()
        self.go(9, far, p.twin)

    def step4(self):
        p = self.at
        for slot, y, x in ((5, p.y, p.x), (7, p.y1, p.x1), (8, p.y2, p.x2), (9, p.y3, p.x3)):
            self.copy(slot, self.column(y, x, 1 - p.c), p.twin).wait_recv()

    def finish(self):
        for copy in self.started:
            copy.wait_send()
        self.started = []


class Reduce:
    def __init__(self, at, keep, give, recvs, own, cols, index, send, recv):
        self.at, self.keep, self.give, self.recvs, self.own, self.cols = at, keep, give, recvs, own, cols
        self.index, self.send, self.recv = index, send, recv

    def copy(self, slot):
        p, cols = self.at, self.cols
        if slot == 0:
            what, where, device = self.give.at[:, :, :, :, cols], self.recvs[0].at[:, :, :, :, cols], p.twin
        elif slot == 1:
            what, where, device = self.keep.at[:, :, 1 - p.i1, :, cols], self.recvs[1].at[:, :, :, cols], p.first
        elif slot == 2:
            what, where, device = self.keep.at[:, 1 - p.i2, p.i1, :, cols], self.recvs[2].at[:, :, cols], p.second
        else:
            d = slot - 2
            what = self.keep.at[lax.rem(p.z + d, 4), p.i2, p.i1, :, cols]
            where, device = self.recvs[3].at[d - 1, :, cols], p.along_z(d)
        return pltpu.make_async_remote_copy(
            src_ref=what,
            dst_ref=where,
            send_sem=self.send.at[self.index, slot],
            recv_sem=self.recv.at[self.index, slot],
            device_id=device,
            device_id_type=MESH,
        )

    def step0(self):
        self.copy(0).start()

    def step1(self):
        cols = self.cols
        self.copy(0).wait_recv()

        def add(z):
            self.keep[z, :, :, :, cols] = (
                self.keep[z, :, :, :, cols].astype(F32) + self.recvs[0][z, :, :, :, cols].astype(F32)
            ).astype(BF)

        loop(4, add)
        self.copy(1).start()

    def step2(self):
        p, cols = self.at, self.cols
        self.copy(1).wait_recv()
        self.keep[:, :, p.i1, :, cols] = (
            self.keep[:, :, p.i1, :, cols].astype(F32) + self.recvs[1][:, :, :, cols].astype(F32)
        ).astype(BF)
        self.copy(2).start()

    def step3(self):
        p, cols = self.at, self.cols
        self.copy(2).wait_recv()
        self.keep[:, p.i2, p.i1, :, cols] = (
            self.keep[:, p.i2, p.i1, :, cols].astype(F32) + self.recvs[2][:, :, cols].astype(F32)
        ).astype(BF)
        for slot in range(3, 6):
            self.copy(slot).start()

    def step4(self):
        p, cols = self.at, self.cols
        total = self.keep[p.z, p.i2, p.i1, :, cols].astype(F32)
        for slot in range(3, 6):
            self.copy(slot).wait_recv()
            total = total + self.recvs[3][slot - 3, :, cols].astype(F32)
        self.own[:, cols] = total

    def finish(self):
        for slot in range(6):
            self.copy(slot).wait_send()


def steps_of(jobs, names=("step0", "step1", "step2", "step3", "step4"), ready=None):
    ticks = []
    for t in range(len(jobs) + len(names) - 1):
        tick = []
        for s in range(len(names)):
            k = t - s
            if 0 <= k < len(jobs):
                tick.append(getattr(jobs[k], names[s]))
        ticks.append(tick)
    return ticks


FUSED_SCRATCH = [
    ("g0", (4, 2, 2, 2, 16, 2176), BF),
    ("g1", (4, 2, 2, 2, 16, 2048), BF),
    ("g2", (4, 2, 2, 2, 16, 2048), BF),
    ("g3", (4, 2, 2, 2, 16, 2048), BF),
    ("own", (64, 2048), F32),
    ("square", (128, 128), F32),
    ("vecs", (VROWS, 512), F32),
    ("ra", (4, 4, 2, 2, 16, 2048), BF),
    ("rb", (4, 4, 2, 16, 2048), BF),
    ("rc", (4, 4, 16, 2048), BF),
    ("rd", (4, 3, 16, 2048), BF),
    ("vkeep", (4, 2, 2, 16, 128), BF),
    ("vgive", (4, 2, 2, 16, 128), BF),
    ("va", (4, 2, 2, 16, 128), BF),
    ("vb", (4, 2, 16, 128), BF),
    ("vc", (4, 16, 128), BF),
    ("vd", (3, 16, 128), BF),
    ("vown", (16, 128), F32),
    ("nsend", (2, 8, 128), F32),
    ("nrecv", (10, 8, 128), F32),
]
N_GATHER = 12
N_REDUCE = 7


def adam_parts(params, grad_in, first, second, factor):
    clipped = factor * grad_in
    first_m = BETA_ONE * first + (1.0 - BETA_ONE) * clipped
    second_m = BETA_TWO * second + (1.0 - BETA_TWO) * clipped * clipped
    stepped = first_m / CORRECT_ONE / (jnp.sqrt(second_m / CORRECT_TWO) + ADAM_EPS)
    return (-LEARN_RATE * (stepped + WEIGHT_DECAY * params), first_m, second_m)


def fused_kernel(
    tlen, slen, tokens, memory, out_grad, weights, vectors, moments, vector_moments,
    layer_out, input_grad, memory_grad, norm_out, mat_out, vec_out, step_out, vstep_out, first_out, second_out, vfirst_out, vsecond_out,
    *scratch,
):
    r = Bag()
    names = [n for n, _, _ in SCRATCH] + [n for n, _, _ in FUSED_SCRATCH]
    for name, ref in zip(names, scratch):
        setattr(r, name, ref)
    g_send, g_recv, s_send, s_recv, n_send, n_recv, l_sem = scratch[len(names) :]
    p = Place()
    r.tlen, r.slen, r.tokens, r.memory = tlen, slen, tokens, memory
    r.g = r.du
    hidden_access(r)
    mats = [r.g0, r.g1, r.g2, r.g3]

    def w(m, a, b):
        shift = 128 if m == 0 else 0
        return mats[m][:, :, :, :, :, a + shift : b + shift].reshape(512, b - a)

    r.w = w

    barrier = pltpu.get_barrier_semaphore()
    for d in range(1, 4):
        pl.semaphore_signal(barrier, inc=1, device_id=p.along_z(d), device_id_type=MESH)
    for n in range(1, 8):
        pl.semaphore_signal(barrier, inc=1, device_id=p.in_plane(n), device_id_type=MESH)

    local = []

    def fetch(k, src, dst):
        copy = pltpu.make_async_copy(src, dst, l_sem.at[k])
        copy.start()
        local.append(copy)
        return copy

    weights_in = fetch(0, weights, r.gate.at[128:192, :])
    grad_in = fetch(1, out_grad, r.db)
    r.square[...] = jnp.zeros((128, 128), F32)
    r.square[0:17, 0:16] = vectors[...]
    r.g0[p.z, p.y, p.x, p.c, :, 0:128] = r.square[...].T[0:16, :].astype(BF)
    weights_in.wait()
    for m in range(4):
        shift = 128 if m == 0 else 0
        mats[m][p.z, p.y, p.x, p.c, :, shift : shift + 2048] = r.gate[128 + 16 * m : 144 + 16 * m, :].astype(BF)
    pl.semaphore_wait(barrier, 10)

    gathers = []
    for m, cuts in ((0, (0, 640, 1152, 1664, 2176)), (1, (0, 512, 1024, 1536, 2048)), (2, (0, 1024, 2048)), (3, (0, 1024, 2048))):
        for a, b in zip(cuts[:-1], cuts[1:]):
            gathers.append(Gather(p, mats[m], slice(a, b), len(gathers), g_send, g_recv))
    ticks = steps_of(gathers)

    def run_ticks(n):
        for _ in range(n):
            if ticks:
                for action in ticks.pop(0):
                    action()

    keeps = {0: r.hd.at[1, 0], 1: r.hd.at[0, 0], 2: r.g2.at[:, :, :, 0], 3: r.g3.at[:, :, :, 0]}
    gives = {0: r.hd.at[1, 1], 1: r.hd.at[0, 1], 2: r.g2.at[:, :, :, 1], 3: r.g3.at[:, :, :, 1]}

    def spread(value, keep, give, cols):
        v = value.reshape(4, 2, 2, 2, 16, value.shape[-1])
        flag = p.c == 0
        for y in range(2):
            for x in range(2):
                i1, i2 = x * (1 - p.c) + y * p.c, y * (1 - p.c) + x * p.c
                even, odd = v[:, y, x, 0], v[:, y, x, 1]
                keep[:, i2, i1, :, cols] = jnp.where(flag, even, odd).astype(BF)
                give[:, i1, i2, :, cols] = jnp.where(flag, odd, even).astype(BF)

    def emit(m, first):
        def one(c, value):
            spread(value, keeps[m], gives[m], pl.ds(pl.multiple_of((first + c) * 256, 256), 256))

        return one

    def job(k, m, a, b):
        return Reduce(
            p, keeps[m], gives[m], (r.ra.at[m], r.rb.at[m], r.rc.at[m], r.rd.at[m]),
            r.own.at[16 * m : 16 * m + 16, :], slice(a, b), k, s_send, s_recv,
        )

    j3, j2, j1o, j1, j0o, j0 = (
        job(0, 3, 0, 2048), job(1, 2, 0, 2048), job(2, 1, 1536, 2048), job(3, 1, 0, 1536), job(4, 0, 1536, 2048), job(5, 0, 0, 1536),
    )
    jv = Reduce(p, r.vkeep, r.vgive, (r.va, r.vb, r.vc, r.vd), r.vown, slice(0, 128), 6, s_send, s_recv)
    jobs = [j3, j2, j1o, j1, j0o, j0, jv]

    def hook(name):
        if name == "start":
            run_ticks(5)
            for b in range(4):
                block = r.g0[b, :, :, :, :, 0:128].reshape(128, 128).astype(F32)
                r.vecs[:, b * 128 : (b + 1) * 128] = block.T[0:VROWS, :]
            run_ticks(2)
        elif name in ("projected", "self0", "self1", "self2", "self3"):
            run_ticks(1)
            if name == "self3":
                run_ticks(1)
        elif name == "cross_ready":
            run_ticks(2)
        elif name == "crossed":
            run_ticks(len(ticks))
            grad_in.wait()
        elif name == "middle":
            for g in gathers:
                g.finish()
            for copy in out_copies:
                copy.wait()
        elif name == "grads3":
            j3.step0()
        elif name == "grads2":
            j2.step0()
            j3.step1()
        elif name == "grads1o":
            j1o.step0()
            j2.step1()
            j3.step2()
        elif name == "grads1":
            j1.step0()
        elif name == "grads0o":
            j0o.step0()
            j1.step1()
        elif name == "grads0":
            j0.step0()

    plan = {
        "cross_back": {2: [j3.step3, j2.step2], 5: [j3.step4, j2.step3], 8: [j2.step4, j1o.step1], 10: [j1o.step2], 12: [j1o.step3], 14: [j1o.step4]},
        "self_back0": {0: [j0o.step1], 2: [j1.step2]},
        "self_back1": {0: [j0o.step2], 2: [j1.step3]},
        "self_back2": {0: [j0o.step3, j1.step4], 1: [j0o.step4]},
    }

    def at_step(name, t):
        for when, actions in plan.get(name, {}).items():

            @pl.when(t == when)
            def _():
                for action in actions:
                    action()

    r.get_out_grad = lambda i: r.db[rows_of(i), :]
    out_copies = []

    def put_layer_out(i, value):
        for k in range(4):

            @pl.when(i == k)
            def _():
                part = r.xt.at[(k // 2) * 256 : (k // 2) * 256 + 256, (k % 2) * 512 : (k % 2) * 512 + 512]
                part[...] = value
                pltpu.make_async_copy(part, layer_out.at[k * 256 : k * 256 + 256, :], l_sem.at[2 + k]).start()

    for k in range(4):
        part = r.xt.at[(k // 2) * 256 : (k // 2) * 256 + 256, (k % 2) * 512 : (k % 2) * 512 + 512]
        out_copies.append(pltpu.make_async_copy(part, layer_out.at[k * 256 : k * 256 + 256, :], l_sem.at[2 + k]))
    r.put_layer_out = put_layer_out

    def memory_part(k):
        return pltpu.make_async_copy(
            r.gate.at[:, k * 512 : k * 512 + 512], memory_grad.at[k * 256 : k * 256 + 256, :], l_sem.at[6 + k]
        )

    def put_memory_grad(i, value):
        for k in range(4):

            @pl.when(i == k)
            def _():
                r.gate[:, k * 512 : k * 512 + 512] = value
                memory_part(k).start()

    r.put_memory_grad = put_memory_grad

    def input_part(i, k):
        return pltpu.make_async_copy(r.dz.at[rows_of(i), :], input_grad.at[rows_of(i), :], l_sem.at[10 + k])

    def put_input_grad(i, value):
        r.dz[rows_of(i), :] = value
        for k in range(4):

            @pl.when(i == k)
            def _():
                input_part(k, k).start()

    r.put_input_grad = put_input_grad

    run(r, emit, hook, at_step)

    for k in range(4):
        memory_part(k).wait()
    moments_in = fetch(14, moments, r.gate.at[0:128, :])
    weights_again = fetch(15, weights, r.gate.at[128:192, :])
    sums = jnp.sum(r.vg[...], axis=1)
    sums = jnp.concatenate([sums, jnp.zeros((128 - VROWS, 512), F32)], axis=0)
    spread(
        jnp.concatenate([sums[:, b * 128 : (b + 1) * 128].T for b in range(4)], axis=0),
        r.vkeep, r.vgive, slice(0, 128),
    )
    jv.step0()
    for name in ("step1", "step2", "step3", "step4"):
        getattr(j0, name)()
        getattr(jv, name)()

    def square(i):
        r.nsend[0] += jnp.broadcast_to(jnp.sum(r.own[pl.ds(pl.multiple_of(i * 8, 8), 8), :] ** 2), (8, 128))

    r.nsend[0] = jnp.broadcast_to(jnp.sum(r.vown[...] * r.vown[...]), (8, 128))
    loop(8, square)
    sends = []
    for n in range(1, 8):
        sends.append(
            pltpu.make_async_remote_copy(
                src_ref=r.nsend.at[0], dst_ref=r.nrecv.at[n - 1], send_sem=n_send.at[n - 1], recv_sem=n_recv.at[n - 1],
                device_id=p.in_plane(n), device_id_type=MESH,
            )
        )
        sends[-1].start()
    total = r.nsend[0]
    for n in range(7):
        sends[n].wait_recv()
        total = total + r.nrecv[n]
    r.nsend[1] = total
    for d in range(1, 4):
        sends.append(
            pltpu.make_async_remote_copy(
                src_ref=r.nsend.at[1], dst_ref=r.nrecv.at[6 + d], send_sem=n_send.at[6 + d], recv_sem=n_recv.at[6 + d],
                device_id=p.along_z(d), device_id_type=MESH,
            )
        )
        sends[-1].start()
    for d in range(3):
        sends[7 + d].wait_recv()
        total = total + r.nrecv[7 + d]
    norm = jnp.sqrt(total)
    norm_out[...] = norm
    factor = jnp.minimum(1.0, CLIP_NORM / (norm[0:1, 0:1] + 1e-06))
    r.square[...] = jnp.zeros((128, 128), F32)
    r.square[0:16, :] = r.vown[...]
    vgrad = r.square[...].T[0:17, 0:16]
    vec_out[...] = vgrad
    vstep_out[...], vfirst_out[...], vsecond_out[...] = adam_parts(
        vectors[...], vgrad, vector_moments[0], vector_moments[1], factor
    )
    moments_in.wait()
    weights_again.wait()
    puts = [pltpu.make_async_copy(r.own, mat_out, l_sem.at[16])]
    puts[0].start()

    def update(i):
        a, b, c = (pl.ds(pl.multiple_of(i * 16 + o, 16), 16) for o in (0, 64, 128))
        s, f, v = adam_parts(r.gate[c, :], r.own[a, :], r.gate[a, :], r.gate[b, :], factor)
        r.gate[a, :] = f
        r.gate[b, :] = v
        r.gate[c, :] = s

    loop(4, update)
    for k, (ref, a) in enumerate(((first_out, 0), (second_out, 64), (step_out, 128))):
        puts.append(pltpu.make_async_copy(r.gate.at[a : a + 64, :], ref, l_sem.at[17 + k]))
        puts[-1].start()
    for k in range(4):
        input_part(k, k).wait()
    for j in jobs:
        j.finish()
    for s in sends:
        s.wait_send()
    for s in puts:
        s.wait()


def fused_body(tokens, memory, target_lengths, source_lengths, out_grad, weights, vectors, weight_moments, vector_moments):
    V = pl.BlockSpec(memory_space=pltpu.VMEM)
    S = pl.BlockSpec(memory_space=pltpu.SMEM)
    A = pl.BlockSpec(memory_space=pl.ANY)
    mat = jax.ShapeDtypeStruct((64, 2048), F32)
    vec_shape = jax.ShapeDtypeStruct(vectors.shape, F32)
    big = jax.ShapeDtypeStruct(tokens.shape, F32)
    layer_out, input_grad, memory_grad, norm, g, vg, st, vst, m1, m2, vm1, vm2 = pl.pallas_call(
        fused_kernel,
        out_shape=(
            jax.ShapeDtypeStruct(tokens.shape, BF), big, big, jax.ShapeDtypeStruct((8, 128), F32),
            mat, vec_shape, mat, vec_shape, mat, mat, vec_shape, vec_shape,
        ),
        in_specs=[S, S, V, V, A, A, V, A, V],
        out_specs=(A, A, A, V, A, V, A, V, A, A, V, V),
        scratch_shapes=[pltpu.VMEM(s, d) for _, s, d in SCRATCH + FUSED_SCRATCH]
        + [
            pltpu.SemaphoreType.DMA((N_GATHER, 10)),
            pltpu.SemaphoreType.DMA((N_GATHER, 10)),
            pltpu.SemaphoreType.DMA((N_REDUCE, 6)),
            pltpu.SemaphoreType.DMA((N_REDUCE, 6)),
            pltpu.SemaphoreType.DMA((10,)),
            pltpu.SemaphoreType.DMA((10,)),
            pltpu.SemaphoreType.DMA((20,)),
        ],
        compiler_params=pltpu.CompilerParams(vmem_limit_bytes=63400000, collective_id=0, has_side_effects=True),
        name="layer",
    )(
        target_lengths, source_lengths, tokens, memory, out_grad, weights.reshape(64, 2048), vectors,
        weight_moments.reshape(128, 2048), vector_moments,
    )
    back = lambda a: a.reshape(weights.shape)
    return (layer_out, input_grad, memory_grad, norm[0, 0], back(g), vg, back(st), vst, back(m1), back(m2), vm1, vm2)


def adam_update(params, grad_in, moments, factor):
    clipped = factor * grad_in
    first_m = BETA_ONE * moments[0] + (1.0 - BETA_ONE) * clipped
    second_m = BETA_TWO * moments[1] + (1.0 - BETA_TWO) * clipped * clipped
    stepped = first_m / CORRECT_ONE / (jnp.sqrt(second_m / CORRECT_TWO) + ADAM_EPS)
    return (-LEARN_RATE * (stepped + WEIGHT_DECAY * params), first_m, second_m)


def generic_body(tokens, memory, target_lengths, source_lengths, out_grad, weights, vectors, weight_moments, vector_moments):
    axes = ("dp", "shard")
    w = lax.all_gather(weights.astype(BF), axes, axis=1, tiled=True)
    vecs = lax.all_gather(vectors.astype(BF), axes, axis=1, tiled=True).astype(F32)
    vecs = jnp.concatenate([vecs, jnp.zeros((VROWS - vecs.shape[0], vecs.shape[1]), F32)], axis=0)
    layer_out, input_grad, memory_grad, mat_grad, vec_grad = plain(
        target_lengths, source_lengths, tokens, memory, out_grad, w, vecs
    )
    mat_share = lax.psum_scatter(mat_grad, axes, scatter_dimension=1, tiled=True)
    vec_share = lax.psum_scatter(vec_grad[: vectors.shape[0]], axes, scatter_dimension=1, tiled=True)
    squares = jnp.sum(mat_share * mat_share) + jnp.sum(vec_share * vec_share)
    grad_norm = jnp.sqrt(lax.psum(squares, axes))
    factor = jnp.minimum(1.0, CLIP_NORM / (grad_norm + 1e-06))
    weight_steps, weight_first, weight_second = adam_update(weights, mat_share, weight_moments, factor)
    vector_steps, vector_first, vector_second = adam_update(vectors, vec_share, vector_moments, factor)
    return (
        layer_out, input_grad, memory_grad, grad_norm, mat_share, vec_share,
        weight_steps, vector_steps, weight_first, weight_second, vector_first, vector_second,
    )


def solution(mesh):
    both = ("dp", "shard")
    rows, mats, vecs = P(both, None), P(None, both, None), P(None, both)
    fits = (mesh.shape["dp"], mesh.shape["shard"]) == (8, 4)
    return jax.shard_map(
        fused_body if fits else generic_body,
        mesh=mesh,
        in_specs=(rows, rows, rows, rows, rows, mats, vecs, P(None, None, both, None), P(None, None, both)),
        out_specs=(rows, rows, rows, P(), mats, vecs, mats, vecs, mats, mats, vecs, vecs),
        check_vma=False,
    )
```

```python
import functools
import jax
import jax.numpy as jnp
from jax import lax
from jax.experimental import pallas as pl
from jax.experimental.pallas import tpu as pltpu
from jax.sharding import PartitionSpec as P

HD = 64
EPSILON = 1e-05
MASKED = -1e30
BF = jnp.bfloat16
F32 = jnp.float32
TILE = 256
VROWS = 24
FWD_UNROLL = 2
BACK_UNROLL = 2
CROSS_KEYS = 512
MESH = pl.DeviceIdType.MESH
CLIP_NORM = 1.0
LEARN_RATE = 0.001
BETA_ONE = 0.9
BETA_TWO = 0.999
ADAM_EPS = 1e-08
WEIGHT_DECAY = 0.1
CORRECT_ONE = 1.0 - 0.9**3
CORRECT_TWO = 1.0 - 0.999**3


def mm(left, right):
    return jnp.dot(left, right, preferred_element_type=F32)


def mm_t(left, right):
    return lax.dot_general(left, right, (((1,), (1,)), ((), ())), preferred_element_type=F32)


def t_mm(left, right):
    return lax.dot_general(left, right, (((0,), (0,)), ((), ())), preferred_element_type=F32)


def rows_of(i, size=TILE):
    return pl.ds(pl.multiple_of(i * size, size), size)


def normed(z):
    centred = z - jnp.mean(z, axis=-1, keepdims=True)
    inverse = lax.rsqrt(jnp.mean(centred * centred, axis=-1, keepdims=True) + EPSILON)
    return centred * inverse, inverse


def norm_back(grad, n, inverse, gain):
    scaled = grad * gain
    return inverse * (
        scaled
        - jnp.mean(scaled, axis=-1, keepdims=True)
        - n * jnp.mean(scaled * n, axis=-1, keepdims=True)
    )


def fold(values):
    r, c = values.shape
    return jnp.sum(values.astype(F32).reshape(r // 8, 8, c), axis=0)


def heads_join(ref, rows):
    return jnp.concatenate([ref[p, rows, :] for p in range(4)], axis=1)


def heads_split(ref, rows, value):
    for p in range(4):
        ref[p, rows, :] = value[:, p * 128 : (p + 1) * 128]


class Bag:
    pass


def head_mask(h, dtype):
    lane = lax.broadcasted_iota(jnp.int32, (1, 128), 1)
    return jnp.where((lane < HD) if h == 0 else (lane >= HD), 1.0, 0.0).astype(dtype)


def segments(r, lengths, row_ref, lane):
    ends = []
    total = jnp.int32(0)
    for s in range(16):
        total = total + lengths[0, s]
        ends.append(total)

    def number(at):
        seg = jnp.zeros(at.shape, F32)
        for e in ends:
            seg = seg + jnp.where(e <= at, 1.0, 0.0)
        return seg

    row_ref[...] = number(lax.broadcasted_iota(jnp.int32, (8, 1024), 1))

    def col(i):
        r.cols[rows_of(i), lane : lane + 1] = number(lax.broadcasted_iota(jnp.int32, (TILE, 128), 0) + i * TILE)[:, 0:1]

    loop(4, col)


def attend(r, q_ref, k_ref, v_ref, out_ref, lse_ref, tile, key_start, key_count, bias):
    rows = rows_of(tile)
    keys = pl.ds(key_start, key_count)
    lane = lax.broadcasted_iota(jnp.int32, (TILE, 128), 1)

    def pair(p, _):
        q = q_ref[p, rows, :]
        k = k_ref[p, keys, :]
        v = v_ref[p, keys, :]
        tops, weights, values = [], [], []
        for h in range(2):
            m = head_mask(h, BF)
            s = mm_t(q * m, k) + bias[:, :key_count]
            tops.append(jnp.max(s, axis=-1, keepdims=True))
            weights.append(jnp.exp(s - tops[h]).astype(BF))
            values.append(jnp.concatenate([v * m, jnp.broadcast_to(m, (key_count, 128))], axis=1))
        both = mm(jnp.concatenate(weights, axis=1), jnp.concatenate(values, axis=0))
        total = both[:, 128:256]
        out_ref[p, rows, :] = (both[:, 0:128] * (1.0 / total)).astype(BF)
        lse = (jnp.where(lane < HD, tops[0], tops[1]) + jnp.log(total)).T
        lse_ref[2 * p, :, rows] = lse[0:1, :]
        lse_ref[2 * p + 1, :, rows] = lse[HD : HD + 1, :]
        return 0

    lax.fori_loop(0, 4, pair, 0, unroll=FWD_UNROLL)


def deltas(r, out_ref, grad_ref, delta_ref, tile):
    rows = rows_of(tile)
    lane = lax.broadcasted_iota(jnp.int32, (TILE, 128), 1)
    table = jnp.zeros((TILE, 128), F32)
    for p in range(4):
        prod = out_ref[p, rows, :].astype(F32) * grad_ref[p, rows, :].astype(F32)
        for h in range(2):
            one = jnp.sum(prod * head_mask(h, F32), axis=-1, keepdims=True)
            table = jnp.where(lane == 2 * p + h, one, table)
    flipped = table.T
    for h in range(8):
        delta_ref[h, :, rows] = flipped[h : h + 1, :]


def attend_back(r, q_ref, k_ref, v_ref, grad_ref, lse_ref, delta_ref, i, key_start, key_count, pairs, unroll):
    qr, kr = rows_of(i), pl.ds(key_start, key_count)
    lane = lax.broadcasted_iota(jnp.int32, (TILE, 128), 1)
    key_lane = lax.broadcasted_iota(jnp.int32, (key_count, 128), 1)

    def pair(p, _):
        q, k, v, g = q_ref[p, qr, :], k_ref[p, kr, :], v_ref[p, kr, :], grad_ref[p, qr, :]
        dv, dk, dq = [], [], []
        for h in range(2):
            m = head_mask(h, BF)
            s = mm_t(k * m, q) + r.bias[0:key_count, :]
            w = jnp.exp(s - lse_ref[2 * p + h, :, qr])
            dp = mm_t(v * m, g)
            ds = (w * (dp - delta_ref[2 * p + h, :, qr])).astype(BF)
            dv.append(mm(w.astype(BF), g))
            dk.append(mm(ds, q))
            dq.append(t_mm(ds, k))
        r.dv[p, kr, :] += jnp.where(key_lane < HD, dv[0], dv[1])
        r.dk[p, kr, :] += jnp.where(key_lane < HD, dk[0], dk[1])
        r.dq[p, qr, :] += jnp.where(lane < HD, dq[0], dq[1])
        return 0

    lax.fori_loop(pairs[0], pairs[1], pair, 0, unroll=unroll)


def zero_grads(r):
    def step(i, _):
        z = jnp.zeros((4, TILE, 128), F32)
        r.dq[:, rows_of(i), :] = z
        r.dk[:, rows_of(i), :] = z
        r.dv[:, rows_of(i), :] = z
        return 0

    lax.fori_loop(0, 4, step, 0)


def vec(r, row):
    return r.vecs[row : row + 1, :]


def add_vec(r, row, value):
    r.vg[row] += value


def project_self(r, i):
    rows = rows_of(i)
    x = r.tokens[rows, :]
    heads_split(r.q, rows, ((mm(x, r.w(0, 0, 512)) + vec(r, 0)).astype(BF) * 0.125).astype(BF))
    heads_split(r.k, rows, mm(x, r.w(0, 512, 1024)).astype(BF))
    heads_split(r.v, rows, (mm(x, r.w(0, 1024, 1536)) + vec(r, 1)).astype(BF))


def self_bias(r, i, start, count):
    qs = r.cols[rows_of(i), 0:1]
    ks = r.trow[0:1, start : start + count]
    at = lax.broadcasted_iota(jnp.int32, (TILE, count), 0) + i * TILE
    key = lax.broadcasted_iota(jnp.int32, (TILE, count), 1) + start
    r.gate[:, 0:count] = jnp.where((qs == ks) & (key <= at), 0.0, MASKED)


def after_self(r, i):
    rows = rows_of(i)
    a = heads_join(r.a, rows)
    z = r.tokens[rows, :].astype(F32) + (mm(a, r.w(0, 1536, 2048)) + vec(r, 2))
    n, inverse = normed(z)
    r.n1[rows, :] = n
    r.cols[rows, 2:3] = inverse
    y = (n * vec(r, 3) + vec(r, 4)).astype(BF)
    r.y1[rows, :] = y
    heads_split(r.q2, rows, ((mm(y, r.w(1, 0, 512)) + vec(r, 5)).astype(BF) * 0.125).astype(BF))


def project_cross(r, i):
    rows = rows_of(i)
    m = r.memory[rows, :]
    heads_split(r.k2, rows, mm(m, r.w(1, 512, 1024)).astype(BF))
    heads_split(r.v2, rows, (mm(m, r.w(1, 1024, 1536)) + vec(r, 6)).astype(BF))


def cross_bias(r, i):
    qs = r.cols[rows_of(i), 0:1]
    ks = r.srow[0:1, :]
    r.gate[:, 0:1024] = jnp.where(qs == ks, 0.0, MASKED)


def middle(r, i):
    rows = rows_of(i)
    y1 = r.n1[rows, :] * vec(r, 3) + vec(r, 4)
    z2 = y1 + (mm(heads_join(r.a2, rows), r.w(1, 1536, 2048)) + vec(r, 7))
    n2, r2 = normed(z2)
    y2 = n2 * vec(r, 8) + vec(r, 9)
    y2l = y2.astype(BF)
    r.y2[rows, :] = y2l
    f = jnp.zeros((TILE, 512), F32)
    for c in range(4):
        cols = slice(c * 512, (c + 1) * 512)
        u = mm(y2l, r.w(2, cols.start, cols.stop)) + vec(r, 10 + c)
        s = jax.nn.sigmoid(u)
        hd = (u * s).astype(BF)
        r.put_hidden(i, cols, hd)
        r.gate[:, cols] = s * (1.0 + u * (1.0 - s))
        f = f + mm_t(hd, r.w(3, cols.start, cols.stop))
    n3, r3 = normed(y2 + (f + vec(r, 14)))
    r.put_layer_out(i, (n3 * vec(r, 15) + vec(r, 16)).astype(BF))
    g = r.get_out_grad(i).astype(F32)
    add_vec(r, 15, fold(g * n3))
    add_vec(r, 16, fold(g))
    dz3 = norm_back(g, n3, r3, vec(r, 15))
    df = dz3.astype(BF)
    r.df[rows, :] = df
    add_vec(r, 14, fold(df))
    dy2 = dz3
    for c in range(4):
        cols = slice(c * 512, (c + 1) * 512)
        du = (mm(df, r.w(3, cols.start, cols.stop)) * r.gate[:, cols]).astype(BF)
        r.du[rows, cols] = du
        add_vec(r, 10 + c, fold(du))
        dy2 = dy2 + mm_t(du, r.w(2, cols.start, cols.stop))
    add_vec(r, 8, fold(dy2 * n2))
    add_vec(r, 9, fold(dy2))
    dz2 = norm_back(dy2, n2, r2, vec(r, 8))
    r.dz[rows, :] = dz2
    db = dz2.astype(BF)
    r.db[rows, :] = db
    add_vec(r, 7, fold(db))
    heads_split(r.da, rows, mm_t(db, r.w(1, 1536, 2048)).astype(BF))
    deltas(r, r.a2, r.da, r.delta, i)


def finish_heads(r, i, vector_row, pairs=(0, 4)):
    rows = rows_of(i)
    a, b = pairs[0] * 128, pairs[1] * 128
    for part, (ref, scale) in enumerate(((r.dq, 0.125), (r.dk, 1.0), (r.dv, 1.0))):
        value = jnp.concatenate([ref[p, rows, :] for p in range(*pairs)], axis=1)
        value = (value * scale).astype(BF)
        r.g[rows, 512 * part + a : 512 * part + b] = value
        if part != 1:
            r.vg[vector_row + part // 2, :, a:b] += fold(value)


def after_cross_back(r, i):
    rows = rows_of(i)
    dq, dk, dv = r.g[rows, 0:512], r.g[rows, 512:1024], r.g[rows, 1024:1536]
    r.put_memory_grad(i, mm_t(dk, r.w(1, 512, 1024)) + mm_t(dv, r.w(1, 1024, 1536)))
    dy1 = r.dz[rows, :] + mm_t(dq, r.w(1, 0, 512))
    n1 = r.n1[rows, :]
    add_vec(r, 3, fold(dy1 * n1))
    add_vec(r, 4, fold(dy1))
    dz1 = norm_back(dy1, n1, r.cols[rows, 2:3], vec(r, 3))
    r.dz[rows, :] = dz1
    db = dz1.astype(BF)
    r.db[rows, :] = db
    add_vec(r, 2, fold(db))
    heads_split(r.da, rows, mm_t(db, r.w(0, 1536, 2048)).astype(BF))
    deltas(r, r.a, r.da, r.delta, i)


def after_self_back(r, i):
    rows = rows_of(i)
    dq, dk, dv = r.g[rows, 0:512], r.g[rows, 512:1024], r.g[rows, 1024:1536]
    r.put_input_grad(
        i,
        r.dz[rows, :]
        + (mm_t(dq, r.w(0, 0, 512)) + mm_t(dk, r.w(0, 512, 1024)) + mm_t(dv, r.w(0, 1024, 1536))),
    )


def cross_bias_t(r, i, key_start, key_count):
    ks = r.cols[pl.ds(key_start, key_count), 1:2]
    qs = r.trow[0:1, rows_of(i)]
    r.bias[0:key_count, :] = jnp.where(ks == qs, 0.0, MASKED)


def self_bias_t(r, i, key_start, key_count):
    ks = r.cols[pl.ds(key_start, key_count), 0:1]
    qs = r.trow[0:1, rows_of(i)]
    key = lax.broadcasted_iota(jnp.int32, (key_count, TILE), 0) + key_start
    at = lax.broadcasted_iota(jnp.int32, (key_count, TILE), 1) + i * TILE
    r.bias[0:key_count, :] = jnp.where((ks == qs) & (key <= at), 0.0, MASKED)


def loop(n, body):
    def step(i, _):
        body(i)
        return 0

    lax.fori_loop(0, n, step, 0)


def flip(r, source):
    def one(i):
        r.xt[:, rows_of(i)] = source(rows_of(i)).T

    loop(4, one)


def weight_grad(r, chunk_of, count, emit):
    def one(c):
        cols = pl.ds(pl.multiple_of(c * 256, 256), 256)
        emit(c, mm(r.xt[...], chunk_of(cols)))

    loop(count, one)


def run(r, emit, hook=lambda name: None, at_step=lambda name, t: None):
    hook("enter")
    segments(r, r.tlen, r.trow, 0)
    segments(r, r.slen, r.srow, 1)

    def clear(i):
        r.vg[i] = jnp.zeros((8, 512), F32)

    loop(VROWS, clear)
    hook("start")
    loop(4, lambda i: project_self(r, i))
    hook("projected")
    for i in range(4):
        start = max(0, i - 2) * TILE
        count = (i + 1) * TILE - start
        self_bias(r, i, start, count)
        attend(r, r.q, r.k, r.v, r.a, r.lse, i, start, count, r.gate)
        hook("self%d" % i)
    loop(4, lambda i: project_cross(r, i))
    loop(4, lambda i: after_self(r, i))
    hook("cross_ready")

    def cross(i):
        cross_bias(r, i)
        attend(r, r.q2, r.k2, r.v2, r.a2, r.lse2, i, 0, 1024, r.gate)
        at_step("cross", i)

    loop(4, cross)
    hook("crossed")
    loop(4, lambda i: middle(r, i))
    hook("middle")
    flip(r, lambda rows: r.df[rows, :])
    weight_grad(r, r.get_hidden, 8, emit(3, 0))
    hook("grads3")
    flip(r, lambda rows: r.y2[rows, :])
    weight_grad(r, lambda cols: r.du[:, cols], 8, emit(2, 0))
    hook("grads2")
    flip(r, lambda rows: heads_join(r.a2, rows))
    weight_grad(r, lambda cols: r.db[:, cols], 2, emit(1, 6))
    hook("grads1o")
    zero_grads(r)

    parts = 1024 // CROSS_KEYS

    def cross_back(t):
        i, start = t // parts, pl.multiple_of(t % parts * CROSS_KEYS, CROSS_KEYS)
        cross_bias_t(r, i, start, CROSS_KEYS)
        attend_back(r, r.q2, r.k2, r.v2, r.da, r.lse2, r.delta, i, start, CROSS_KEYS, (0, 4), BACK_UNROLL)
        at_step("cross_back", t)

    loop(4 * parts, cross_back)
    loop(4, lambda i: finish_heads(r, i, 5))
    flip(r, lambda rows: r.y1[rows, :])
    weight_grad(r, lambda cols: r.g[:, cols], 2, emit(1, 0))
    flip(r, lambda rows: r.memory[rows, :])
    weight_grad(r, lambda cols: r.g[:, pl.ds(cols.start + 512, 256)], 4, emit(1, 2))
    hook("grads1")
    loop(4, lambda i: after_cross_back(r, i))
    flip(r, lambda rows: heads_join(r.a, rows))
    weight_grad(r, lambda cols: r.db[:, cols], 2, emit(0, 6))
    hook("grads0o")
    zero_grads(r)
    flip(r, lambda rows: r.tokens[rows, :])
    for half in range(2):
        pairs = (2 * half, 2 * half + 2)
        for i in range(4):
            start = max(0, i - 2) * TILE
            count = (i + 1) * TILE - start
            self_bias_t(r, i, start, count)
            attend_back(r, r.q, r.k, r.v, r.da, r.lse, r.delta, i, start, count, pairs, BACK_UNROLL)
            hook("self_back%d%d" % (half, i))
        loop(4, lambda i: finish_heads(r, i, 0, pairs))

        def chunk(cols):
            return r.g[:, pl.ds(pl.multiple_of(cols.start * 2 + half * 256, 256), 256)]

        weight_grad(r, chunk, 3, emit(0, 3 * half))
        hook("grads0%d" % half)
    loop(4, lambda i: after_self_back(r, i))


SCRATCH = [
    ("trow", (8, 1024), F32), ("srow", (8, 1024), F32), ("cols", (1024, 128), F32),
    ("q", (4, 1024, 128), BF), ("k", (4, 1024, 128), BF), ("v", (4, 1024, 128), BF), ("a", (4, 1024, 128), BF),
    ("q2", (4, 1024, 128), BF), ("k2", (4, 1024, 128), BF), ("v2", (4, 1024, 128), BF), ("a2", (4, 1024, 128), BF),
    ("da", (4, 1024, 128), BF), ("lse", (8, 1, 1024), F32), ("lse2", (8, 1, 1024), F32), ("delta", (8, 1, 1024), F32),
    ("n1", (1024, 512), F32), ("y1", (1024, 512), BF), ("y2", (1024, 512), BF),
    ("hd", (2, 2, 4, 2, 2, 16, 2048), BF), ("du", (1024, 2048), BF), ("df", (1024, 512), BF), ("db", (1024, 512), BF),
    ("gate", (256, 2048), F32), ("dz", (1024, 512), F32), ("bias", (768, 256), F32),
    ("dq", (4, 1024, 128), F32), ("dk", (4, 1024, 128), F32), ("dv", (4, 1024, 128), F32),
    ("xt", (512, 1024), BF), ("vg", (24, 8, 512), F32),
]


def hidden_access(r):
    def put(i, cols, value):
        r.hd[i // 2, i % 2, :, :, :, :, cols] = value.reshape(4, 2, 2, 16, 512)

    def get(cols):
        return r.hd[:, :, :, :, :, :, cols].reshape(1024, 256)

    r.put_hidden, r.get_hidden = put, get


def plain_kernel(
    tlen, slen, tokens, memory, out_grad, w, vecs, layer_out, input_grad, memory_grad, mat_grad, vec_grad, stage, sem, *scratch
):
    r = Bag()
    r.tlen, r.slen, r.tokens, r.memory, r.vecs = tlen, slen, tokens, memory, vecs
    for (name, _, _), ref in zip(SCRATCH, scratch):
        setattr(r, name, ref)
    r.g = r.du
    r.w = lambda m, a, b: w[m, :, a:b]
    hidden_access(r)
    r.get_out_grad = lambda i: out_grad[rows_of(i), :]

    def put_to(ref):
        def put(i, value):
            ref[rows_of(i), :] = value

        return put

    r.put_layer_out, r.put_memory_grad, r.put_input_grad = put_to(layer_out), put_to(memory_grad), put_to(input_grad)

    def emit(m, first):
        def one(c, value):
            stage[...] = value
            at = first + c
            if m == 0 and first < 6:
                at = c * 2 + first // 3
            cols = pl.ds(pl.multiple_of(at * 256, 256), 256)
            copy = pltpu.make_async_copy(stage, mat_grad.at[m, :, cols], sem)
            copy.start()
            copy.wait()

        return one

    run(r, emit)
    vec_grad[...] = jnp.sum(r.vg[...], axis=1)


def plain(tlen, slen, tokens, memory, out_grad, w, vecs):
    V = pl.BlockSpec(memory_space=pltpu.VMEM)
    S = pl.BlockSpec(memory_space=pltpu.SMEM)
    return pl.pallas_call(
        plain_kernel,
        out_shape=(
            jax.ShapeDtypeStruct((1024, 512), BF),
            jax.ShapeDtypeStruct((1024, 512), F32),
            jax.ShapeDtypeStruct((1024, 512), F32),
            jax.ShapeDtypeStruct((4, 512, 2048), F32),
            jax.ShapeDtypeStruct((VROWS, 512), F32),
        ),
        in_specs=[S, S, V, V, V, V, V],
        out_specs=(V, V, V, pl.BlockSpec(memory_space=pl.ANY), V),
        scratch_shapes=[pltpu.VMEM((512, 256), F32), pltpu.SemaphoreType.DMA] + [pltpu.VMEM(s, d) for _, s, d in SCRATCH],
        compiler_params=pltpu.CompilerParams(vmem_limit_bytes=63400000),
        name="layer",
    )(tlen, slen, tokens, memory, out_grad, w, vecs)


class Place:
    def __init__(self):
        dp, sh = lax.axis_index("dp"), lax.axis_index("shard")
        self.z, self.y, self.x, self.c = dp // 2, dp % 2, sh // 2, sh % 2
        z, y, x, c = self.z, self.y, self.x, self.c
        self.y1, self.x1 = y + c * (1 - 2 * y), x + (1 - c) * (1 - 2 * x)
        self.y2, self.x2 = y + (1 - c) * (1 - 2 * y), x + c * (1 - 2 * x)
        self.y3, self.x3 = 1 - y, 1 - x
        self.i1, self.i2 = x * (1 - c) + y * c, y * (1 - c) + x * c
        self.first = (z * 2 + self.y1, self.x1 * 2 + c)
        self.second = (z * 2 + self.y2, self.x2 * 2 + c)
        self.twin = (z * 2 + y, x * 2 + 1 - c)

    def along_z(self, d):
        return (lax.rem(self.z + d, 4) * 2 + self.y, self.x * 2 + self.c)

    def in_plane(self, n):
        flat = lax.rem(self.y * 4 + self.x * 2 + self.c + n, 8)
        return (self.z * 2 + flat // 4, flat % 4)


class Gather:
    def __init__(self, at, ref, cols, index, send, recv):
        self.at, self.ref, self.cols, self.index, self.send, self.recv = at, ref, cols, index, send, recv

    def copy(self, slot, arriving=False):
        p, c = self.at, self.at.c
        if slot < 3:
            d = slot + 1
            z = lax.rem(p.z + 4 - d, 4) if arriving else p.z
            what, device = self.ref.at[z, p.y, p.x, c, :, self.cols], p.along_z(d)
        else:
            own, second, first, far = (p.y, p.x), (p.y2, p.x2), (p.y1, p.x1), (p.y3, p.x3)
            sent, got, device = {
                3: (own, second, p.second),
                4: (own, first, p.first),
                5: (own, own, p.twin),
                6: (second, far, p.first),
                7: (second, first, p.twin),
                8: (first, second, p.twin),
                9: (far, far, p.twin),
            }[slot]
            y, x = got if arriving else sent
            if arriving and slot not in (3, 4, 6):
                c = 1 - c
            what = self.ref.at[:, y, x, c, :, self.cols]
        return pltpu.make_async_remote_copy(
            src_ref=what,
            dst_ref=what,
            send_sem=self.send.at[self.index, slot],
            recv_sem=self.recv.at[self.index, slot],
            device_id=device,
            device_id_type=MESH,
        )

    def go(self, *slots):
        for slot in slots:
            self.copy(slot).start()

    def await_slots(self, *slots):
        for slot in slots:
            self.copy(slot, True).wait_recv()

    def step0(self):
        self.go(0, 1, 2)

    def step1(self):
        self.await_slots(0, 1, 2)
        self.go(3, 4, 5)

    def step2(self):
        self.await_slots(3)
        self.go(6, 7)

    def step3(self):
        self.await_slots(4)
        self.go(8)
        self.await_slots(6)
        self.go(9)

    def step4(self):
        self.await_slots(5, 7, 8, 9)

    def finish(self):
        for slot in range(10):
            self.copy(slot).wait_send()


class Reduce:
    def __init__(self, at, keep, give, recvs, own, cols, places, index, send, recv):
        self.at, self.keep, self.give, self.recvs, self.own, self.cols = at, keep, give, recvs, own, cols
        self.places = places
        self.index, self.send, self.recv = index, send, recv

    def copy(self, slot):
        p, cols = self.at, self.cols
        if slot == 0:
            what, where, device = self.give.at[:, :, :, :, cols], self.recvs[0].at[:, :, :, :, cols], p.twin
        elif slot == 1:
            what, where, device = self.keep.at[:, :, 1 - p.i1, :, cols], self.recvs[1].at[:, :, :, cols], p.first
        elif slot == 2:
            what, where, device = self.keep.at[:, 1 - p.i2, p.i1, :, cols], self.recvs[2].at[:, :, cols], p.second
        else:
            d = slot - 2
            what = self.keep.at[lax.rem(p.z + d, 4), p.i2, p.i1, :, cols]
            where, device = self.recvs[3].at[d - 1, :, cols], p.along_z(d)
        return pltpu.make_async_remote_copy(
            src_ref=what,
            dst_ref=where,
            send_sem=self.send.at[self.index, slot],
            recv_sem=self.recv.at[self.index, slot],
            device_id=device,
            device_id_type=MESH,
        )

    def step0(self):
        self.copy(0).start()

    def step1(self):
        cols = self.cols
        self.copy(0).wait_recv()

        def add(z):
            self.keep[z, :, :, :, cols] = self.keep[z, :, :, :, cols] + self.recvs[0][z, :, :, :, cols]

        loop(4, add)
        self.copy(1).start()

    def step2(self):
        p, cols = self.at, self.cols
        self.copy(1).wait_recv()
        self.keep[:, :, p.i1, :, cols] = self.keep[:, :, p.i1, :, cols] + self.recvs[1][:, :, :, cols]
        self.copy(2).start()

    def step3(self):
        p, cols = self.at, self.cols
        self.copy(2).wait_recv()
        self.keep[:, p.i2, p.i1, :, cols] = self.keep[:, p.i2, p.i1, :, cols] + self.recvs[2][:, :, cols]
        for slot in range(3, 6):
            self.copy(slot).start()

    def step4(self):
        p, cols = self.at, self.cols
        total = self.keep[p.z, p.i2, p.i1, :, cols].astype(F32)
        for slot in range(3, 6):
            self.copy(slot).wait_recv()
            total = total + self.recvs[3][slot - 3, :, cols].astype(F32)
        for source, target, width in self.places:
            self.own[:, target : target + width] = total[:, source : source + width]

    def finish(self):
        for slot in range(6):
            self.copy(slot).wait_send()


def steps_of(jobs, names=("step1", "step2", "step3", "step4")):
    ticks = []
    for t in range(len(jobs) + len(names) - 1):
        tick = []
        for s in range(len(names)):
            k = t - s
            if 0 <= k < len(jobs):
                tick.append(getattr(jobs[k], names[s]))
        ticks.append(tick)
    return ticks


FUSED_SCRATCH = [
    ("g0", (4, 2, 2, 2, 16, 2176), BF),
    ("g1", (4, 2, 2, 2, 16, 2048), BF),
    ("g2", (4, 2, 2, 2, 16, 2048), BF),
    ("g3", (4, 2, 2, 2, 16, 2048), BF),
    ("vecs", (VROWS, 512), F32),
    ("ra", (4, 4, 2, 2, 16, 2048), BF),
    ("rb", (4, 4, 2, 16, 2048), BF),
    ("rc", (4, 4, 16, 2048), BF),
    ("rd", (4, 3, 16, 2048), BF),
    ("vkeep", (4, 2, 2, 16, 128), BF),
    ("vgive", (4, 2, 2, 16, 128), BF),
    ("va", (4, 2, 2, 16, 128), BF),
    ("vb", (4, 2, 16, 128), BF),
    ("vc", (4, 16, 128), BF),
    ("vd", (3, 16, 128), BF),
    ("nsend", (2, 8, 128), F32),
    ("nrecv", (10, 8, 128), F32),
]
N_GATHER = 12
N_REDUCE = 8


def adam_parts(params, grad_in, first, second, factor):
    clipped = factor * grad_in
    first_m = BETA_ONE * first + (1.0 - BETA_ONE) * clipped
    second_m = BETA_TWO * second + (1.0 - BETA_TWO) * clipped * clipped
    stepped = first_m / CORRECT_ONE / (jnp.sqrt(second_m / CORRECT_TWO) + ADAM_EPS)
    return (-LEARN_RATE * (stepped + WEIGHT_DECAY * params), first_m, second_m)


def fused_kernel(
    tlen, slen, tokens, memory, out_grad, weights, vectors, layer_out, input_grad, memory_grad, own, vown, norm_out, *scratch
):
    r = Bag()
    names = [n for n, _, _ in SCRATCH] + [n for n, _, _ in FUSED_SCRATCH]
    for name, ref in zip(names, scratch):
        setattr(r, name, ref)
    g_send, g_recv, s_send, s_recv, n_send, n_recv, l_sem = scratch[len(names) :]
    p = Place()
    r.tlen, r.slen, r.tokens, r.memory, r.own, r.vown = tlen, slen, tokens, memory, own, vown
    r.g = r.du
    hidden_access(r)
    mats = [r.g0, r.g1, r.g2, r.g3]

    def w(m, a, b):
        shift = 128 if m == 0 else 0
        return mats[m][:, :, :, :, :, a + shift : b + shift].reshape(512, b - a)

    r.w = w

    barrier = pltpu.get_barrier_semaphore()
    for d in range(1, 4):
        pl.semaphore_signal(barrier, inc=1, device_id=p.along_z(d), device_id_type=MESH)
    for n in range(1, 8):
        pl.semaphore_signal(barrier, inc=1, device_id=p.in_plane(n), device_id_type=MESH)
    grad_in = pltpu.make_async_copy(out_grad, r.db, l_sem.at[0])
    grad_in.start()
    r.g0[p.z, p.y, p.x, p.c, :, 0:128] = jnp.concatenate(
        [vectors[...], jnp.zeros((16, 128 - vectors.shape[1]), F32)], axis=1
    ).astype(BF)
    for m in range(4):
        shift = 128 if m == 0 else 0
        mats[m][p.z, p.y, p.x, p.c, :, shift : shift + 2048] = weights[16 * m : 16 * m + 16, :].astype(BF)
    pl.semaphore_wait(barrier, 10)

    gathers = []
    for m, cuts in ((0, (0, 640, 1152, 1664, 2176)), (1, (0, 512, 1024, 1536, 2048)), (2, (0, 1024, 2048)), (3, (0, 1024, 2048))):
        for a, b in zip(cuts[:-1], cuts[1:]):
            gathers.append(Gather(p, mats[m], slice(a, b), len(gathers), g_send, g_recv))
    for g in gathers:
        g.step0()
    ticks = steps_of(gathers)

    def run_tick(t):
        for action in ticks[t]:
            action()

    keeps = {0: r.hd.at[1, 0], 1: r.hd.at[0, 0], 2: r.g2.at[:, :, :, 0], 3: r.g3.at[:, :, :, 0]}
    gives = {0: r.hd.at[1, 1], 1: r.hd.at[0, 1], 2: r.g2.at[:, :, :, 1], 3: r.g3.at[:, :, :, 1]}

    def spread(value, keep, give, cols):
        v = value.reshape(4, 2, 2, 2, 16, value.shape[-1])
        flag = p.c == 0
        for y in range(2):
            for x in range(2):
                i1, i2 = x * (1 - p.c) + y * p.c, y * (1 - p.c) + x * p.c
                even, odd = v[:, y, x, 0], v[:, y, x, 1]
                keep[:, i2, i1, :, cols] = jnp.where(flag, even, odd).astype(BF)
                give[:, i1, i2, :, cols] = jnp.where(flag, odd, even).astype(BF)

    def emit(m, first):
        def one(c, value):
            spread(value, keeps[m], gives[m], pl.ds(pl.multiple_of((first + c) * 256, 256), 256))

        return one

    def job(k, m, a, b, places=None):
        return Reduce(
            p, keeps[m], gives[m], (r.ra.at[m], r.rb.at[m], r.rc.at[m], r.rd.at[m]), r.own.at[16 * m : 16 * m + 16, :],
            slice(a, b), places or ((0, a, b - a),), k, s_send, s_recv,
        )

    halves = [tuple((256 * part, 512 * part + 256 * h, 256) for part in range(3)) for h in range(2)]
    j3, j2, j1o, j1 = job(0, 3, 0, 2048), job(1, 2, 0, 2048), job(2, 1, 1536, 2048), job(3, 1, 0, 1536)
    j0o, j0a, j0b = job(4, 0, 1536, 2048), job(5, 0, 0, 768, halves[0]), job(6, 0, 768, 1536, halves[1])
    jv = Reduce(
        p, r.vkeep, r.vgive, (r.va, r.vb, r.vc, r.vd), r.vown, slice(0, 128), ((0, 0, 128),), 7, s_send, s_recv
    )
    jobs = [j3, j2, j1o, j1, j0o, j0a, j0b, jv]

    def start():
        for t in range(4):
            run_tick(t)
        for b in range(4):
            block = r.g0[b, :, :, :, :, 0:128].reshape(128, 128).astype(F32)
            r.vecs[:, b * 128 : (b + 1) * 128] = block.T[0:VROWS, :]
        run_tick(4)
        run_tick(5)

    def middle_done():
        for g in gathers:
            g.finish()
        for k in range(4):
            layer_part(k).wait()

    hooks = {
        "start": [start],
        "projected": ticks[6],
        "self0": ticks[7],
        "self1": ticks[8],
        "self2": ticks[9],
        "self3": ticks[10],
        "crossed": [grad_in.wait],
        "middle": [middle_done],
        "grads3": [j3.step0],
        "grads2": [j2.step0, j3.step1],
        "grads1o": [j1o.step0],
        "grads1": [j1.step0, j2.step4, j1o.step3],
        "grads0o": [j0o.step0, j1.step1, j1o.step4],
        "self_back00": [j0o.step1],
        "self_back03": [j1.step2, j0o.step2],
        "grads00": [j0a.step0],
        "self_back11": [j1.step3, j0o.step3, j0a.step1],
        "self_back13": [j1.step4, j0o.step4, j0a.step2],
        "grads01": [j0b.step0, j0a.step3],
    }
    plan = {
        "cross": {0: ticks[11], 1: ticks[12], 2: ticks[13], 3: ticks[14]},
        "cross_back": {
            0: [j2.step1],
            1: [j3.step2],
            3: [j3.step3],
            4: [j2.step2, j1o.step1],
            6: [j3.step4, j2.step3, j1o.step2],
        },
    }

    def hook(name):
        for action in hooks.get(name, ()):
            action()

    def at_step(name, t):
        for when, actions in plan.get(name, {}).items():

            @pl.when(t == when)
            def _():
                for action in actions:
                    action()

    r.get_out_grad = lambda i: r.db[rows_of(i), :]

    def on_tile(i, put, copy):
        for k in range(4):

            @pl.when(i == k)
            def _():
                put(k)
                copy(k).start()

    def layer_piece(k):
        return r.xt.at[(k // 2) * 256 : (k // 2) * 256 + 256, (k % 2) * 512 : (k % 2) * 512 + 512]

    def layer_part(k):
        return pltpu.make_async_copy(layer_piece(k), layer_out.at[k * 256 : k * 256 + 256, :], l_sem.at[2 + k])

    def put_layer_out(i, value):
        def put(k):
            layer_piece(k)[...] = value

        on_tile(i, put, layer_part)

    def memory_part(k):
        return pltpu.make_async_copy(
            r.gate.at[:, k * 512 : k * 512 + 512], memory_grad.at[k * 256 : k * 256 + 256, :], l_sem.at[6 + k]
        )

    def put_memory_grad(i, value):
        def put(k):
            r.gate[:, k * 512 : k * 512 + 512] = value

        on_tile(i, put, memory_part)

    def input_part(k):
        rows = slice(k * 256, k * 256 + 256)
        return pltpu.make_async_copy(r.dz.at[rows, :], input_grad.at[rows, :], l_sem.at[10 + k])

    def put_input_grad(i, value):
        def put(k):
            r.dz[k * 256 : k * 256 + 256, :] = value

        on_tile(i, put, input_part)

    r.put_layer_out, r.put_memory_grad, r.put_input_grad = put_layer_out, put_memory_grad, put_input_grad

    run(r, emit, hook, at_step)

    sums = jnp.sum(r.vg[...], axis=1)
    sums = jnp.concatenate([sums, jnp.zeros((128 - VROWS, 512), F32)], axis=0)
    spread(
        jnp.concatenate([sums[:, b * 128 : (b + 1) * 128].T for b in range(4)], axis=0),
        r.vkeep, r.vgive, slice(0, 128),
    )
    jv.step0()
    j0b.step1()
    jv.step1()
    j0a.step4()
    for name in ("step2", "step3", "step4"):
        getattr(j0b, name)()
        getattr(jv, name)()

    r.nsend[0] = jnp.broadcast_to(jnp.sum(r.vown[...] * r.vown[...]), (8, 128))

    def square(i):
        part = r.own[pl.ds(pl.multiple_of(i * 8, 8), 8), :]
        r.nsend[0] += jnp.broadcast_to(jnp.sum(part * part), (8, 128))

    loop(8, square)

    def plane_part(n):
        return pltpu.make_async_remote_copy(
            src_ref=r.nsend.at[0], dst_ref=r.nrecv.at[n - 1], send_sem=n_send.at[n - 1], recv_sem=n_recv.at[n - 1],
            device_id=p.in_plane(n), device_id_type=MESH,
        )

    def z_part(d):
        return pltpu.make_async_remote_copy(
            src_ref=r.nsend.at[1], dst_ref=r.nrecv.at[6 + d], send_sem=n_send.at[6 + d], recv_sem=n_recv.at[6 + d],
            device_id=p.along_z(d), device_id_type=MESH,
        )

    for n in range(1, 8):
        plane_part(n).start()
    total = r.nsend[0]
    for n in range(1, 8):
        plane_part(n).wait_recv()
        total = total + r.nrecv[n - 1]
    r.nsend[1] = total
    for d in range(1, 4):
        z_part(d).start()
    for k in range(4):
        memory_part(k).wait()
        input_part(k).wait()
    for j in jobs:
        j.finish()
    for n in range(1, 8):
        plane_part(n).wait_send()
    for d in range(1, 4):
        z_part(d).wait_recv()
        total = total + r.nrecv[6 + d]
    norm_out[...] = jnp.sqrt(total)
    for d in range(1, 4):
        z_part(d).wait_send()


def finish_kernel(
    layer_in, input_in, memory_in, own, vown, norm, norm_scalar, weights, vectors, moments, vector_moments,
    layer_out, input_grad, memory_grad, norm_out, mat_out, vec_out, step_out, vstep_out, first_out, second_out, vfirst_out,
    vsecond_out, low_room, big_room, sems, out_sems,
):
    arrivals, departures = [], []
    for source, target, room, pieces in (
        (layer_in, layer_out, low_room, 2),
        (memory_in, memory_grad, big_room.at[0], 4),
        (input_in, input_grad, big_room.at[1], 4),
    ):
        size = source.shape[0] // pieces
        for k in range(pieces):
            rows, n = slice(k * size, k * size + size), len(arrivals)
            arrivals.append(pltpu.make_async_copy(source.at[rows, :], room.at[rows, :], sems.at[n]))
            departures.append(pltpu.make_async_copy(room.at[rows, :], target.at[rows, :], out_sems.at[n]))
            arrivals[-1].start()
    norm_out[0, 0] = norm_scalar[0, 0]
    factor = jnp.minimum(1.0, CLIP_NORM / (norm[0:1, 0:1] + 1e-06))
    count = vectors.shape[1]
    vgrad = vown[:, 0:count]
    vec_out[...] = vgrad
    vstep_out[...], vfirst_out[...], vsecond_out[...] = adam_parts(
        vectors[...], vgrad, vector_moments[0], vector_moments[1], factor
    )

    def update(i):
        rows = pl.ds(pl.multiple_of(i * 16, 16), 16)
        later = pl.ds(pl.multiple_of(i * 16 + 64, 16), 16)
        grad = own[rows, :]
        mat_out[rows, :] = grad
        step_out[rows, :], first_out[rows, :], second_out[rows, :] = adam_parts(
            weights[rows, :], grad, moments[rows, :], moments[later, :], factor
        )

    for arrival, departure in zip(arrivals, departures):
        arrival.wait()
        departure.start()
    loop(4, update)
    for departure in departures:
        departure.wait()


def fused_body(tokens, memory, target_lengths, source_lengths, out_grad, weights, vectors, weight_moments, vector_moments):
    V = pl.BlockSpec(memory_space=pltpu.VMEM)
    S = pl.BlockSpec(memory_space=pltpu.SMEM)
    A = pl.BlockSpec(memory_space=pl.ANY)
    mat = jax.ShapeDtypeStruct((64, 2048), F32)
    vec_shape = jax.ShapeDtypeStruct(vectors.shape[::-1], F32)
    low = jax.ShapeDtypeStruct(tokens.shape, BF)
    big = jax.ShapeDtypeStruct(tokens.shape, F32)
    flat_weights, flat_vectors = weights.reshape(64, 2048), vectors.T
    layer_out, input_grad, memory_grad, own, vown, norm = pl.pallas_call(
        fused_kernel,
        out_shape=(low, big, big, mat, jax.ShapeDtypeStruct((16, 128), F32), jax.ShapeDtypeStruct((8, 128), F32)),
        in_specs=[S, S, V, V, A, V, V],
        out_specs=(A, A, A, V, V, V),
        scratch_shapes=[pltpu.VMEM(s, d) for _, s, d in SCRATCH + FUSED_SCRATCH]
        + [
            pltpu.SemaphoreType.DMA((N_GATHER, 10)),
            pltpu.SemaphoreType.DMA((N_GATHER, 10)),
            pltpu.SemaphoreType.DMA((N_REDUCE, 6)),
            pltpu.SemaphoreType.DMA((N_REDUCE, 6)),
            pltpu.SemaphoreType.DMA((10,)),
            pltpu.SemaphoreType.DMA((10,)),
            pltpu.SemaphoreType.DMA((14,)),
        ],
        compiler_params=pltpu.CompilerParams(vmem_limit_bytes=63400000, collective_id=0, has_side_effects=True),
        name="layer",
    )(target_lengths, source_lengths, tokens, memory, out_grad, flat_weights, flat_vectors)
    layer_out, input_grad, memory_grad, norm, g, vg, st, vst, m1, m2, vm1, vm2 = pl.pallas_call(
        finish_kernel,
        out_shape=(
            low, big, big, jax.ShapeDtypeStruct((1, 1), F32), mat, vec_shape, mat, vec_shape, mat, mat, vec_shape, vec_shape,
        ),
        in_specs=[A, A, A, V, V, V, S, V, V, V, V],
        out_specs=(A, A, A, S, V, V, V, V, V, V, V, V),
        scratch_shapes=[
            pltpu.VMEM(tokens.shape, BF),
            pltpu.VMEM((2,) + tokens.shape, F32),
            pltpu.SemaphoreType.DMA((10,)),
            pltpu.SemaphoreType.DMA((10,)),
        ],
        compiler_params=pltpu.CompilerParams(vmem_limit_bytes=63400000),
        name="finish",
    )(
        layer_out, input_grad, memory_grad, own, vown, norm, norm, flat_weights, flat_vectors,
        weight_moments.reshape(128, 2048), vector_moments.transpose(0, 2, 1),
    )
    back = lambda a: a.reshape(weights.shape)
    return (
        layer_out, input_grad, memory_grad, norm[0, 0], back(g), vg.T, back(st), vst.T, back(m1), back(m2), vm1.T, vm2.T,
    )


def adam_update(params, grad_in, moments, factor):
    clipped = factor * grad_in
    first_m = BETA_ONE * moments[0] + (1.0 - BETA_ONE) * clipped
    second_m = BETA_TWO * moments[1] + (1.0 - BETA_TWO) * clipped * clipped
    stepped = first_m / CORRECT_ONE / (jnp.sqrt(second_m / CORRECT_TWO) + ADAM_EPS)
    return (-LEARN_RATE * (stepped + WEIGHT_DECAY * params), first_m, second_m)


def generic_body(tokens, memory, target_lengths, source_lengths, out_grad, weights, vectors, weight_moments, vector_moments):
    axes = ("dp", "shard")
    w = lax.all_gather(weights.astype(BF), axes, axis=1, tiled=True)
    vecs = lax.all_gather(vectors.astype(BF), axes, axis=1, tiled=True).astype(F32)
    vecs = jnp.concatenate([vecs, jnp.zeros((VROWS - vecs.shape[0], vecs.shape[1]), F32)], axis=0)
    layer_out, input_grad, memory_grad, mat_grad, vec_grad = plain(
        target_lengths, source_lengths, tokens, memory, out_grad, w, vecs
    )
    mat_share = lax.psum_scatter(mat_grad, axes, scatter_dimension=1, tiled=True)
    vec_share = lax.psum_scatter(vec_grad[: vectors.shape[0]], axes, scatter_dimension=1, tiled=True)
    squares = jnp.sum(mat_share * mat_share) + jnp.sum(vec_share * vec_share)
    grad_norm = jnp.sqrt(lax.psum(squares, axes))
    factor = jnp.minimum(1.0, CLIP_NORM / (grad_norm + 1e-06))
    weight_steps, weight_first, weight_second = adam_update(weights, mat_share, weight_moments, factor)
    vector_steps, vector_first, vector_second = adam_update(vectors, vec_share, vector_moments, factor)
    return (
        layer_out, input_grad, memory_grad, grad_norm, mat_share, vec_share,
        weight_steps, vector_steps, weight_first, weight_second, vector_first, vector_second,
    )


def solution(mesh):
    both = ("dp", "shard")
    rows, mats, vecs = P(both, None), P(None, both, None), P(None, both)
    fits = (mesh.shape["dp"], mesh.shape["shard"]) == (8, 4)
    return jax.shard_map(
        fused_body if fits else generic_body,
        mesh=mesh,
        in_specs=(rows, rows, rows, rows, rows, mats, vecs, P(None, None, both, None), P(None, None, both)),
        out_specs=(rows, rows, rows, P(), mats, vecs, mats, vecs, mats, mats, vecs, vecs),
        check_vma=False,
    )
```

```python
import functools
import jax
import jax.numpy as jnp
from jax import lax
from jax.experimental import pallas as pl
from jax.experimental.pallas import tpu as pltpu
from jax.sharding import PartitionSpec as P

HD = 64
EPSILON = 1e-05
MASKED = -1e30
BF = jnp.bfloat16
F32 = jnp.float32
TILE = 256
VROWS = 24
FWD_UNROLL = 4
GRAD_UNROLL = 2
BACK_UNROLL = 2
CROSS_KEYS = 512
MESH = pl.DeviceIdType.MESH
CLIP_NORM = 1.0
LEARN_RATE = 0.001
BETA_ONE = 0.9
BETA_TWO = 0.999
ADAM_EPS = 1e-08
WEIGHT_DECAY = 0.1
CORRECT_ONE = 1.0 - 0.9**3
CORRECT_TWO = 1.0 - 0.999**3


def mm(left, right):
    return jnp.dot(left, right, preferred_element_type=F32)


def mm_t(left, right):
    return lax.dot_general(left, right, (((1,), (1,)), ((), ())), preferred_element_type=F32)


def t_mm(left, right):
    return lax.dot_general(left, right, (((0,), (0,)), ((), ())), preferred_element_type=F32)


def rows_of(i, size=TILE):
    return pl.ds(pl.multiple_of(i * size, size), size)


def normed(z):
    centred = z - jnp.mean(z, axis=-1, keepdims=True)
    inverse = lax.rsqrt(jnp.mean(centred * centred, axis=-1, keepdims=True) + EPSILON)
    return centred * inverse, inverse


def norm_back(grad, n, inverse, gain):
    scaled = grad * gain
    return inverse * (
        scaled
        - jnp.mean(scaled, axis=-1, keepdims=True)
        - n * jnp.mean(scaled * n, axis=-1, keepdims=True)
    )


def fold(values):
    r, c = values.shape
    return jnp.sum(values.astype(F32).reshape(r // 8, 8, c), axis=0)


def heads_join(ref, rows):
    return jnp.concatenate([ref[p, rows, :] for p in range(4)], axis=1)


def heads_split(ref, rows, value):
    for p in range(4):
        ref[p, rows, :] = value[:, p * 128 : (p + 1) * 128]


class Bag:
    pass


def head_mask(h, dtype):
    lane = lax.broadcasted_iota(jnp.int32, (1, 128), 1)
    return jnp.where((lane < HD) if h == 0 else (lane >= HD), 1.0, 0.0).astype(dtype)


def segments(r, lengths, row_ref, lane):
    ends = []
    total = jnp.int32(0)
    for s in range(16):
        total = total + lengths[0, s]
        ends.append(total)

    def number(at):
        seg = jnp.zeros(at.shape, F32)
        for e in ends:
            seg = seg + jnp.where(e <= at, 1.0, 0.0)
        return seg

    row_ref[...] = number(lax.broadcasted_iota(jnp.int32, (8, 1024), 1))

    def col(i):
        r.cols[rows_of(i), lane : lane + 1] = number(lax.broadcasted_iota(jnp.int32, (TILE, 128), 0) + i * TILE)[:, 0:1]

    loop(4, col)


def attend(r, q_ref, k_ref, v_ref, out_ref, lse_ref, tile, key_start, key_count, bias):
    rows = rows_of(tile)
    keys = pl.ds(key_start, key_count)
    lane = lax.broadcasted_iota(jnp.int32, (TILE, 128), 1)

    def pair(p, _):
        q = q_ref[p, rows, :]
        k = k_ref[p, keys, :]
        v = v_ref[p, keys, :]
        tops, weights, values = [], [], []
        for h in range(2):
            m = head_mask(h, BF)
            s = mm_t(q * m, k) + bias[:, :key_count]
            tops.append(jnp.max(s, axis=-1, keepdims=True))
            weights.append(jnp.exp(s - tops[h]).astype(BF))
            values.append(jnp.concatenate([v * m, jnp.broadcast_to(m, (key_count, 128))], axis=1))
        both = mm(jnp.concatenate(weights, axis=1), jnp.concatenate(values, axis=0))
        total = both[:, 128:256]
        out_ref[p, rows, :] = (both[:, 0:128] * (1.0 / total)).astype(BF)
        lse = (jnp.where(lane < HD, tops[0], tops[1]) + jnp.log(total)).T
        lse_ref[2 * p, :, rows] = lse[0:1, :]
        lse_ref[2 * p + 1, :, rows] = lse[HD : HD + 1, :]
        return 0

    lax.fori_loop(0, 4, pair, 0, unroll=FWD_UNROLL)


def deltas(r, out_ref, grad_ref, delta_ref, tile):
    rows = rows_of(tile)
    lane = lax.broadcasted_iota(jnp.int32, (TILE, 128), 1)
    table = jnp.zeros((TILE, 128), F32)
    for p in range(4):
        prod = out_ref[p, rows, :].astype(F32) * grad_ref[p, rows, :].astype(F32)
        for h in range(2):
            one = jnp.sum(prod * head_mask(h, F32), axis=-1, keepdims=True)
            table = jnp.where(lane == 2 * p + h, one, table)
    flipped = table.T
    for h in range(8):
        delta_ref[h, :, rows] = flipped[h : h + 1, :]


def attend_back(r, q_ref, k_ref, v_ref, grad_ref, lse_ref, delta_ref, i, key_start, key_count, pairs, unroll):
    qr, kr = rows_of(i), pl.ds(key_start, key_count)
    lane = lax.broadcasted_iota(jnp.int32, (TILE, 128), 1)
    key_lane = lax.broadcasted_iota(jnp.int32, (key_count, 128), 1)

    def pair(p, _):
        q, k, v, g = q_ref[p, qr, :], k_ref[p, kr, :], v_ref[p, kr, :], grad_ref[p, qr, :]
        dv, dk, dq = [], [], []
        for h in range(2):
            m = head_mask(h, BF)
            s = mm_t(k * m, q) + r.bias[0:key_count, :]
            w = jnp.exp(s - lse_ref[2 * p + h, :, qr])
            dp = mm_t(v * m, g)
            ds = (w * (dp - delta_ref[2 * p + h, :, qr])).astype(BF)
            dv.append(mm(w.astype(BF), g))
            dk.append(mm(ds, q))
            dq.append(t_mm(ds, k))
        r.dv[p, kr, :] += jnp.where(key_lane < HD, dv[0], dv[1])
        r.dk[p, kr, :] += jnp.where(key_lane < HD, dk[0], dk[1])
        r.dq[p, qr, :] += jnp.where(lane < HD, dq[0], dq[1])
        return 0

    lax.fori_loop(pairs[0], pairs[1], pair, 0, unroll=unroll)


def zero_grads(r):
    def step(i, _):
        z = jnp.zeros((4, TILE, 128), F32)
        r.dq[:, rows_of(i), :] = z
        r.dk[:, rows_of(i), :] = z
        r.dv[:, rows_of(i), :] = z
        return 0

    lax.fori_loop(0, 4, step, 0)


def vec(r, row):
    return r.vecs[row : row + 1, :]


def add_vec(r, row, value):
    r.vg[row] += value


def project_self(r, i, part):
    rows = rows_of(i)
    value = mm(r.tokens[rows, :], r.w(0, 512 * part, 512 * part + 512))
    if part == 0:
        heads_split(r.q, rows, ((value + vec(r, 0)).astype(BF) * 0.125).astype(BF))
    elif part == 1:
        heads_split(r.k, rows, value.astype(BF))
    else:
        heads_split(r.v, rows, (value + vec(r, 1)).astype(BF))


def self_bias(r, i, start, count):
    qs = r.cols[rows_of(i), 0:1]
    ks = r.trow[0:1, start : start + count]
    at = lax.broadcasted_iota(jnp.int32, (TILE, count), 0) + i * TILE
    key = lax.broadcasted_iota(jnp.int32, (TILE, count), 1) + start
    r.gate[:, 0:count] = jnp.where((qs == ks) & (key <= at), 0.0, MASKED)


def after_self(r, i):
    rows = rows_of(i)
    a = heads_join(r.a, rows)
    z = r.tokens[rows, :].astype(F32) + (mm(a, r.w(0, 1536, 2048)) + vec(r, 2))
    n, inverse = normed(z)
    r.n1[rows, :] = n
    r.cols[rows, 2:3] = inverse
    y = (n * vec(r, 3) + vec(r, 4)).astype(BF)
    r.y1[rows, :] = y
    heads_split(r.q2, rows, ((mm(y, r.w(1, 0, 512)) + vec(r, 5)).astype(BF) * 0.125).astype(BF))


def project_cross(r, i):
    rows = rows_of(i)
    m = r.memory[rows, :]
    heads_split(r.k2, rows, mm(m, r.w(1, 512, 1024)).astype(BF))
    heads_split(r.v2, rows, (mm(m, r.w(1, 1024, 1536)) + vec(r, 6)).astype(BF))


def cross_bias(r, i):
    qs = r.cols[rows_of(i), 0:1]
    ks = r.srow[0:1, :]
    r.gate[:, 0:1024] = jnp.where(qs == ks, 0.0, MASKED)


def middle(r, half, k, room):
    i = 2 * half + k
    rows = rows_of(i)
    y1 = r.n1[rows, :] * vec(r, 3) + vec(r, 4)
    z2 = y1 + (mm(heads_join(r.a2, rows), r.w(1, 1536, 2048)) + vec(r, 7))
    n2, r2 = normed(z2)
    y2 = n2 * vec(r, 8) + vec(r, 9)
    y2l = y2.astype(BF)
    r.y2[rows, :] = y2l
    f = jnp.zeros((TILE, 512), F32)
    for c in range(4):
        cols = slice(c * 512, (c + 1) * 512)
        u = mm(y2l, r.w(2, cols.start, cols.stop)) + vec(r, 10 + c)
        s = jax.nn.sigmoid(u)
        hd = (u * s).astype(BF)
        r.put_hidden(i, cols, hd)
        heads_split(room, rows_of(c), s * (1.0 + u * (1.0 - s)))
        f = f + mm_t(hd, r.w(3, cols.start, cols.stop))
    n3, r3 = normed(y2 + (f + vec(r, 14)))
    r.put_layer_out(half, k, (n3 * vec(r, 15) + vec(r, 16)).astype(BF))
    g = r.get_out_grad(i).astype(F32)
    add_vec(r, 15, fold(g * n3))
    add_vec(r, 16, fold(g))
    dz3 = norm_back(g, n3, r3, vec(r, 15))
    df = dz3.astype(BF)
    r.df[rows, :] = df
    add_vec(r, 14, fold(df))
    dy2 = dz3
    for c in range(4):
        cols = slice(c * 512, (c + 1) * 512)
        du = (mm(df, r.w(3, cols.start, cols.stop)) * heads_join(room, rows_of(c))).astype(BF)
        r.du[rows, cols] = du
        add_vec(r, 10 + c, fold(du))
        dy2 = dy2 + mm_t(du, r.w(2, cols.start, cols.stop))
    add_vec(r, 8, fold(dy2 * n2))
    add_vec(r, 9, fold(dy2))
    dz2 = norm_back(dy2, n2, r2, vec(r, 8))
    r.dz[rows, :] = dz2
    db = dz2.astype(BF)
    r.db[rows, :] = db
    add_vec(r, 7, fold(db))
    heads_split(r.da, rows, mm_t(db, r.w(1, 1536, 2048)).astype(BF))
    deltas(r, r.a2, r.da, r.delta, i)


def finish_heads(r, i, vector_row, targets, pairs=(0, 4)):
    rows = rows_of(i)
    a, b = pairs[0] * 128, pairs[1] * 128
    for part, (ref, scale) in enumerate(((r.dq, 0.125), (r.dk, 1.0), (r.dv, 1.0))):
        value = jnp.concatenate([ref[p, rows, :] for p in range(*pairs)], axis=1)
        value = (value * scale).astype(BF)
        targets[part][rows, a:b] = value
        if part != 1:
            r.vg[vector_row + part // 2, :, a:b] += fold(value)


def after_cross_back(r, i):
    rows = rows_of(i)
    dy1 = r.dz[rows, :] + mm_t(r.g[rows, 0:512], r.w(1, 0, 512))
    n1 = r.n1[rows, :]
    add_vec(r, 3, fold(dy1 * n1))
    add_vec(r, 4, fold(dy1))
    dz1 = norm_back(dy1, n1, r.cols[rows, 2:3], vec(r, 3))
    r.dz[rows, :] = dz1
    db = dz1.astype(BF)
    r.db[rows, :] = db
    add_vec(r, 2, fold(db))
    heads_split(r.da, rows, mm_t(db, r.w(0, 1536, 2048)).astype(BF))
    deltas(r, r.a, r.da, r.delta, i)


def after_self_back(r, i):
    rows = rows_of(i)
    r.put_input_grad(
        i,
        r.dz[rows, :]
        + (
            mm_t(r.y1[rows, :], r.w(0, 0, 512))
            + mm_t(r.y2[rows, :], r.w(0, 512, 1024))
            + mm_t(r.df[rows, :], r.w(0, 1024, 1536))
        ),
    )


def memory_back(r, i):
    rows = rows_of(i)
    r.put_memory_grad(
        i, mm_t(r.g[rows, 512:1024], r.w(1, 512, 1024)) + mm_t(r.g[rows, 1024:1536], r.w(1, 1024, 1536))
    )


def cross_bias_t(r, i, key_start, key_count):
    ks = r.cols[pl.ds(key_start, key_count), 1:2]
    qs = r.trow[0:1, rows_of(i)]
    r.bias[0:key_count, :] = jnp.where(ks == qs, 0.0, MASKED)


def self_bias_t(r, i, key_start, key_count):
    ks = r.cols[pl.ds(key_start, key_count), 0:1]
    qs = r.trow[0:1, rows_of(i)]
    key = lax.broadcasted_iota(jnp.int32, (key_count, TILE), 0) + key_start
    at = lax.broadcasted_iota(jnp.int32, (key_count, TILE), 1) + i * TILE
    r.bias[0:key_count, :] = jnp.where((ks == qs) & (key <= at), 0.0, MASKED)


def loop(n, body):
    def step(i, _):
        body(i)
        return 0

    lax.fori_loop(0, n, step, 0)


def flip(r, source):
    def one(i):
        r.xt[:, rows_of(i)] = source(rows_of(i)).T

    loop(4, one)


def weight_grad(r, chunk_of, count, emit):
    def one(c, _):
        cols = pl.ds(pl.multiple_of(c * 256, 256), 256)
        emit(c, mm(r.xt[...], chunk_of(cols)))
        return 0

    lax.fori_loop(0, count, one, 0, unroll=GRAD_UNROLL)


def run(r, emit, hook=lambda name: None, at_step=lambda name, t: None):
    hook("enter")
    segments(r, r.tlen, r.trow, 0)
    segments(r, r.slen, r.srow, 1)

    def clear(i):
        r.vg[i] = jnp.zeros((8, 512), F32)

    loop(VROWS, clear)
    for part in range(3):
        hook("start%d" % part)
        loop(4, lambda i: project_self(r, i, part))
    hook("projected")
    for i in range(4):
        start = max(0, i - 2) * TILE
        count = (i + 1) * TILE - start
        self_bias(r, i, start, count)
        attend(r, r.q, r.k, r.v, r.a, r.lse, i, start, count, r.gate)
        hook("self%d" % i)
    loop(4, lambda i: project_cross(r, i))
    loop(4, lambda i: after_self(r, i))
    hook("cross_ready")

    def cross(i):
        cross_bias(r, i)
        attend(r, r.q2, r.k2, r.v2, r.a2, r.lse2, i, 0, 1024, r.gate)
        at_step("cross", i)

    loop(4, cross)
    hook("crossed")

    def two_tiles(i):
        middle(r, i, 0, r.dk)
        middle(r, i, 1, r.dv)

    loop(2, two_tiles)
    hook("middle")
    flip(r, lambda rows: r.df[rows, :])
    weight_grad(r, r.get_hidden, 8, emit(3, 0))
    hook("grads3")
    flip(r, lambda rows: r.y2[rows, :])
    weight_grad(r, lambda cols: r.du[:, cols], 8, emit(2, 0))
    hook("grads2")
    flip(r, lambda rows: heads_join(r.a2, rows))
    weight_grad(r, lambda cols: r.db[:, cols], 2, emit(1, 6))
    hook("grads1o")
    zero_grads(r)

    parts = 1024 // CROSS_KEYS

    def cross_back(t):
        i, start = t // parts, pl.multiple_of(t % parts * CROSS_KEYS, CROSS_KEYS)
        cross_bias_t(r, i, start, CROSS_KEYS)
        attend_back(r, r.q2, r.k2, r.v2, r.da, r.lse2, r.delta, i, start, CROSS_KEYS, (0, 4), BACK_UNROLL)
        at_step("cross_back", t)

    loop(4 * parts, cross_back)
    cross_g = [r.g.at[:, 512 * part : 512 * part + 512] for part in range(3)]
    loop(4, lambda i: finish_heads(r, i, 5, cross_g))
    flip(r, lambda rows: r.y1[rows, :])
    weight_grad(r, lambda cols: r.g[:, cols], 2, emit(1, 0))
    flip(r, lambda rows: r.memory[rows, :])
    weight_grad(r, lambda cols: r.g[:, pl.ds(cols.start + 512, 256)], 4, emit(1, 2))
    hook("grads1")
    loop(4, lambda i: after_cross_back(r, i))
    flip(r, lambda rows: heads_join(r.a, rows))
    weight_grad(r, lambda cols: r.db[:, cols], 2, emit(0, 6))
    hook("grads0o")
    zero_grads(r)
    flip(r, lambda rows: r.tokens[rows, :])
    for half in range(2):
        pairs = (2 * half, 2 * half + 2)
        for i in range(4):
            start = max(0, i - 2) * TILE
            count = (i + 1) * TILE - start
            self_bias_t(r, i, start, count)
            attend_back(r, r.q, r.k, r.v, r.da, r.lse, r.delta, i, start, count, pairs, BACK_UNROLL)
            hook("self_back%d%d" % (half, i))
        loop(4, lambda i: finish_heads(r, i, 0, (r.y1, r.y2, r.df), pairs))

        for part, ref in enumerate((r.y1, r.y2, r.df)):
            emit(0, 3 * half)(part, mm(r.xt[...], ref[:, half * 256 : half * 256 + 256]))
        hook("grads0%d" % half)
    loop(2, lambda i: after_self_back(r, i))
    hook("tail0")
    loop(2, lambda i: after_self_back(r, i + 2))
    hook("tail1")
    loop(4, lambda i: memory_back(r, i))


SCRATCH = [
    ("trow", (8, 1024), F32), ("srow", (8, 1024), F32), ("cols", (1024, 128), F32),
    ("q", (4, 1024, 128), BF), ("k", (4, 1024, 128), BF), ("v", (4, 1024, 128), BF), ("a", (4, 1024, 128), BF),
    ("q2", (4, 1024, 128), BF), ("k2", (4, 1024, 128), BF), ("v2", (4, 1024, 128), BF), ("a2", (4, 1024, 128), BF),
    ("da", (4, 1024, 128), BF), ("lse", (8, 1, 1024), F32), ("lse2", (8, 1, 1024), F32), ("delta", (8, 1, 1024), F32),
    ("n1", (1024, 512), F32), ("y1", (1024, 512), BF), ("y2", (1024, 512), BF),
    ("hd", (2, 2, 4, 2, 2, 16, 2048), BF), ("du", (1024, 2048), BF), ("df", (1024, 512), BF), ("db", (1024, 512), BF),
    ("gate", (256, 1024), F32), ("dz", (1024, 512), F32), ("bias", (768, 256), F32),
    ("dq", (4, 1024, 128), F32), ("dk", (4, 1024, 128), F32), ("dv", (4, 1024, 128), F32),
    ("xt", (512, 1024), BF), ("vg", (24, 8, 512), F32),
]


def hidden_access(r):
    def put(i, cols, value):
        r.hd[i // 2, i % 2, :, :, :, :, cols] = value.reshape(4, 2, 2, 16, 512)

    def get(cols):
        return r.hd[:, :, :, :, :, :, cols].reshape(1024, 256)

    r.put_hidden, r.get_hidden = put, get


def plain_kernel(
    tlen, slen, tokens, memory, out_grad, w, vecs, layer_out, input_grad, memory_grad, mat_grad, vec_grad, stage, sem, *scratch
):
    r = Bag()
    r.tlen, r.slen, r.tokens, r.memory, r.vecs = tlen, slen, tokens, memory, vecs
    for (name, _, _), ref in zip(SCRATCH, scratch):
        setattr(r, name, ref)
    r.g = r.du
    r.w = lambda m, a, b: w[m, :, a:b]
    hidden_access(r)
    r.get_out_grad = lambda i: out_grad[rows_of(i), :]

    def send(source, target):
        copy = pltpu.make_async_copy(source, target, sem)
        copy.start()
        copy.wait()

    def put_layer_out(half, k, value):
        piece = r.xt.at[rows_of(half), k * 512 : k * 512 + 512]
        piece[...] = value
        send(piece, layer_out.at[rows_of(2 * half + k), :])

    def put_memory_grad(i, value):
        r.n1[rows_of(i), :] = value
        send(r.n1.at[rows_of(i), :], memory_grad.at[rows_of(i), :])

    def put_input_grad(i, value):
        r.dz[rows_of(i), :] = value
        send(r.dz.at[rows_of(i), :], input_grad.at[rows_of(i), :])

    r.put_layer_out, r.put_memory_grad, r.put_input_grad = put_layer_out, put_memory_grad, put_input_grad

    def emit(m, first):
        def one(c, value):
            stage[...] = value
            at = first + c
            if m == 0 and first < 6:
                at = c * 2 + first // 3
            cols = pl.ds(pl.multiple_of(at * 256, 256), 256)
            copy = pltpu.make_async_copy(stage, mat_grad.at[m, :, cols], sem)
            copy.start()
            copy.wait()

        return one

    run(r, emit)
    vec_grad[...] = jnp.sum(r.vg[...], axis=1)


def plain(tlen, slen, tokens, memory, out_grad, w, vecs):
    V = pl.BlockSpec(memory_space=pltpu.VMEM)
    S = pl.BlockSpec(memory_space=pltpu.SMEM)
    A = pl.BlockSpec(memory_space=pl.ANY)
    return pl.pallas_call(
        plain_kernel,
        out_shape=(
            jax.ShapeDtypeStruct((1024, 512), BF),
            jax.ShapeDtypeStruct((1024, 512), F32),
            jax.ShapeDtypeStruct((1024, 512), F32),
            jax.ShapeDtypeStruct((4, 512, 2048), F32),
            jax.ShapeDtypeStruct((VROWS, 512), F32),
        ),
        in_specs=[S, S, V, V, V, V, V],
        out_specs=(A, A, A, A, V),
        scratch_shapes=[pltpu.VMEM((512, 256), F32), pltpu.SemaphoreType.DMA] + [pltpu.VMEM(s, d) for _, s, d in SCRATCH],
        compiler_params=pltpu.CompilerParams(vmem_limit_bytes=63400000),
        name="layer",
    )(tlen, slen, tokens, memory, out_grad, w, vecs)


class Place:
    def __init__(self):
        dp, sh = lax.axis_index("dp"), lax.axis_index("shard")
        self.z, self.y, self.x, self.c = dp // 2, dp % 2, sh // 2, sh % 2
        z, y, x, c = self.z, self.y, self.x, self.c
        self.y1, self.x1 = y + c * (1 - 2 * y), x + (1 - c) * (1 - 2 * x)
        self.y2, self.x2 = y + (1 - c) * (1 - 2 * y), x + c * (1 - 2 * x)
        self.y3, self.x3 = 1 - y, 1 - x
        self.i1, self.i2 = x * (1 - c) + y * c, y * (1 - c) + x * c
        self.first = (z * 2 + self.y1, self.x1 * 2 + c)
        self.second = (z * 2 + self.y2, self.x2 * 2 + c)
        self.twin = (z * 2 + y, x * 2 + 1 - c)

    def along_z(self, d):
        return (lax.rem(self.z + d, 4) * 2 + self.y, self.x * 2 + self.c)

    def in_plane(self, n):
        flat = lax.rem(self.y * 4 + self.x * 2 + self.c + n, 8)
        return (self.z * 2 + flat // 4, flat % 4)


class Gather:
    def __init__(self, at, ref, cols, index, send, recv):
        self.at, self.ref, self.cols, self.index, self.send, self.recv = at, ref, cols, index, send, recv

    def copy(self, slot, arriving=False):
        p, c = self.at, self.at.c
        if slot < 3:
            d = slot + 1
            z = lax.rem(p.z + 4 - d, 4) if arriving else p.z
            what, device = self.ref.at[z, p.y, p.x, c, :, self.cols], p.along_z(d)
        else:
            own, second, first, far = (p.y, p.x), (p.y2, p.x2), (p.y1, p.x1), (p.y3, p.x3)
            sent, got, device = {
                3: (own, second, p.second),
                4: (own, first, p.first),
                5: (own, own, p.twin),
                6: (second, far, p.first),
                7: (second, first, p.twin),
                8: (first, second, p.twin),
                9: (far, far, p.twin),
            }[slot]
            y, x = got if arriving else sent
            if arriving and slot not in (3, 4, 6):
                c = 1 - c
            what = self.ref.at[:, y, x, c, :, self.cols]
        return pltpu.make_async_remote_copy(
            src_ref=what,
            dst_ref=what,
            send_sem=self.send.at[self.index, slot],
            recv_sem=self.recv.at[self.index, slot],
            device_id=device,
            device_id_type=MESH,
        )

    def go(self, *slots):
        for slot in slots:
            self.copy(slot).start()

    def await_slots(self, *slots):
        for slot in slots:
            self.copy(slot, True).wait_recv()

    def step0(self):
        self.go(0, 1, 2)

    def step1(self):
        self.await_slots(0, 1, 2)
        self.go(3, 4, 5)

    def step2(self):
        self.await_slots(3)
        self.go(6, 7)

    def step3(self):
        self.await_slots(4)
        self.go(8)
        self.await_slots(6)
        self.go(9)

    def step4(self):
        self.await_slots(5, 7, 8, 9)

    def finish(self):
        for slot in range(10):
            self.copy(slot).wait_send()


class Reduce:
    def __init__(self, at, keep, give, recvs, own, cols, places, index, send, recv):
        self.at, self.keep, self.give, self.recvs, self.own, self.cols = at, keep, give, recvs, own, cols
        self.places = places
        self.index, self.send, self.recv = index, send, recv

    def copy(self, slot):
        p, cols = self.at, self.cols
        if slot == 0:
            what, where, device = self.give.at[:, :, :, :, cols], self.recvs[0].at[:, :, :, :, cols], p.twin
        elif slot == 1:
            what, where, device = self.keep.at[:, :, 1 - p.i1, :, cols], self.recvs[1].at[:, :, :, cols], p.first
        elif slot == 2:
            what, where, device = self.keep.at[:, 1 - p.i2, p.i1, :, cols], self.recvs[2].at[:, :, cols], p.second
        else:
            d = slot - 2
            what = self.keep.at[lax.rem(p.z + d, 4), p.i2, p.i1, :, cols]
            where, device = self.recvs[3].at[d - 1, :, cols], p.along_z(d)
        return pltpu.make_async_remote_copy(
            src_ref=what,
            dst_ref=where,
            send_sem=self.send.at[self.index, slot],
            recv_sem=self.recv.at[self.index, slot],
            device_id=device,
            device_id_type=MESH,
        )

    def step0(self):
        self.copy(0).start()

    def step1(self):
        cols = self.cols
        self.copy(0).wait_recv()

        def add(z):
            self.keep[z, :, :, :, cols] = self.keep[z, :, :, :, cols] + self.recvs[0][z, :, :, :, cols]

        loop(4, add)
        self.copy(1).start()

    def step2(self):
        p, cols = self.at, self.cols
        self.copy(1).wait_recv()
        self.keep[:, :, p.i1, :, cols] = self.keep[:, :, p.i1, :, cols] + self.recvs[1][:, :, :, cols]
        self.copy(2).start()

    def step3(self):
        p, cols = self.at, self.cols
        self.copy(2).wait_recv()
        self.keep[:, p.i2, p.i1, :, cols] = self.keep[:, p.i2, p.i1, :, cols] + self.recvs[2][:, :, cols]
        for slot in range(3, 6):
            self.copy(slot).start()

    def step4(self):
        p, cols = self.at, self.cols
        total = self.keep[p.z, p.i2, p.i1, :, cols].astype(F32)
        for slot in range(3, 6):
            self.copy(slot).wait_recv()
            total = total + self.recvs[3][slot - 3, :, cols].astype(F32)
        for source, target, width in self.places:
            self.own[:, target : target + width] = total[:, source : source + width]

    def finish(self):
        for slot in range(6):
            self.copy(slot).wait_send()


FUSED_SCRATCH = [
    ("g0", (4, 2, 2, 2, 16, 2176), BF),
    ("g1", (4, 2, 2, 2, 16, 2048), BF),
    ("g2", (4, 2, 2, 2, 16, 2048), BF),
    ("g3", (4, 2, 2, 2, 16, 2048), BF),
    ("vecs", (VROWS, 512), F32),
    ("ra", (4, 4, 2, 2, 16, 2048), BF),
    ("rb", (4, 4, 2, 16, 2048), BF),
    ("rc", (4, 4, 16, 2048), BF),
    ("rd", (4, 3, 16, 2048), BF),
    ("vkeep", (4, 2, 2, 16, 128), BF),
    ("vgive", (4, 2, 2, 16, 128), BF),
    ("va", (4, 2, 2, 16, 128), BF),
    ("vb", (4, 2, 16, 128), BF),
    ("vc", (4, 16, 128), BF),
    ("vd", (3, 16, 128), BF),
    ("nsend", (2, 8, 128), F32),
    ("nrecv", (10, 8, 128), F32),
]
N_GATHER = 12
N_REDUCE = 8


def adam_parts(params, grad_in, first, second, factor):
    clipped = factor * grad_in
    first_m = BETA_ONE * first + (1.0 - BETA_ONE) * clipped
    second_m = BETA_TWO * second + (1.0 - BETA_TWO) * clipped * clipped
    stepped = first_m / CORRECT_ONE / (jnp.sqrt(second_m / CORRECT_TWO) + ADAM_EPS)
    return (-LEARN_RATE * (stepped + WEIGHT_DECAY * params), first_m, second_m)


def fused_kernel(
    tlen, slen, tokens, memory, out_grad, weights, vectors, layer_out, input_grad, memory_grad, own, vown, norm_out, *scratch
):
    r = Bag()
    names = [n for n, _, _ in SCRATCH] + [n for n, _, _ in FUSED_SCRATCH]
    for name, ref in zip(names, scratch):
        setattr(r, name, ref)
    g_send, g_recv, s_send, s_recv, n_send, n_recv, l_sem = scratch[len(names) :]
    p = Place()
    r.tlen, r.slen, r.tokens, r.memory, r.own, r.vown = tlen, slen, tokens, memory, own, vown
    r.g = r.du
    hidden_access(r)
    mats = [r.g0, r.g1, r.g2, r.g3]

    def w(m, a, b):
        shift = 128 if m == 0 else 0
        return mats[m][:, :, :, :, :, a + shift : b + shift].reshape(512, b - a)

    r.w = w

    barrier = pltpu.get_barrier_semaphore()
    for d in range(1, 4):
        pl.semaphore_signal(barrier, inc=1, device_id=p.along_z(d), device_id_type=MESH)
    for n in range(1, 8):
        pl.semaphore_signal(barrier, inc=1, device_id=p.in_plane(n), device_id_type=MESH)
    grad_in = pltpu.make_async_copy(out_grad, r.db, l_sem.at[0])
    grad_in.start()
    r.g0[p.z, p.y, p.x, p.c, :, 0:128] = jnp.concatenate(
        [vectors[...], jnp.zeros((16, 128 - vectors.shape[1]), F32)], axis=1
    ).astype(BF)
    for m in range(4):
        shift = 128 if m == 0 else 0
        mats[m][p.z, p.y, p.x, p.c, :, shift : shift + 2048] = weights[16 * m : 16 * m + 16, :].astype(BF)
    pl.semaphore_wait(barrier, 10)

    gathers = []
    for m, cuts in ((0, (0, 640, 1152, 1664, 2176)), (1, (0, 512, 1024, 1536, 2048)), (2, (0, 1024, 2048)), (3, (0, 1024, 2048))):
        for a, b in zip(cuts[:-1], cuts[1:]):
            gathers.append(Gather(p, mats[m], slice(a, b), len(gathers), g_send, g_recv))
    for g in gathers:
        g.step0()

    def steps(*pairs):
        return [getattr(gathers[k], "step%d" % s) for k, s in pairs]

    keeps = {0: r.hd.at[1, 0], 1: r.hd.at[0, 0], 2: r.g2.at[:, :, :, 0], 3: r.g3.at[:, :, :, 0]}
    gives = {0: r.hd.at[1, 1], 1: r.hd.at[0, 1], 2: r.g2.at[:, :, :, 1], 3: r.g3.at[:, :, :, 1]}

    def spread(value, keep, give, cols):
        v = value.reshape(4, 2, 2, 2, 16, value.shape[-1])
        flag = p.c == 0
        for y in range(2):
            for x in range(2):
                i1, i2 = x * (1 - p.c) + y * p.c, y * (1 - p.c) + x * p.c
                even, odd = v[:, y, x, 0], v[:, y, x, 1]
                keep[:, i2, i1, :, cols] = jnp.where(flag, even, odd).astype(BF)
                give[:, i1, i2, :, cols] = jnp.where(flag, odd, even).astype(BF)

    def emit(m, first):
        def one(c, value):
            spread(value, keeps[m], gives[m], pl.ds(pl.multiple_of((first + c) * 256, 256), 256))

        return one

    def job(k, m, a, b, places=None):
        return Reduce(
            p, keeps[m], gives[m], (r.ra.at[m], r.rb.at[m], r.rc.at[m], r.rd.at[m]), r.own.at[16 * m : 16 * m + 16, :],
            slice(a, b), places or ((0, a, b - a),), k, s_send, s_recv,
        )

    halves = [tuple((256 * part, 512 * part + 256 * h, 256) for part in range(3)) for h in range(2)]
    j3, j2, j1o, j1 = job(0, 3, 0, 2048), job(1, 2, 0, 2048), job(2, 1, 1536, 2048), job(3, 1, 0, 1536)
    j0o, j0a, j0b = job(4, 0, 1536, 2048), job(5, 0, 0, 768, halves[0]), job(6, 0, 768, 1536, halves[1])
    jv = Reduce(
        p, r.vkeep, r.vgive, (r.va, r.vb, r.vc, r.vd), r.vown, slice(0, 128), ((0, 0, 128),), 7, s_send, s_recv
    )
    jobs = [j3, j2, j1o, j1, j0o, j0a, j0b, jv]

    def read_vectors():
        for b in range(4):
            block = r.g0[b, :, :, :, :, 0:128].reshape(128, 128).astype(F32)
            r.vecs[:, b * 128 : (b + 1) * 128] = block.T[0:VROWS, :]

    def middle_done():
        for g in gathers:
            g.finish()
        for k in range(4):
            layer_part(k // 2, k % 2).wait()

    hooks = {
        "start0": steps((0, 1), (1, 1), (0, 2), (2, 1), (1, 2), (0, 3), (3, 1), (2, 2), (1, 3), (0, 4)) + [read_vectors],
        "start1": steps((4, 1), (3, 2), (2, 3), (1, 4)),
        "start2": steps((5, 1), (4, 2), (2, 4)),
        "projected": steps((6, 1), (3, 3), (5, 2)),
        "self0": steps((7, 1), (3, 4), (4, 3), (6, 2)),
        "self1": steps((8, 1), (4, 4), (5, 3), (7, 2)),
        "self2": steps((9, 1), (5, 4), (6, 3), (7, 3), (8, 2)),
        "self3": steps((10, 1), (6, 4), (7, 4), (9, 2)),
        "cross_ready": steps((11, 1), (8, 3), (10, 2)),
        "crossed": [grad_in.wait],
        "middle": [middle_done],
        "grads3": [j3.step0],
        "grads2": [j2.step0, j3.step1],
        "grads1o": [j1o.step0],
        "grads1": [j1.step0, j2.step4, j1o.step3],
        "grads0o": [j0o.step0, j1.step1, j1o.step4],
        "self_back00": [j0o.step1],
        "self_back03": [j1.step2, j0o.step2],
        "grads00": [j0a.step0],
        "self_back11": [j1.step3, j0o.step3, j0a.step1],
        "self_back13": [j1.step4, j0o.step4, j0a.step2],
    }
    plan = {
        "cross": {
            0: steps((8, 4), (9, 3), (11, 2)),
            1: steps((9, 4), (10, 3)),
            2: steps((10, 4), (11, 3)),
            3: steps((11, 4)),
        },
        "cross_back": {
            0: [j2.step1],
            1: [j3.step2],
            3: [j3.step3],
            4: [j2.step2, j1o.step1],
            6: [j3.step4, j2.step3, j1o.step2],
        },
    }

    def vectors_out():
        sums = jnp.sum(r.vg[...], axis=1)
        sums = jnp.concatenate([sums, jnp.zeros((128 - VROWS, 512), F32)], axis=0)
        columns = jnp.concatenate([sums[:, b * 128 : (b + 1) * 128].T for b in range(4)], axis=0)
        spread(columns, r.vkeep, r.vgive, slice(0, 128))
        jv.step0()

    hooks["grads01"] = [j0b.step0, vectors_out]
    hooks["tail0"] = [j0a.step3]
    hooks["tail1"] = [j0b.step1, jv.step1]

    def hook(name):
        for action in hooks.get(name, ()):
            action()

    def at_step(name, t):
        for when, actions in plan.get(name, {}).items():

            @pl.when(t == when)
            def _():
                for action in actions:
                    action()

    r.get_out_grad = lambda i: r.db[rows_of(i), :]

    def layer_part(half, k):
        piece = r.xt.at[rows_of(half), k * 512 : k * 512 + 512]
        i = 2 * half + k
        return pltpu.make_async_copy(piece, layer_out.at[rows_of(i), :], l_sem.at[2 + i])

    def put_layer_out(half, k, value):
        r.xt[rows_of(half), k * 512 : k * 512 + 512] = value
        layer_part(half, k).start()

    def memory_part(i):
        return pltpu.make_async_copy(r.n1.at[rows_of(i), :], memory_grad.at[rows_of(i), :], l_sem.at[6 + i])

    def put_memory_grad(i, value):
        r.n1[rows_of(i), :] = value
        memory_part(i).start()

    def input_part(i):
        return pltpu.make_async_copy(r.dz.at[rows_of(i), :], input_grad.at[rows_of(i), :], l_sem.at[10 + i])

    def put_input_grad(i, value):
        r.dz[rows_of(i), :] = value
        input_part(i).start()

    r.put_layer_out, r.put_memory_grad, r.put_input_grad = put_layer_out, put_memory_grad, put_input_grad

    run(r, emit, hook, at_step)

    for step in (j0b.step2, jv.step2, j0a.step4, j0b.step3, jv.step3, j0b.step4, jv.step4):
        step()

    squares = jnp.sum((r.vown[...] * r.vown[...]).reshape(2, 8, 128), axis=0)
    for k in range(8):
        part = r.own[8 * k : 8 * k + 8, :]
        part = part * part
        for b in range(16):
            squares = squares + part[:, 128 * b : 128 * b + 128]
    r.nsend[0] = squares

    def plane_part(n):
        return pltpu.make_async_remote_copy(
            src_ref=r.nsend.at[0], dst_ref=r.nrecv.at[n - 1], send_sem=n_send.at[n - 1], recv_sem=n_recv.at[n - 1],
            device_id=p.in_plane(n), device_id_type=MESH,
        )

    def z_part(d):
        return pltpu.make_async_remote_copy(
            src_ref=r.nsend.at[1], dst_ref=r.nrecv.at[6 + d], send_sem=n_send.at[6 + d], recv_sem=n_recv.at[6 + d],
            device_id=p.along_z(d), device_id_type=MESH,
        )

    for n in range(1, 8):
        plane_part(n).start()
    total = r.nsend[0]
    for n in range(1, 8):
        plane_part(n).wait_recv()
        total = total + r.nrecv[n - 1]
    r.nsend[1] = total
    for d in range(1, 4):
        z_part(d).start()
    for k in range(4):
        memory_part(k).wait()
        input_part(k).wait()
    for j in jobs:
        j.finish()
    for n in range(1, 8):
        plane_part(n).wait_send()
    for d in range(1, 4):
        z_part(d).wait_recv()
        total = total + r.nrecv[6 + d]
    norm_out[...] = jnp.broadcast_to(jnp.sqrt(jnp.sum(total)), (8, 128))
    for d in range(1, 4):
        z_part(d).wait_send()


def finish_kernel(
    layer_in, input_in, memory_in, own, weights, moments, vown, norm, norm_scalar, vectors, vector_moments,
    layer_out, input_grad, memory_grad, norm_out, mat_out, step_out, first_out, second_out, vec_out, vstep_out, vfirst_out,
    vsecond_out, low_room, big_room, mats, sems, out_sems,
):
    small = []
    for n, (source, at, size) in enumerate(((own, 0, 64), (weights, 64, 64), (moments, 128, 128))):
        small.append(pltpu.make_async_copy(source, mats.at[at : at + size, :], sems.at[10 + n]))
        small[-1].start()
    arrivals, departures = [], []
    for source, target, room, pieces in (
        (layer_in, layer_out, low_room, 2),
        (memory_in, memory_grad, big_room.at[0], 4),
        (input_in, input_grad, big_room.at[1], 4),
    ):
        size = source.shape[0] // pieces
        for k in range(pieces):
            rows, n = slice(k * size, k * size + size), len(arrivals)
            arrivals.append(pltpu.make_async_copy(source.at[rows, :], room.at[rows, :], sems.at[n]))
            departures.append(pltpu.make_async_copy(room.at[rows, :], target.at[rows, :], out_sems.at[n]))
            arrivals[-1].start()
    norm_out[0, 0] = norm_scalar[0, 0]
    factor = jnp.minimum(1.0, CLIP_NORM / (norm[0:1, 0:1] + 1e-06))
    count = vectors.shape[1]
    vgrad = vown[:, 0:count]
    vec_out[...] = vgrad
    vstep_out[...], vfirst_out[...], vsecond_out[...] = adam_parts(
        vectors[...], vgrad, vector_moments[0], vector_moments[1], factor
    )
    for copy in small:
        copy.wait()
    for n, (target, at) in enumerate(((mat_out, 0), (step_out, 64), (first_out, 128), (second_out, 192))):
        departures.append(pltpu.make_async_copy(mats.at[at : at + 64, :], target, out_sems.at[10 + n]))
    departures[10].start()

    def update(i):
        a, b, c, d = (pl.ds(pl.multiple_of(i * 16 + o, 16), 16) for o in (0, 64, 128, 192))
        mats[b, :], mats[c, :], mats[d, :] = adam_parts(mats[b, :], mats[a, :], mats[c, :], mats[d, :], factor)

    for arrival, departure in zip(arrivals[:5], departures[:5]):
        arrival.wait()
        departure.start()
    loop(4, update)
    for departure in departures[11:]:
        departure.start()
    for arrival, departure in zip(arrivals[5:], departures[5:10]):
        arrival.wait()
        departure.start()
    for departure in departures:
        departure.wait()


def fused_body(tokens, memory, target_lengths, source_lengths, out_grad, weights, vectors, weight_moments, vector_moments):
    V = pl.BlockSpec(memory_space=pltpu.VMEM)
    S = pl.BlockSpec(memory_space=pltpu.SMEM)
    A = pl.BlockSpec(memory_space=pl.ANY)
    mat = jax.ShapeDtypeStruct((64, 2048), F32)
    vec_shape = jax.ShapeDtypeStruct(vectors.shape[::-1], F32)
    low = jax.ShapeDtypeStruct(tokens.shape, BF)
    big = jax.ShapeDtypeStruct(tokens.shape, F32)
    flat_weights, flat_vectors = weights.reshape(64, 2048), vectors.T
    layer_out, input_grad, memory_grad, own, vown, norm = pl.pallas_call(
        fused_kernel,
        out_shape=(low, big, big, mat, jax.ShapeDtypeStruct((16, 128), F32), jax.ShapeDtypeStruct((8, 128), F32)),
        in_specs=[S, S, V, V, A, V, V],
        out_specs=(A, A, A, V, V, V),
        scratch_shapes=[pltpu.VMEM(s, d) for _, s, d in SCRATCH + FUSED_SCRATCH]
        + [
            pltpu.SemaphoreType.DMA((N_GATHER, 10)),
            pltpu.SemaphoreType.DMA((N_GATHER, 10)),
            pltpu.SemaphoreType.DMA((N_REDUCE, 6)),
            pltpu.SemaphoreType.DMA((N_REDUCE, 6)),
            pltpu.SemaphoreType.DMA((10,)),
            pltpu.SemaphoreType.DMA((10,)),
            pltpu.SemaphoreType.DMA((14,)),
        ],
        compiler_params=pltpu.CompilerParams(vmem_limit_bytes=63400000, collective_id=0, has_side_effects=True),
        name="layer",
    )(target_lengths, source_lengths, tokens, memory, out_grad, flat_weights, flat_vectors)
    layer_out, input_grad, memory_grad, norm, g, st, m1, m2, vg, vst, vm1, vm2 = pl.pallas_call(
        finish_kernel,
        out_shape=(low, big, big, jax.ShapeDtypeStruct((1, 1), F32), mat, mat, mat, mat) + (vec_shape,) * 4,
        in_specs=[A, A, A, A, A, A, V, V, S, V, V],
        out_specs=(A, A, A, S, A, A, A, A, V, V, V, V),
        scratch_shapes=[
            pltpu.VMEM(tokens.shape, BF),
            pltpu.VMEM((2,) + tokens.shape, F32),
            pltpu.VMEM((256, 2048), F32),
            pltpu.SemaphoreType.DMA((13,)),
            pltpu.SemaphoreType.DMA((14,)),
        ],
        compiler_params=pltpu.CompilerParams(vmem_limit_bytes=63400000),
        name="finish",
    )(
        layer_out, input_grad, memory_grad, own, flat_weights, weight_moments.reshape(128, 2048), vown, norm, norm, flat_vectors,
        vector_moments.transpose(0, 2, 1),
    )
    back = lambda a: a.reshape(weights.shape)
    return (
        layer_out, input_grad, memory_grad, norm[0, 0], back(g), vg.T, back(st), vst.T, back(m1), back(m2), vm1.T, vm2.T,
    )


def adam_update(params, grad_in, moments, factor):
    clipped = factor * grad_in
    first_m = BETA_ONE * moments[0] + (1.0 - BETA_ONE) * clipped
    second_m = BETA_TWO * moments[1] + (1.0 - BETA_TWO) * clipped * clipped
    stepped = first_m / CORRECT_ONE / (jnp.sqrt(second_m / CORRECT_TWO) + ADAM_EPS)
    return (-LEARN_RATE * (stepped + WEIGHT_DECAY * params), first_m, second_m)


def generic_body(tokens, memory, target_lengths, source_lengths, out_grad, weights, vectors, weight_moments, vector_moments):
    axes = ("dp", "shard")
    w = lax.all_gather(weights.astype(BF), axes, axis=1, tiled=True)
    vecs = lax.all_gather(vectors.astype(BF), axes, axis=1, tiled=True).astype(F32)
    vecs = jnp.concatenate([vecs, jnp.zeros((VROWS - vecs.shape[0], vecs.shape[1]), F32)], axis=0)
    layer_out, input_grad, memory_grad, mat_grad, vec_grad = plain(
        target_lengths, source_lengths, tokens, memory, out_grad, w, vecs
    )
    mat_share = lax.psum_scatter(mat_grad, axes, scatter_dimension=1, tiled=True)
    vec_share = lax.psum_scatter(vec_grad[: vectors.shape[0]], axes, scatter_dimension=1, tiled=True)
    squares = jnp.sum(mat_share * mat_share) + jnp.sum(vec_share * vec_share)
    grad_norm = jnp.sqrt(lax.psum(squares, axes))
    factor = jnp.minimum(1.0, CLIP_NORM / (grad_norm + 1e-06))
    weight_steps, weight_first, weight_second = adam_update(weights, mat_share, weight_moments, factor)
    vector_steps, vector_first, vector_second = adam_update(vectors, vec_share, vector_moments, factor)
    return (
        layer_out, input_grad, memory_grad, grad_norm, mat_share, vec_share,
        weight_steps, vector_steps, weight_first, weight_second, vector_first, vector_second,
    )


def solution(mesh):
    both = ("dp", "shard")
    rows, mats, vecs = P(both, None), P(None, both, None), P(None, both)
    fits = (mesh.shape["dp"], mesh.shape["shard"]) == (8, 4)
    return jax.shard_map(
        fused_body if fits else generic_body,
        mesh=mesh,
        in_specs=(rows, rows, rows, rows, rows, mats, vecs, P(None, None, both, None), P(None, None, both)),
        out_specs=(rows, rows, rows, P(), mats, vecs, mats, vecs, mats, mats, vecs, vecs),
        check_vma=False,
    )
```

```python
import functools
import jax
import jax.numpy as jnp
from jax import lax
from jax.experimental import pallas as pl
from jax.experimental.pallas import tpu as pltpu
from jax.sharding import PartitionSpec as P

HD = 64
EPSILON = 1e-05
MASKED = -1e30
BF = jnp.bfloat16
F32 = jnp.float32
TILE = 256
VROWS = 24
FWD_UNROLL = 4
GRAD_UNROLL = 2
GRAD_WIDTH = 256
TILE_UNROLL = 4
BACK_UNROLL = 2
CROSS_KEYS = 512
MESH = pl.DeviceIdType.MESH
CLIP_NORM = 1.0
LEARN_RATE = 0.001
BETA_ONE = 0.9
BETA_TWO = 0.999
ADAM_EPS = 1e-08
WEIGHT_DECAY = 0.1
CORRECT_ONE = 1.0 - 0.9**3
CORRECT_TWO = 1.0 - 0.999**3


def mm(left, right):
    return jnp.dot(left, right, preferred_element_type=F32)


def mm_t(left, right):
    return lax.dot_general(left, right, (((1,), (1,)), ((), ())), preferred_element_type=F32)


def t_mm(left, right):
    return lax.dot_general(left, right, (((0,), (0,)), ((), ())), preferred_element_type=F32)


def rows_of(i, size=TILE):
    return pl.ds(pl.multiple_of(i * size, size), size)


def normed(z):
    centred = z - jnp.mean(z, axis=-1, keepdims=True)
    inverse = lax.rsqrt(jnp.mean(centred * centred, axis=-1, keepdims=True) + EPSILON)
    return centred * inverse, inverse


def norm_back(grad, n, inverse, gain):
    scaled = grad * gain
    return inverse * (
        scaled
        - jnp.mean(scaled, axis=-1, keepdims=True)
        - n * jnp.mean(scaled * n, axis=-1, keepdims=True)
    )


def fold(values):
    r, c = values.shape
    return jnp.sum(values.astype(F32).reshape(r // 8, 8, c), axis=0)


def heads_join(ref, rows):
    return jnp.concatenate([ref[p, rows, :] for p in range(4)], axis=1)


def heads_split(ref, rows, value):
    for p in range(4):
        ref[p, rows, :] = value[:, p * 128 : (p + 1) * 128]


class Bag:
    pass


def head_mask(h, dtype):
    lane = lax.broadcasted_iota(jnp.int32, (1, 128), 1)
    return jnp.where((lane < HD) if h == 0 else (lane >= HD), 1.0, 0.0).astype(dtype)


def segments(r, lengths, row_ref, lane):
    ends = []
    total = jnp.int32(0)
    for s in range(16):
        total = total + lengths[0, s]
        ends.append(total)

    def number(at):
        seg = jnp.zeros(at.shape, F32)
        for e in ends:
            seg = seg + jnp.where(e <= at, 1.0, 0.0)
        return seg

    row_ref[...] = number(lax.broadcasted_iota(jnp.int32, (8, 1024), 1))

    def col(i):
        r.cols[rows_of(i), lane : lane + 1] = number(lax.broadcasted_iota(jnp.int32, (TILE, 128), 0) + i * TILE)[:, 0:1]

    loop(4, col)


def attend(r, q_ref, k_ref, v_ref, out_ref, lse_ref, tile, key_start, key_count, bias):
    rows = rows_of(tile)
    keys = pl.ds(key_start, key_count)
    lane = lax.broadcasted_iota(jnp.int32, (TILE, 128), 1)

    def pair(p, _):
        q = q_ref[p, rows, :]
        k = k_ref[p, keys, :]
        v = v_ref[p, keys, :]
        tops, weights, values = [], [], []
        for h in range(2):
            m = head_mask(h, BF)
            s = mm_t(q * m, k) + bias[:, :key_count]
            tops.append(jnp.max(s, axis=-1, keepdims=True))
            weights.append(jnp.exp(s - tops[h]).astype(BF))
            values.append(jnp.concatenate([v * m, jnp.broadcast_to(m, (key_count, 128))], axis=1))
        both = mm(jnp.concatenate(weights, axis=1), jnp.concatenate(values, axis=0))
        total = both[:, 128:256]
        out_ref[p, rows, :] = (both[:, 0:128] * (1.0 / total)).astype(BF)
        lse = (jnp.where(lane < HD, tops[0], tops[1]) + jnp.log(total)).T
        lse_ref[2 * p, :, rows] = lse[0:1, :]
        lse_ref[2 * p + 1, :, rows] = lse[HD : HD + 1, :]
        return 0

    lax.fori_loop(0, 4, pair, 0, unroll=FWD_UNROLL)


def deltas(r, out_ref, grad_ref, delta_ref, tile):
    rows = rows_of(tile)
    lane = lax.broadcasted_iota(jnp.int32, (TILE, 128), 1)
    table = jnp.zeros((TILE, 128), F32)
    for p in range(4):
        prod = out_ref[p, rows, :].astype(F32) * grad_ref[p, rows, :].astype(F32)
        for h in range(2):
            one = jnp.sum(prod * head_mask(h, F32), axis=-1, keepdims=True)
            table = jnp.where(lane == 2 * p + h, one, table)
    flipped = table.T
    for h in range(8):
        delta_ref[h, :, rows] = flipped[h : h + 1, :]


def attend_back(r, q_ref, k_ref, v_ref, grad_ref, lse_ref, delta_ref, i, key_start, key_count, pairs, unroll):
    qr, kr = rows_of(i), pl.ds(key_start, key_count)
    lane = lax.broadcasted_iota(jnp.int32, (TILE, 128), 1)
    key_lane = lax.broadcasted_iota(jnp.int32, (key_count, 128), 1)

    def pair(p, _):
        q, k, v, g = q_ref[p, qr, :], k_ref[p, kr, :], v_ref[p, kr, :], grad_ref[p, qr, :]
        dv, dk, dq = [], [], []
        for h in range(2):
            m = head_mask(h, BF)
            s = mm_t(k * m, q) + r.bias[0:key_count, :]
            w = jnp.exp(s - lse_ref[2 * p + h, :, qr])
            dp = mm_t(v * m, g)
            ds = (w * (dp - delta_ref[2 * p + h, :, qr])).astype(BF)
            dv.append(mm(w.astype(BF), g))
            dk.append(mm(ds, q))
            dq.append(t_mm(ds, k))
        r.dv[p, kr, :] += jnp.where(key_lane < HD, dv[0], dv[1])
        r.dk[p, kr, :] += jnp.where(key_lane < HD, dk[0], dk[1])
        r.dq[p, qr, :] += jnp.where(lane < HD, dq[0], dq[1])
        return 0

    lax.fori_loop(pairs[0], pairs[1], pair, 0, unroll=unroll)


def zero_grads(r):
    def step(i, _):
        z = jnp.zeros((4, TILE, 128), F32)
        r.dq[:, rows_of(i), :] = z
        r.dk[:, rows_of(i), :] = z
        r.dv[:, rows_of(i), :] = z
        return 0

    lax.fori_loop(0, 4, step, 0)


def vec(r, row):
    return r.vecs[row : row + 1, :]


def add_vec(r, row, value):
    r.vg[row] += value


def project_self(r, i, part):
    rows = rows_of(i)
    value = mm(r.tokens[rows, :], r.w(0, 512 * part, 512 * part + 512))
    if part == 0:
        heads_split(r.q, rows, ((value + vec(r, 0)).astype(BF) * 0.125).astype(BF))
    elif part == 1:
        heads_split(r.k, rows, value.astype(BF))
    else:
        heads_split(r.v, rows, (value + vec(r, 1)).astype(BF))


def self_bias(r, i, start, count):
    qs = r.cols[rows_of(i), 0:1]
    ks = r.trow[0:1, start : start + count]
    at = lax.broadcasted_iota(jnp.int32, (TILE, count), 0) + i * TILE
    key = lax.broadcasted_iota(jnp.int32, (TILE, count), 1) + start
    r.gate[:, 0:count] = jnp.where((qs == ks) & (key <= at), 0.0, MASKED)


def after_self(r, i):
    rows = rows_of(i)
    a = heads_join(r.a, rows)
    z = r.tokens[rows, :].astype(F32) + (mm(a, r.w(0, 1536, 2048)) + vec(r, 2))
    n, inverse = normed(z)
    r.n1[rows, :] = n
    r.cols[rows, 2:3] = inverse
    y = (n * vec(r, 3) + vec(r, 4)).astype(BF)
    r.y1[rows, :] = y
    heads_split(r.q2, rows, ((mm(y, r.w(1, 0, 512)) + vec(r, 5)).astype(BF) * 0.125).astype(BF))


def project_cross(r, i):
    rows = rows_of(i)
    m = r.memory[rows, :]
    heads_split(r.k2, rows, mm(m, r.w(1, 512, 1024)).astype(BF))
    heads_split(r.v2, rows, (mm(m, r.w(1, 1024, 1536)) + vec(r, 6)).astype(BF))


def cross_bias(r, i):
    qs = r.cols[rows_of(i), 0:1]
    ks = r.srow[0:1, :]
    r.gate[:, 0:1024] = jnp.where(qs == ks, 0.0, MASKED)


def middle(r, half, k, room):
    i = 2 * half + k
    rows = rows_of(i)
    y1 = r.n1[rows, :] * vec(r, 3) + vec(r, 4)
    z2 = y1 + (mm(heads_join(r.a2, rows), r.w(1, 1536, 2048)) + vec(r, 7))
    n2, r2 = normed(z2)
    y2 = n2 * vec(r, 8) + vec(r, 9)
    y2l = y2.astype(BF)
    r.y2[rows, :] = y2l
    f = jnp.zeros((TILE, 512), F32)
    for c in range(4):
        cols = slice(c * 512, (c + 1) * 512)
        u = mm(y2l, r.w(2, cols.start, cols.stop)) + vec(r, 10 + c)
        s = jax.nn.sigmoid(u)
        hd = (u * s).astype(BF)
        r.put_hidden(i, cols, hd)
        heads_split(room, rows_of(c), s * (1.0 + u * (1.0 - s)))
        f = f + mm_t(hd, r.w(3, cols.start, cols.stop))
    n3, r3 = normed(y2 + (f + vec(r, 14)))
    r.put_layer_out(half, k, (n3 * vec(r, 15) + vec(r, 16)).astype(BF))
    g = r.get_out_grad(i).astype(F32)
    add_vec(r, 15, fold(g * n3))
    add_vec(r, 16, fold(g))
    dz3 = norm_back(g, n3, r3, vec(r, 15))
    df = dz3.astype(BF)
    r.df[rows, :] = df
    add_vec(r, 14, fold(df))
    dy2 = dz3
    for c in range(4):
        cols = slice(c * 512, (c + 1) * 512)
        du = (mm(df, r.w(3, cols.start, cols.stop)) * heads_join(room, rows_of(c))).astype(BF)
        r.du[rows, cols] = du
        add_vec(r, 10 + c, fold(du))
        dy2 = dy2 + mm_t(du, r.w(2, cols.start, cols.stop))
    add_vec(r, 8, fold(dy2 * n2))
    add_vec(r, 9, fold(dy2))
    dz2 = norm_back(dy2, n2, r2, vec(r, 8))
    r.dz[rows, :] = dz2
    db = dz2.astype(BF)
    r.db[rows, :] = db
    add_vec(r, 7, fold(db))
    heads_split(r.da, rows, mm_t(db, r.w(1, 1536, 2048)).astype(BF))
    deltas(r, r.a2, r.da, r.delta, i)


def finish_heads(r, i, vector_row, targets, pairs=(0, 4)):
    rows = rows_of(i)
    a, b = pairs[0] * 128, pairs[1] * 128
    for part, (ref, scale) in enumerate(((r.dq, 0.125), (r.dk, 1.0), (r.dv, 1.0))):
        value = jnp.concatenate([ref[p, rows, :] for p in range(*pairs)], axis=1)
        value = (value * scale).astype(BF)
        targets[part][rows, a:b] = value
        if part != 1:
            r.vg[vector_row + part // 2, :, a:b] += fold(value)


def after_cross_back(r, i):
    rows = rows_of(i)
    dy1 = r.dz[rows, :] + mm_t(r.g[rows, 0:512], r.w(1, 0, 512))
    n1 = r.n1[rows, :]
    add_vec(r, 3, fold(dy1 * n1))
    add_vec(r, 4, fold(dy1))
    dz1 = norm_back(dy1, n1, r.cols[rows, 2:3], vec(r, 3))
    r.dz[rows, :] = dz1
    db = dz1.astype(BF)
    r.db[rows, :] = db
    add_vec(r, 2, fold(db))
    heads_split(r.da, rows, mm_t(db, r.w(0, 1536, 2048)).astype(BF))
    deltas(r, r.a, r.da, r.delta, i)


def after_self_back(r, i):
    rows = rows_of(i)
    r.put_input_grad(
        i,
        r.dz[rows, :]
        + (
            mm_t(r.y1[rows, :], r.w(0, 0, 512))
            + mm_t(r.y2[rows, :], r.w(0, 512, 1024))
            + mm_t(r.df[rows, :], r.w(0, 1024, 1536))
        ),
    )


def memory_back(r, i):
    rows = rows_of(i)
    r.put_memory_grad(
        i, mm_t(r.g[rows, 512:1024], r.w(1, 512, 1024)) + mm_t(r.g[rows, 1024:1536], r.w(1, 1024, 1536))
    )


def cross_bias_t(r, i, key_start, key_count):
    ks = r.cols[pl.ds(key_start, key_count), 1:2]
    qs = r.trow[0:1, rows_of(i)]
    r.bias[0:key_count, :] = jnp.where(ks == qs, 0.0, MASKED)


def self_bias_t(r, i, key_start, key_count):
    ks = r.cols[pl.ds(key_start, key_count), 0:1]
    qs = r.trow[0:1, rows_of(i)]
    key = lax.broadcasted_iota(jnp.int32, (key_count, TILE), 0) + key_start
    at = lax.broadcasted_iota(jnp.int32, (key_count, TILE), 1) + i * TILE
    r.bias[0:key_count, :] = jnp.where((ks == qs) & (key <= at), 0.0, MASKED)


def loop(n, body, unroll=1):
    def step(i, _):
        body(i)
        return 0

    lax.fori_loop(0, n, step, 0, unroll=unroll)


def flip(r, source):
    def one(i):
        r.xt[:, rows_of(i)] = source(rows_of(i)).T

    loop(4, one, TILE_UNROLL)


def weight_grad(r, chunk_of, count, emit):
    def one(c, _):
        cols = pl.ds(pl.multiple_of(c * 256, 256), 256)
        emit(c, mm(r.xt[...], chunk_of(cols)))
        return 0

    lax.fori_loop(0, count, one, 0, unroll=GRAD_UNROLL)


def run(r, emit, hook=lambda name: None, at_step=lambda name, t: None):
    hook("enter")
    segments(r, r.tlen, r.trow, 0)
    segments(r, r.slen, r.srow, 1)

    def clear(i):
        r.vg[i] = jnp.zeros((8, 512), F32)

    loop(VROWS, clear)
    for part in range(3):
        hook("start%d" % part)
        loop(4, lambda i: project_self(r, i, part), TILE_UNROLL)
    hook("projected")
    for i in range(4):
        start = max(0, i - 2) * TILE
        count = (i + 1) * TILE - start
        self_bias(r, i, start, count)
        attend(r, r.q, r.k, r.v, r.a, r.lse, i, start, count, r.gate)
        hook("self%d" % i)
    loop(4, lambda i: project_cross(r, i), TILE_UNROLL)
    loop(4, lambda i: after_self(r, i), TILE_UNROLL)
    hook("cross_ready")

    def cross(i):
        cross_bias(r, i)
        attend(r, r.q2, r.k2, r.v2, r.a2, r.lse2, i, 0, 1024, r.gate)
        at_step("cross", i)

    loop(4, cross)
    hook("crossed")

    def two_tiles(i):
        middle(r, i, 0, r.dk)
        middle(r, i, 1, r.dv)

    loop(2, two_tiles)
    hook("middle")
    flip(r, lambda rows: r.df[rows, :])
    weight_grad(r, r.get_hidden, 8, emit(3, 0))
    hook("grads3")
    flip(r, lambda rows: r.y2[rows, :])
    weight_grad(r, lambda cols: r.du[:, cols], 8, emit(2, 0))
    hook("grads2")
    flip(r, lambda rows: heads_join(r.a2, rows))
    weight_grad(r, lambda cols: r.db[:, cols], 2, emit(1, 6))
    hook("grads1o")
    zero_grads(r)

    parts = 1024 // CROSS_KEYS

    def cross_back(t):
        i, start = t // parts, pl.multiple_of(t % parts * CROSS_KEYS, CROSS_KEYS)
        cross_bias_t(r, i, start, CROSS_KEYS)
        attend_back(r, r.q2, r.k2, r.v2, r.da, r.lse2, r.delta, i, start, CROSS_KEYS, (0, 4), BACK_UNROLL)
        at_step("cross_back", t)

    loop(4 * parts, cross_back)
    cross_g = [r.g.at[:, 512 * part : 512 * part + 512] for part in range(3)]
    loop(4, lambda i: finish_heads(r, i, 5, cross_g), TILE_UNROLL)
    flip(r, lambda rows: r.y1[rows, :])
    weight_grad(r, lambda cols: r.g[:, cols], 2, emit(1, 0))
    flip(r, lambda rows: r.memory[rows, :])
    weight_grad(r, lambda cols: r.g[:, pl.ds(cols.start + 512, 256)], 4, emit(1, 2))
    hook("grads1")
    loop(4, lambda i: after_cross_back(r, i), TILE_UNROLL)
    flip(r, lambda rows: heads_join(r.a, rows))
    weight_grad(r, lambda cols: r.db[:, cols], 2, emit(0, 6))
    hook("grads0o")
    zero_grads(r)
    flip(r, lambda rows: r.tokens[rows, :])
    for half in range(2):
        pairs = (2 * half, 2 * half + 2)
        for i in range(4):
            start = max(0, i - 2) * TILE
            count = (i + 1) * TILE - start
            self_bias_t(r, i, start, count)
            attend_back(r, r.q, r.k, r.v, r.da, r.lse, r.delta, i, start, count, pairs, BACK_UNROLL)
            hook("self_back%d%d" % (half, i))
        loop(4, lambda i: finish_heads(r, i, 0, (r.y1, r.y2, r.df), pairs), TILE_UNROLL)

        for part, ref in enumerate((r.y1, r.y2, r.df)):
            emit(0, 3 * half)(part, mm(r.xt[...], ref[:, half * 256 : half * 256 + 256]))
        hook("grads0%d" % half)
    loop(2, lambda i: after_self_back(r, i), 2)
    hook("tail0")
    loop(2, lambda i: after_self_back(r, i + 2), 2)
    hook("tail1")
    loop(4, lambda i: memory_back(r, i), TILE_UNROLL)


SCRATCH = [
    ("trow", (8, 1024), F32), ("srow", (8, 1024), F32), ("cols", (1024, 128), F32),
    ("q", (4, 1024, 128), BF), ("k", (4, 1024, 128), BF), ("v", (4, 1024, 128), BF), ("a", (4, 1024, 128), BF),
    ("q2", (4, 1024, 128), BF), ("k2", (4, 1024, 128), BF), ("v2", (4, 1024, 128), BF), ("a2", (4, 1024, 128), BF),
    ("da", (4, 1024, 128), BF), ("lse", (8, 1, 1024), F32), ("lse2", (8, 1, 1024), F32), ("delta", (8, 1, 1024), F32),
    ("n1", (1024, 512), F32), ("y1", (1024, 512), BF), ("y2", (1024, 512), BF),
    ("hd", (2, 2, 4, 2, 2, 16, 2048), BF), ("du", (1024, 2048), BF), ("df", (1024, 512), BF), ("db", (1024, 512), BF),
    ("gate", (256, 1024), F32), ("dz", (1024, 512), F32), ("bias", (768, 256), F32),
    ("dq", (4, 1024, 128), F32), ("dk", (4, 1024, 128), F32), ("dv", (4, 1024, 128), F32),
    ("xt", (512, 1024), BF), ("vg", (24, 8, 512), F32),
]


def hidden_access(r):
    def put(i, cols, value):
        r.hd[i // 2, i % 2, :, :, :, :, cols] = value.reshape(4, 2, 2, 16, 512)

    def get(cols):
        return r.hd[:, :, :, :, :, :, cols].reshape(1024, 256)

    r.put_hidden, r.get_hidden = put, get


def plain_kernel(
    tlen, slen, tokens, memory, out_grad, w, vecs, layer_out, input_grad, memory_grad, mat_grad, vec_grad, stage, sem, *scratch
):
    r = Bag()
    r.tlen, r.slen, r.tokens, r.memory, r.vecs = tlen, slen, tokens, memory, vecs
    for (name, _, _), ref in zip(SCRATCH, scratch):
        setattr(r, name, ref)
    r.g = r.du
    r.w = lambda m, a, b: w[m, :, a:b]
    hidden_access(r)
    r.get_out_grad = lambda i: out_grad[rows_of(i), :]

    def send(source, target):
        copy = pltpu.make_async_copy(source, target, sem)
        copy.start()
        copy.wait()

    def put_layer_out(half, k, value):
        piece = r.xt.at[rows_of(half), k * 512 : k * 512 + 512]
        piece[...] = value
        send(piece, layer_out.at[rows_of(2 * half + k), :])

    def put_memory_grad(i, value):
        r.n1[rows_of(i), :] = value
        send(r.n1.at[rows_of(i), :], memory_grad.at[rows_of(i), :])

    def put_input_grad(i, value):
        r.dz[rows_of(i), :] = value
        send(r.dz.at[rows_of(i), :], input_grad.at[rows_of(i), :])

    r.put_layer_out, r.put_memory_grad, r.put_input_grad = put_layer_out, put_memory_grad, put_input_grad

    def emit(m, first):
        def one(c, value):
            stage[...] = value
            at = first + c
            if m == 0 and first < 6:
                at = c * 2 + first // 3
            cols = pl.ds(pl.multiple_of(at * 256, 256), 256)
            copy = pltpu.make_async_copy(stage, mat_grad.at[m, :, cols], sem)
            copy.start()
            copy.wait()

        return one

    run(r, emit)
    vec_grad[...] = jnp.sum(r.vg[...], axis=1)


def plain(tlen, slen, tokens, memory, out_grad, w, vecs):
    V = pl.BlockSpec(memory_space=pltpu.VMEM)
    S = pl.BlockSpec(memory_space=pltpu.SMEM)
    A = pl.BlockSpec(memory_space=pl.ANY)
    return pl.pallas_call(
        plain_kernel,
        out_shape=(
            jax.ShapeDtypeStruct((1024, 512), BF),
            jax.ShapeDtypeStruct((1024, 512), F32),
            jax.ShapeDtypeStruct((1024, 512), F32),
            jax.ShapeDtypeStruct((4, 512, 2048), F32),
            jax.ShapeDtypeStruct((VROWS, 512), F32),
        ),
        in_specs=[S, S, V, V, V, V, V],
        out_specs=(A, A, A, A, V),
        scratch_shapes=[pltpu.VMEM((512, 256), F32), pltpu.SemaphoreType.DMA] + [pltpu.VMEM(s, d) for _, s, d in SCRATCH],
        compiler_params=pltpu.CompilerParams(vmem_limit_bytes=63400000),
        name="layer",
    )(tlen, slen, tokens, memory, out_grad, w, vecs)


class Place:
    def __init__(self):
        dp, sh = lax.axis_index("dp"), lax.axis_index("shard")
        self.z, self.y, self.x, self.c = dp // 2, dp % 2, sh // 2, sh % 2
        z, y, x, c = self.z, self.y, self.x, self.c
        self.y1, self.x1 = y + c * (1 - 2 * y), x + (1 - c) * (1 - 2 * x)
        self.y2, self.x2 = y + (1 - c) * (1 - 2 * y), x + c * (1 - 2 * x)
        self.y3, self.x3 = 1 - y, 1 - x
        self.i1, self.i2 = x * (1 - c) + y * c, y * (1 - c) + x * c
        self.first = (z * 2 + self.y1, self.x1 * 2 + c)
        self.second = (z * 2 + self.y2, self.x2 * 2 + c)
        self.twin = (z * 2 + y, x * 2 + 1 - c)

    def along_z(self, d):
        return (lax.rem(self.z + d, 4) * 2 + self.y, self.x * 2 + self.c)

    def in_plane(self, n):
        flat = lax.rem(self.y * 4 + self.x * 2 + self.c + n, 8)
        return (self.z * 2 + flat // 4, flat % 4)


class Gather:
    def __init__(self, at, ref, cols, index, send, recv):
        self.at, self.ref, self.cols, self.index, self.send, self.recv = at, ref, cols, index, send, recv

    def copy(self, slot, arriving=False):
        p, c = self.at, self.at.c
        if slot < 3:
            d = slot + 1
            z = lax.rem(p.z + 4 - d, 4) if arriving else p.z
            what, device = self.ref.at[z, p.y, p.x, c, :, self.cols], p.along_z(d)
        else:
            own, second, first, far = (p.y, p.x), (p.y2, p.x2), (p.y1, p.x1), (p.y3, p.x3)
            sent, got, device = {
                3: (own, second, p.second),
                4: (own, first, p.first),
                5: (own, own, p.twin),
                6: (second, far, p.first),
                7: (second, first, p.twin),
                8: (first, second, p.twin),
                9: (far, far, p.twin),
            }[slot]
            y, x = got if arriving else sent
            if arriving and slot not in (3, 4, 6):
                c = 1 - c
            what = self.ref.at[:, y, x, c, :, self.cols]
        return pltpu.make_async_remote_copy(
            src_ref=what,
            dst_ref=what,
            send_sem=self.send.at[self.index, slot],
            recv_sem=self.recv.at[self.index, slot],
            device_id=device,
            device_id_type=MESH,
        )

    def go(self, *slots):
        for slot in slots:
            self.copy(slot).start()

    def await_slots(self, *slots):
        for slot in slots:
            self.copy(slot, True).wait_recv()

    def step0(self):
        self.go(0, 1, 2)

    def step1(self):
        self.await_slots(0, 1, 2)
        self.go(3, 4, 5)

    def step2(self):
        self.await_slots(3)
        self.go(6, 7)

    def step3(self):
        self.await_slots(4)
        self.go(8)
        self.await_slots(6)
        self.go(9)

    def step4(self):
        self.await_slots(5, 7, 8, 9)

    def finish(self):
        for slot in range(10):
            self.copy(slot).wait_send()


class Reduce:
    def __init__(self, at, keep, give, recvs, own, cols, places, index, send, recv):
        self.at, self.keep, self.give, self.recvs, self.own, self.cols = at, keep, give, recvs, own, cols
        self.places = places
        self.index, self.send, self.recv = index, send, recv

    def copy(self, slot):
        p, cols = self.at, self.cols
        if slot == 0:
            what, where, device = self.give.at[:, :, :, :, cols], self.recvs[0].at[:, :, :, :, cols], p.twin
        elif slot == 1:
            what, where, device = self.keep.at[:, :, 1 - p.i1, :, cols], self.recvs[1].at[:, :, :, cols], p.first
        elif slot == 2:
            what, where, device = self.keep.at[:, 1 - p.i2, p.i1, :, cols], self.recvs[2].at[:, :, cols], p.second
        else:
            d = slot - 2
            what = self.keep.at[lax.rem(p.z + d, 4), p.i2, p.i1, :, cols]
            where, device = self.recvs[3].at[d - 1, :, cols], p.along_z(d)
        return pltpu.make_async_remote_copy(
            src_ref=what,
            dst_ref=where,
            send_sem=self.send.at[self.index, slot],
            recv_sem=self.recv.at[self.index, slot],
            device_id=device,
            device_id_type=MESH,
        )

    def step0(self):
        self.copy(0).start()

    def step1(self):
        cols = self.cols
        self.copy(0).wait_recv()

        def add(z):
            self.keep[z, :, :, :, cols] = self.keep[z, :, :, :, cols] + self.recvs[0][z, :, :, :, cols]

        loop(4, add, TILE_UNROLL)
        self.copy(1).start()

    def step2(self):
        p, cols = self.at, self.cols
        self.copy(1).wait_recv()
        self.keep[:, :, p.i1, :, cols] = self.keep[:, :, p.i1, :, cols] + self.recvs[1][:, :, :, cols]
        self.copy(2).start()

    def step3(self):
        p, cols = self.at, self.cols
        self.copy(2).wait_recv()
        self.keep[:, p.i2, p.i1, :, cols] = self.keep[:, p.i2, p.i1, :, cols] + self.recvs[2][:, :, cols]
        for slot in range(3, 6):
            self.copy(slot).start()

    def step4(self):
        p, cols = self.at, self.cols
        total = self.keep[p.z, p.i2, p.i1, :, cols].astype(F32)
        for slot in range(3, 6):
            self.copy(slot).wait_recv()
            total = total + self.recvs[3][slot - 3, :, cols].astype(F32)
        for source, target, width in self.places:
            self.own[:, target : target + width] = total[:, source : source + width]

    def finish(self):
        for slot in range(6):
            self.copy(slot).wait_send()


FUSED_SCRATCH = [
    ("g0", (4, 2, 2, 2, 16, 2176), BF),
    ("g1", (4, 2, 2, 2, 16, 2048), BF),
    ("g2", (4, 2, 2, 2, 16, 2048), BF),
    ("g3", (4, 2, 2, 2, 16, 2048), BF),
    ("vecs", (VROWS, 512), F32),
    ("ra", (4, 4, 2, 2, 16, 2048), BF),
    ("rb", (4, 4, 2, 16, 2048), BF),
    ("rc", (4, 4, 16, 2048), BF),
    ("rd", (4, 3, 16, 2048), BF),
    ("vkeep", (4, 2, 2, 16, 128), BF),
    ("vgive", (4, 2, 2, 16, 128), BF),
    ("va", (4, 2, 2, 16, 128), BF),
    ("vb", (4, 2, 16, 128), BF),
    ("vc", (4, 16, 128), BF),
    ("vd", (3, 16, 128), BF),
    ("nsend", (2, 8, 128), F32),
    ("nrecv", (10, 8, 128), F32),
]
N_GATHER = 12
N_REDUCE = 8


def adam_parts(params, grad_in, first, second, factor):
    clipped = factor * grad_in
    first_m = BETA_ONE * first + (1.0 - BETA_ONE) * clipped
    second_m = BETA_TWO * second + (1.0 - BETA_TWO) * clipped * clipped
    stepped = first_m / CORRECT_ONE / (jnp.sqrt(second_m / CORRECT_TWO) + ADAM_EPS)
    return (-LEARN_RATE * (stepped + WEIGHT_DECAY * params), first_m, second_m)


def fused_kernel(
    tlen, slen, tokens, memory, out_grad, weights, vectors, layer_out, input_grad, memory_grad, own, vown, norm_out, *scratch
):
    r = Bag()
    names = [n for n, _, _ in SCRATCH] + [n for n, _, _ in FUSED_SCRATCH]
    for name, ref in zip(names, scratch):
        setattr(r, name, ref)
    g_send, g_recv, s_send, s_recv, n_send, n_recv, l_sem = scratch[len(names) :]
    p = Place()
    r.tlen, r.slen, r.tokens, r.memory, r.own, r.vown = tlen, slen, tokens, memory, own, vown
    r.g = r.du
    hidden_access(r)
    mats = [r.g0, r.g1, r.g2, r.g3]

    def w(m, a, b):
        shift = 128 if m == 0 else 0
        return mats[m][:, :, :, :, :, a + shift : b + shift].reshape(512, b - a)

    r.w = w

    barrier = pltpu.get_barrier_semaphore()
    for d in range(1, 4):
        pl.semaphore_signal(barrier, inc=1, device_id=p.along_z(d), device_id_type=MESH)
    for n in range(1, 8):
        pl.semaphore_signal(barrier, inc=1, device_id=p.in_plane(n), device_id_type=MESH)
    grad_in = pltpu.make_async_copy(out_grad, r.db, l_sem.at[0])
    grad_in.start()
    r.g0[p.z, p.y, p.x, p.c, :, 0:128] = jnp.concatenate(
        [vectors[...], jnp.zeros((16, 128 - vectors.shape[1]), F32)], axis=1
    ).astype(BF)
    for m in range(4):
        shift = 128 if m == 0 else 0
        mats[m][p.z, p.y, p.x, p.c, :, shift : shift + 2048] = weights[16 * m : 16 * m + 16, :].astype(BF)
    pl.semaphore_wait(barrier, 10)

    gathers = []
    for m, cuts in ((0, (0, 640, 1152, 1664, 2176)), (1, (0, 512, 1024, 1536, 2048)), (2, (0, 1024, 2048)), (3, (0, 1024, 2048))):
        for a, b in zip(cuts[:-1], cuts[1:]):
            gathers.append(Gather(p, mats[m], slice(a, b), len(gathers), g_send, g_recv))
    for g in gathers:
        g.step0()

    def steps(*pairs):
        return [getattr(gathers[k], "step%d" % s) for k, s in pairs]

    keeps = {0: r.hd.at[1, 0], 1: r.hd.at[0, 0], 2: r.g2.at[:, :, :, 0], 3: r.g3.at[:, :, :, 0]}
    gives = {0: r.hd.at[1, 1], 1: r.hd.at[0, 1], 2: r.g2.at[:, :, :, 1], 3: r.g3.at[:, :, :, 1]}

    def spread(value, keep, give, cols):
        v = value.reshape(4, 2, 2, 2, 16, value.shape[-1])
        flag = p.c == 0
        for y in range(2):
            for x in range(2):
                i1, i2 = x * (1 - p.c) + y * p.c, y * (1 - p.c) + x * p.c
                even, odd = v[:, y, x, 0], v[:, y, x, 1]
                keep[:, i2, i1, :, cols] = jnp.where(flag, even, odd).astype(BF)
                give[:, i1, i2, :, cols] = jnp.where(flag, odd, even).astype(BF)

    def emit(m, first):
        def one(c, value):
            spread(value, keeps[m], gives[m], pl.ds(pl.multiple_of((first + c) * 256, 256), 256))

        return one

    def job(k, m, a, b, places=None):
        return Reduce(
            p, keeps[m], gives[m], (r.ra.at[m], r.rb.at[m], r.rc.at[m], r.rd.at[m]), r.own.at[16 * m : 16 * m + 16, :],
            slice(a, b), places or ((0, a, b - a),), k, s_send, s_recv,
        )

    halves = [tuple((256 * part, 512 * part + 256 * h, 256) for part in range(3)) for h in range(2)]
    j3, j2, j1o, j1 = job(0, 3, 0, 2048), job(1, 2, 0, 2048), job(2, 1, 1536, 2048), job(3, 1, 0, 1536)
    j0o, j0a, j0b = job(4, 0, 1536, 2048), job(5, 0, 0, 768, halves[0]), job(6, 0, 768, 1536, halves[1])
    jv = Reduce(
        p, r.vkeep, r.vgive, (r.va, r.vb, r.vc, r.vd), r.vown, slice(0, 128), ((0, 0, 128),), 7, s_send, s_recv
    )
    jobs = [j3, j2, j1o, j1, j0o, j0a, j0b, jv]

    def read_vectors():
        for b in range(4):
            block = r.g0[b, :, :, :, :, 0:128].reshape(128, 128).astype(F32)
            r.vecs[:, b * 128 : (b + 1) * 128] = block.T[0:VROWS, :]

    def middle_done():
        for g in gathers:
            g.finish()
        for k in range(4):
            layer_part(k // 2, k % 2).wait()

    hooks = {
        "start0": steps((0, 1), (1, 1), (0, 2), (2, 1), (1, 2), (0, 3), (3, 1), (2, 2), (1, 3), (0, 4)) + [read_vectors],
        "start1": steps((4, 1), (3, 2), (2, 3), (1, 4)),
        "start2": steps((5, 1), (4, 2), (2, 4)),
        "projected": steps((6, 1), (3, 3), (5, 2)),
        "self0": steps((7, 1), (3, 4), (4, 3), (6, 2)),
        "self1": steps((8, 1), (4, 4), (5, 3), (7, 2)),
        "self2": steps((9, 1), (5, 4), (6, 3), (7, 3), (8, 2)),
        "self3": steps((10, 1), (6, 4), (7, 4), (9, 2)),
        "cross_ready": steps((11, 1), (8, 3), (10, 2)),
        "crossed": [grad_in.wait],
        "middle": [middle_done],
        "grads3": [j3.step0],
        "grads2": [j2.step0, j3.step1],
        "grads1o": [j1o.step0],
        "grads1": [j1.step0, j2.step4, j1o.step3],
        "grads0o": [j0o.step0, j1.step1, j1o.step4],
        "self_back00": [j0o.step1],
        "self_back03": [j1.step2, j0o.step2],
        "grads00": [j0a.step0],
        "self_back11": [j1.step3, j0o.step3, j0a.step1],
        "self_back13": [j1.step4, j0o.step4, j0a.step2],
    }
    plan = {
        "cross": {
            0: steps((8, 4), (9, 3), (11, 2)),
            1: steps((9, 4), (10, 3)),
            2: steps((10, 4), (11, 3)),
            3: steps((11, 4)),
        },
        "cross_back": {
            0: [j2.step1],
            1: [j3.step2],
            3: [j3.step3],
            4: [j2.step2, j1o.step1],
            6: [j3.step4, j2.step3, j1o.step2],
        },
    }

    def vectors_out():
        sums = jnp.sum(r.vg[...], axis=1)
        sums = jnp.concatenate([sums, jnp.zeros((128 - VROWS, 512), F32)], axis=0)
        columns = jnp.concatenate([sums[:, b * 128 : (b + 1) * 128].T for b in range(4)], axis=0)
        spread(columns, r.vkeep, r.vgive, slice(0, 128))
        jv.step0()

    hooks["grads01"] = [j0b.step0, vectors_out]
    hooks["tail0"] = [j0a.step3]
    hooks["tail1"] = [j0b.step1, jv.step1]

    def hook(name):
        for action in hooks.get(name, ()):
            action()

    def at_step(name, t):
        for when, actions in plan.get(name, {}).items():

            @pl.when(t == when)
            def _():
                for action in actions:
                    action()

    r.get_out_grad = lambda i: r.db[rows_of(i), :]

    def layer_part(half, k):
        piece = r.xt.at[rows_of(half), k * 512 : k * 512 + 512]
        i = 2 * half + k
        return pltpu.make_async_copy(piece, layer_out.at[rows_of(i), :], l_sem.at[2 + i])

    def put_layer_out(half, k, value):
        r.xt[rows_of(half), k * 512 : k * 512 + 512] = value
        layer_part(half, k).start()

    def memory_part(i):
        return pltpu.make_async_copy(r.n1.at[rows_of(i), :], memory_grad.at[rows_of(i), :], l_sem.at[6 + i])

    def put_memory_grad(i, value):
        r.n1[rows_of(i), :] = value
        memory_part(i).start()

    def input_part(i):
        return pltpu.make_async_copy(r.dz.at[rows_of(i), :], input_grad.at[rows_of(i), :], l_sem.at[10 + i])

    def put_input_grad(i, value):
        r.dz[rows_of(i), :] = value
        input_part(i).start()

    r.put_layer_out, r.put_memory_grad, r.put_input_grad = put_layer_out, put_memory_grad, put_input_grad

    run(r, emit, hook, at_step)

    for step in (j0b.step2, jv.step2, j0a.step4, j0b.step3, jv.step3, j0b.step4, jv.step4):
        step()

    squares = jnp.sum((r.vown[...] * r.vown[...]).reshape(2, 8, 128), axis=0)
    for k in range(8):
        part = r.own[8 * k : 8 * k + 8, :]
        part = part * part
        for b in range(16):
            squares = squares + part[:, 128 * b : 128 * b + 128]
    r.nsend[0] = squares

    def plane_part(n):
        return pltpu.make_async_remote_copy(
            src_ref=r.nsend.at[0], dst_ref=r.nrecv.at[n - 1], send_sem=n_send.at[n - 1], recv_sem=n_recv.at[n - 1],
            device_id=p.in_plane(n), device_id_type=MESH,
        )

    def z_part(d):
        return pltpu.make_async_remote_copy(
            src_ref=r.nsend.at[1], dst_ref=r.nrecv.at[6 + d], send_sem=n_send.at[6 + d], recv_sem=n_recv.at[6 + d],
            device_id=p.along_z(d), device_id_type=MESH,
        )

    for n in range(1, 8):
        plane_part(n).start()
    total = r.nsend[0]
    for n in range(1, 8):
        plane_part(n).wait_recv()
        total = total + r.nrecv[n - 1]
    r.nsend[1] = total
    for d in range(1, 4):
        z_part(d).start()
    for k in range(4):
        memory_part(k).wait()
        input_part(k).wait()
    for j in jobs:
        j.finish()
    for n in range(1, 8):
        plane_part(n).wait_send()
    for d in range(1, 4):
        z_part(d).wait_recv()
        total = total + r.nrecv[6 + d]
    norm_out[...] = jnp.broadcast_to(jnp.sqrt(jnp.sum(total)), (8, 128))
    for d in range(1, 4):
        z_part(d).wait_send()


def finish_kernel(
    layer_in, input_in, memory_in, own, weights, moments, vown, norm, norm_scalar, vectors, vector_moments,
    layer_out, input_grad, memory_grad, norm_out, mat_out, step_out, first_out, second_out, vec_out, vstep_out, vfirst_out,
    vsecond_out, low_room, big_room, mats, sems, out_sems,
):
    small = []
    for n, (source, at, size) in enumerate(((own, 0, 64), (weights, 64, 64), (moments, 128, 128))):
        small.append(pltpu.make_async_copy(source, mats.at[at : at + size, :], sems.at[10 + n]))
        small[-1].start()
    arrivals, departures = [], []
    for source, target, room, pieces in (
        (layer_in, layer_out, low_room, 2),
        (memory_in, memory_grad, big_room.at[0], 4),
        (input_in, input_grad, big_room.at[1], 4),
    ):
        size = source.shape[0] // pieces
        for k in range(pieces):
            rows, n = slice(k * size, k * size + size), len(arrivals)
            arrivals.append(pltpu.make_async_copy(source.at[rows, :], room.at[rows, :], sems.at[n]))
            departures.append(pltpu.make_async_copy(room.at[rows, :], target.at[rows, :], out_sems.at[n]))
            arrivals[-1].start()
    norm_out[0, 0] = norm_scalar[0, 0]
    factor = jnp.minimum(1.0, CLIP_NORM / (norm[0:1, 0:1] + 1e-06))
    count = vectors.shape[1]
    vgrad = vown[:, 0:count]
    vec_out[...] = vgrad
    vstep_out[...], vfirst_out[...], vsecond_out[...] = adam_parts(
        vectors[...], vgrad, vector_moments[0], vector_moments[1], factor
    )
    for copy in small:
        copy.wait()
    for n, (target, at) in enumerate(((mat_out, 0), (step_out, 64), (first_out, 128), (second_out, 192))):
        departures.append(pltpu.make_async_copy(mats.at[at : at + 64, :], target, out_sems.at[10 + n]))
    departures[10].start()

    def update(i):
        a, b, c, d = (pl.ds(pl.multiple_of(i * 16 + o, 16), 16) for o in (0, 64, 128, 192))
        mats[b, :], mats[c, :], mats[d, :] = adam_parts(mats[b, :], mats[a, :], mats[c, :], mats[d, :], factor)

    for arrival, departure in zip(arrivals[:5], departures[:5]):
        arrival.wait()
        departure.start()
    loop(4, update)
    for departure in departures[11:]:
        departure.start()
    for arrival, departure in zip(arrivals[5:], departures[5:10]):
        arrival.wait()
        departure.start()
    for departure in departures:
        departure.wait()


def fused_body(tokens, memory, target_lengths, source_lengths, out_grad, weights, vectors, weight_moments, vector_moments):
    V = pl.BlockSpec(memory_space=pltpu.VMEM)
    S = pl.BlockSpec(memory_space=pltpu.SMEM)
    A = pl.BlockSpec(memory_space=pl.ANY)
    mat = jax.ShapeDtypeStruct((64, 2048), F32)
    vec_shape = jax.ShapeDtypeStruct(vectors.shape[::-1], F32)
    low = jax.ShapeDtypeStruct(tokens.shape, BF)
    big = jax.ShapeDtypeStruct(tokens.shape, F32)
    flat_weights, flat_vectors = weights.reshape(64, 2048), vectors.T
    layer_out, input_grad, memory_grad, own, vown, norm = pl.pallas_call(
        fused_kernel,
        out_shape=(low, big, big, mat, jax.ShapeDtypeStruct((16, 128), F32), jax.ShapeDtypeStruct((8, 128), F32)),
        in_specs=[S, S, V, V, A, V, V],
        out_specs=(A, A, A, V, V, V),
        scratch_shapes=[pltpu.VMEM(s, d) for _, s, d in SCRATCH + FUSED_SCRATCH]
        + [
            pltpu.SemaphoreType.DMA((N_GATHER, 10)),
            pltpu.SemaphoreType.DMA((N_GATHER, 10)),
            pltpu.SemaphoreType.DMA((N_REDUCE, 6)),
            pltpu.SemaphoreType.DMA((N_REDUCE, 6)),
            pltpu.SemaphoreType.DMA((10,)),
            pltpu.SemaphoreType.DMA((10,)),
            pltpu.SemaphoreType.DMA((14,)),
        ],
        compiler_params=pltpu.CompilerParams(vmem_limit_bytes=63400000, collective_id=0, has_side_effects=True),
        name="layer",
    )(target_lengths, source_lengths, tokens, memory, out_grad, flat_weights, flat_vectors)
    layer_out, input_grad, memory_grad, norm, g, st, m1, m2, vg, vst, vm1, vm2 = pl.pallas_call(
        finish_kernel,
        out_shape=(low, big, big, jax.ShapeDtypeStruct((1, 1), F32), mat, mat, mat, mat) + (vec_shape,) * 4,
        in_specs=[A, A, A, A, A, A, V, V, S, V, V],
        out_specs=(A, A, A, S, A, A, A, A, V, V, V, V),
        scratch_shapes=[
            pltpu.VMEM(tokens.shape, BF),
            pltpu.VMEM((2,) + tokens.shape, F32),
            pltpu.VMEM((256, 2048), F32),
            pltpu.SemaphoreType.DMA((13,)),
            pltpu.SemaphoreType.DMA((14,)),
        ],
        compiler_params=pltpu.CompilerParams(vmem_limit_bytes=63400000),
        name="finish",
    )(
        layer_out, input_grad, memory_grad, own, flat_weights, weight_moments.reshape(128, 2048), vown, norm, norm, flat_vectors,
        vector_moments.transpose(0, 2, 1),
    )
    back = lambda a: a.reshape(weights.shape)
    return (
        layer_out, input_grad, memory_grad, norm[0, 0], back(g), vg.T, back(st), vst.T, back(m1), back(m2), vm1.T, vm2.T,
    )


def adam_update(params, grad_in, moments, factor):
    clipped = factor * grad_in
    first_m = BETA_ONE * moments[0] + (1.0 - BETA_ONE) * clipped
    second_m = BETA_TWO * moments[1] + (1.0 - BETA_TWO) * clipped * clipped
    stepped = first_m / CORRECT_ONE / (jnp.sqrt(second_m / CORRECT_TWO) + ADAM_EPS)
    return (-LEARN_RATE * (stepped + WEIGHT_DECAY * params), first_m, second_m)


def generic_body(tokens, memory, target_lengths, source_lengths, out_grad, weights, vectors, weight_moments, vector_moments):
    axes = ("dp", "shard")
    w = lax.all_gather(weights.astype(BF), axes, axis=1, tiled=True)
    vecs = lax.all_gather(vectors.astype(BF), axes, axis=1, tiled=True).astype(F32)
    vecs = jnp.concatenate([vecs, jnp.zeros((VROWS - vecs.shape[0], vecs.shape[1]), F32)], axis=0)
    layer_out, input_grad, memory_grad, mat_grad, vec_grad = plain(
        target_lengths, source_lengths, tokens, memory, out_grad, w, vecs
    )
    mat_share = lax.psum_scatter(mat_grad, axes, scatter_dimension=1, tiled=True)
    vec_share = lax.psum_scatter(vec_grad[: vectors.shape[0]], axes, scatter_dimension=1, tiled=True)
    squares = jnp.sum(mat_share * mat_share) + jnp.sum(vec_share * vec_share)
    grad_norm = jnp.sqrt(lax.psum(squares, axes))
    factor = jnp.minimum(1.0, CLIP_NORM / (grad_norm + 1e-06))
    weight_steps, weight_first, weight_second = adam_update(weights, mat_share, weight_moments, factor)
    vector_steps, vector_first, vector_second = adam_update(vectors, vec_share, vector_moments, factor)
    return (
        layer_out, input_grad, memory_grad, grad_norm, mat_share, vec_share,
        weight_steps, vector_steps, weight_first, weight_second, vector_first, vector_second,
    )


def solution(mesh):
    both = ("dp", "shard")
    rows, mats, vecs = P(both, None), P(None, both, None), P(None, both)
    fits = (mesh.shape["dp"], mesh.shape["shard"]) == (8, 4)
    return jax.shard_map(
        fused_body if fits else generic_body,
        mesh=mesh,
        in_specs=(rows, rows, rows, rows, rows, mats, vecs, P(None, None, both, None), P(None, None, both)),
        out_specs=(rows, rows, rows, P(), mats, vecs, mats, vecs, mats, mats, vecs, vecs),
        check_vma=False,
    )
```
